32 devices in a mesh: seq: 8 (over z, y), head: 4 (over x, core).
Axes of the slice: x: 2, y: 2, z: 4, core: 2. Of those that a mesh axis runs over, the one named last changes fastest.
Arguments:
- tokens: bfloat16 [3, 1024, 768], P(None, 'seq'), may hold values from -6 to 6
- cotangent: bfloat16 [3, 1024, 768], P(None, 'seq'), may hold values from -6 to 6
- lengths: int32 [3, 3], replicated, may hold values from 1 to 960, 1024 in all within a row
- coords: int32 [2, 3, 1024], P(None, None, 'seq'), may hold values from 0 to 255
- keep_mask: int32 [3, 1024], P(None, 'seq'), may hold values 0 or 1
- ln_gains: bfloat16 [2, 768], P(None, 'seq'), may hold values from 0.5 to 1.5
- ln_shifts: bfloat16 [2, 768], P(None, 'seq'), may hold values from -2 to 2
- out_bias: bfloat16 [2, 768], P(None, 'seq'), may hold values from -2 to 2
- w_qkv: bfloat16 [768, 3, 768], P('seq', None, 'head'), may hold values from -0.3125 to 0.3125
- qv_bias: bfloat16 [2, 768], P(None, 'head'), may hold values from -2 to 2
- w_out: bfloat16 [768, 768], P('head', 'seq'), may hold values from -1.75 to 1.75
- w_up: bfloat16 [768, 3072], P('seq', 'head'), may hold values from -0.21875 to 0.21875
- up_bias: bfloat16 [3072], P('head'), may hold values from -2 to 2
- w_down: bfloat16 [3072, 768], P('head', 'seq'), may hold values from -0.109375 to 0.109375
Outputs:
- out_tokens: bfloat16 [3, 1024, 768], P(None, 'seq')
- grad_tokens: bfloat16 [3, 1024, 768], P(None, 'seq')
- grad_ln_gains: float32 [2, 768], P(None, 'seq')
- grad_ln_shifts: float32 [2, 768], P(None, 'seq')
- grad_out_bias: float32 [2, 768], P(None, 'seq')
- grad_qkv: float32 [768, 3, 768], P('seq', None, 'head')
- grad_qv_bias: float32 [2, 768], P(None, 'head')
- grad_out: float32 [768, 768], P('head', 'seq')
- grad_up: float32 [768, 3072], P('seq', 'head')
- grad_up_bias: float32 [3072], P('head')
- grad_down: float32 [3072, 768], P('head', 'seq')
The draws below stay inside these ranges and needn't reach their ends.
Inputs may be any that keep to these rules, and one draw needn't show every extreme that they name: Each micro-batch row holds 3 slides end to end, their lengths summing to 1024; the longest has exactly 960 tiles.
All inputs are finite; a program needn't handle non-finite values. No bound on the sum of `keep_mask` on one device may be relied on, other than what follows from the above.
Results may differ from the reference program's by a relative error of at most 0.02.
Values may be sent and summed in bfloat16 or wider, within the bound.
A program may use at most 256 MiB of HBM per device.

```python
import math
from functools import partial
import jax
import jax.numpy as jnp
import numpy as np
from jax import lax

HEADS = 16
HDIM = 48
D = 768
FF = 3072
UNIT = 1024
TOK_DEV = 128
MICRO = 3
SLIDES = 3
BRANCHES = 5
ROW = 1024


def plant(values, own_key, low, top_value):
    place = [jax.random.randint(jax.random.fold_in(own_key, axis), (), 0, length) for axis, length in enumerate(values.shape)]
    longest = values.shape.index(max(values.shape))
    next_to = place[:longest] + [(place[longest] + 1) % values.shape[longest]] + place[longest + 1:]
    return values.at[tuple(place)].set(low).at[tuple(next_to)].set(top_value)


def steps_of(rng, extent, cuts, least, largest):
    def one(dim, parts):
        steps = jax.random.uniform(jax.random.fold_in(jax.random.fold_in(rng, 6), dim), (parts,), jnp.float32, least / len(cuts), largest / len(cuts))
        return jnp.repeat(jnp.exp(steps), extent[dim] // parts).reshape((-1,) + (1,) * (len(extent) - dim - 1))

    gain = one(*cuts[0])
    for cut in cuts[1:]:
        gain = gain * one(*cut)
    return gain


def profile(amount, total, limit, skew):
    portions = [(1 << 20) // math.isqrt(rank ** skew) + 1 for rank in range(2, amount + 1)]
    spare, given = total - limit - (amount - 1), [1] * (amount - 1)
    while spare > 0:
        candidates = [i for i in range(amount - 1) if given[i] < limit]
        mass, remaining = sum([portions[i] for i in candidates]), spare
        for i in candidates:
            more = min(limit - given[i], max(1, remaining * portions[i] // mass), spare)
            given[i] = given[i] + more
            spare = spare - more
    return np.array([limit] + given)


def ragged(own_key, amount, total, limit, slope):
    if amount == 2:
        one = jax.random.randint(own_key, (), max(1, total - limit), min(limit, total - 1) + 1)
        return jnp.stack([one, total - one])
    sizes = jnp.asarray(profile(amount, total, limit, slope), jnp.int32)
    couples = (amount - 1) // 2
    giver, receiver = sizes[1:1 + 2 * couples:2], sizes[2:2 + 2 * couples:2]
    slack = jnp.minimum(giver - 1, limit - receiver)
    shifted = jax.random.randint(jax.random.fold_in(own_key, 1), (couples,), 0, 1 << 20) % (slack + 1)
    sizes = sizes.at[1:1 + 2 * couples:2].set(giver - shifted).at[2:2 + 2 * couples:2].set(receiver + shifted)
    return sizes[jax.random.permutation(jax.random.fold_in(own_key, 2), amount)]


def centred(key, extent, scale, reach, cuts=(), held_as=jnp.bfloat16):
    values = scale * jax.random.normal(key, extent, jnp.float32)
    if cuts:
        values = values * steps_of(key, extent, cuts, -0.22, 0.18)
    return jnp.clip(values, -reach, reach).astype(held_as)


def setup_inputs(seed: int = 0) -> dict:
    key_list = jax.random.split(jax.random.key(seed), 15)
    tokens = centred(key_list[0], (MICRO, ROW, D), 1.0, 6.0, ((1, 8),))
    cotangent = centred(key_list[1], (MICRO, ROW, D), 1.0, 6.0, ((1, 8),))
    lengths = jax.vmap(lambda own: ragged(own, SLIDES, ROW, ROW - TOK_DEV // 2, 2))(jax.random.split(key_list[2], MICRO)).reshape((MICRO, SLIDES)).astype(jnp.int32)
    coords = plant(jax.random.randint(key_list[3], (2, MICRO, ROW), 0, 256), jax.random.fold_in(key_list[3], 1), 0, 255).astype(jnp.int32)
    keep_mask = plant((jax.random.randint(key_list[4], (MICRO, ROW), 0, 8) < 7).astype(jnp.int32), jax.random.fold_in(key_list[4], 1), 0, 1)
    ln_gains = jnp.clip(1.0 + 0.1 * jax.random.normal(key_list[5], (2, D), jnp.float32), 0.5, 1.5).astype(jnp.bfloat16)
    ln_shifts = centred(key_list[6], (2, D), 0.3, 2.0, ((1, 8),))
    out_bias = centred(key_list[7], (2, D), 0.3, 2.0, ((1, 8),))
    w_qkv = centred(key_list[8], (D, 3, D), (D // 2) ** -0.5, 0.3125, ((0, 8), (2, 4)))
    qv_bias = centred(key_list[9], (2, D), 0.3, 2.0, ((1, 4),))
    w_out = centred(key_list[10], (D, D), (D // 64) ** -0.5, 1.75, ((0, 4), (1, 8)))
    w_up = centred(key_list[11], (D, FF), D ** -0.5, 0.21875, ((0, 8), (1, 4)))
    up_bias = centred(key_list[12], (FF,), 0.3, 2.0, ((0, 4),))
    w_down = centred(key_list[13], (FF, D), FF ** -0.5, 0.109375, ((0, 4), (1, 8)))
    return {"tokens": tokens, "cotangent": cotangent, "lengths": lengths, "coords": coords, "keep_mask": keep_mask, "ln_gains": ln_gains, "ln_shifts": ln_shifts, "out_bias": out_bias, "w_qkv": w_qkv, "qv_bias": qv_bias, "w_out": w_out, "w_up": w_up, "up_bias": up_bias, "w_down": w_down}


@jax.custom_vjp
def low(v):
    return lax.optimization_barrier(v.astype(jnp.bfloat16)).astype(jnp.float32)

@jax.custom_vjp
def low_back(v):
    return v

def low_keep(v):
    return (low(v), None)

def low_pass(kept, grad):
    return (grad,)

def back_keep(v):
    return (v, None)

def back_low(kept, grad):
    return (low(grad),)
low.defvjp(low_keep, low_pass)
low_back.defvjp(back_keep, back_low)
EPSILON = 1e-05
HIGHEST = lax.Precision.HIGHEST

def position_table(grid_rows):
    quarter = D // 4
    frequency = jnp.exp(-jnp.log(10000.0) * jnp.arange(quarter, dtype=jnp.float32) / quarter)
    along_row = grid_rows[0].astype(jnp.float32)[:, None] * frequency[None, :]
    along_col = grid_rows[1].astype(jnp.float32)[:, None] * frequency[None, :]
    return jnp.concatenate([jnp.sin(along_row), jnp.cos(along_row), jnp.sin(along_col), jnp.cos(along_col)], axis=1)

def layer_norm(values, gain_vec, shift_vec):
    centre = values - lax.optimization_barrier(jnp.mean(values, axis=-1, keepdims=True))
    spread = lax.optimization_barrier(jnp.mean(centre * centre, axis=-1, keepdims=True))
    return centre * lax.rsqrt(spread + EPSILON) * gain_vec + shift_vec

def branch_weight(branch, head_id, picked, slide_ids, keep_row):
    pos_query = picked[:, :, None]
    pos_key = picked[:, None, :]
    slide_pick = slide_ids[picked]
    visible = (slide_pick[:, :, None] == slide_pick[:, None, :]) & ((keep_row[picked][:, None, :] > 0) | (pos_query == pos_key))
    counted = jnp.zeros(picked.shape + (picked.shape[1],), jnp.float32)
    for wider in range(branch, BRANCHES):
        stride = 2 ** wider
        both_on = (pos_query % stride == head_id % stride) & (pos_key % stride == head_id % stride)
        counted = counted + both_on.astype(jnp.float32)
    if branch > 0:
        half_span = UNIT * 2 ** (branch - 1)
        visible = visible & (pos_query // half_span != pos_key // half_span)
    return counted * visible.astype(jnp.float32)

def head_attention(query_head, key_head, value_head, head_id, slide_ids, keep_row):
    inv_root = 1.0 / jnp.sqrt(jnp.float32(HDIM))
    row_denom = jnp.zeros((ROW,), jnp.float32)
    pieces = []
    for branch in range(BRANCHES):
        stride = 2 ** branch
        group = min(UNIT, ROW // stride)
        picked = (head_id % stride + stride * jnp.arange(ROW // stride, dtype=jnp.int32)).reshape(-1, group)
        scores = jnp.einsum('gid,gjd->gij', query_head[picked], key_head[picked], precision=HIGHEST) * inv_root
        scores = low_back(scores)
        weight = branch_weight(branch, head_id, picked, slide_ids, keep_row)
        row_denom = row_denom.at[picked].add(lax.optimization_barrier(jnp.sum(weight * jnp.exp(scores), axis=2)))
        pieces.append((picked, scores, weight))
    log_total = jnp.log(row_denom)
    result = jnp.zeros((ROW, HDIM), jnp.float32)
    for picked, scores, weight in pieces:
        probs = low(weight * jnp.exp(scores - log_total[picked][:, :, None]))
        result = result.at[picked].add(jnp.einsum('gij,gjd->gid', probs, value_head[picked], precision=HIGHEST))
    return result

def row_forward(params, row_tokens, row_coords, row_lengths, row_keep):
    gains, shifts, obias, wqkv, qvb, wout, wup, upb, wdown = params
    positions = jnp.arange(ROW, dtype=jnp.int32)
    bounds = jnp.cumsum(row_lengths)[:-1]
    slide_ids = lax.optimization_barrier(jnp.sum((positions[:, None] >= bounds[None, :]).astype(jnp.int32), axis=1))
    inputs = row_tokens + position_table(row_coords)
    normed = low(layer_norm(inputs, gains[0], shifts[0]))
    projected = jnp.einsum('td,dcf->tcf', normed, wqkv, precision=HIGHEST)
    queries = low_back(low(projected[:, 0] + qvb[0]))
    key_rows = low_back(low(projected[:, 1]))
    value_rows = low_back(low(projected[:, 2] + qvb[1]))
    split_heads = lambda matrix: matrix.reshape(ROW, HEADS, HDIM).transpose(1, 0, 2)
    attend = jax.checkpoint(partial(head_attention, slide_ids=slide_ids, keep_row=row_keep))

    def one_head(packed):
        return attend(packed[0], packed[1], packed[2], packed[3])
    attended = lax.map(one_head, (split_heads(queries), split_heads(key_rows), split_heads(value_rows), jnp.arange(HEADS, dtype=jnp.int32)))
    attended = low_back(low(attended.transpose(1, 0, 2).reshape(ROW, D)))
    branch_out = low_back(jnp.dot(attended, wout, precision=HIGHEST) + obias[0])
    middle = inputs + branch_out
    normed_two = low(layer_norm(middle, gains[1], shifts[1]))
    hidden_pre = low_back(jnp.dot(normed_two, wup, precision=HIGHEST) + upb)
    activated = low(jax.nn.gelu(hidden_pre, approximate=False))
    return middle + jnp.dot(activated, wdown, precision=HIGHEST) + obias[1]

def reference(tokens, cotangent, lengths, coords, keep_mask, ln_gains, ln_shifts, out_bias, w_qkv, qv_bias, w_out, w_up, up_bias, w_down):
    floats = tuple((array.astype(jnp.float32) for array in (tokens, ln_gains, ln_shifts, out_bias, w_qkv, qv_bias, w_out, w_up, up_bias, w_down)))

    def forward(tokens_f, *params):

        def row_step(running, packed):
            return (running, row_forward(params, packed[0], packed[1], packed[2], packed[3]))
        _, result = lax.scan(row_step, None, (tokens_f, jnp.transpose(coords, (1, 0, 2)), lengths, keep_mask))
        return result
    outputs, pullback = jax.vjp(forward, *floats)
    grads = pullback(cotangent.astype(jnp.float32))
    return (outputs.astype(jnp.bfloat16), grads[0].astype(jnp.bfloat16), grads[1], grads[2], grads[3], grads[4], grads[5], grads[6], grads[7], grads[8], grads[9])
```

```python
from functools import partial
import math

import jax
import jax.numpy as jnp
import ml_dtypes
import numpy as np
from jax import lax
from jax.experimental import pallas as pl
from jax.experimental.pallas import tpu as pltpu
from jax.sharding import PartitionSpec as P

HDIM = 48
UNIT = 1024
BRANCHES = 5


EPSILON = 1e-05


def position_table(grid_rows, width):
    quarter = width // 4
    frequency = jnp.exp(-jnp.log(10000.0) * jnp.arange(quarter, dtype=jnp.float32) / quarter)
    along_row = grid_rows[0].astype(jnp.float32)[:, None] * frequency[None, :]
    along_col = grid_rows[1].astype(jnp.float32)[:, None] * frequency[None, :]
    return jnp.concatenate(
        [jnp.sin(along_row), jnp.cos(along_row), jnp.sin(along_col), jnp.cos(along_col)], axis=1
    )


def layer_norm(values, gain_vec, shift_vec):
    centre = values - jnp.mean(values, axis=-1, keepdims=True)
    spread = jnp.mean(centre * centre, axis=-1, keepdims=True)
    return centre * lax.rsqrt(spread + EPSILON) * gain_vec + shift_vec


def slide_of(positions, bounds):
    return jnp.sum((positions[:, None] >= bounds[None, :]).astype(jnp.int32), axis=1)


def pair_weight(query_pos, key_pos, key_keep, head_ids, bounds, seg_unit):
    same_slide = slide_of(query_pos, bounds)[:, None] == slide_of(key_pos, bounds)[None, :]
    visible = same_slide & ((key_keep[None, :] > 0) | (query_pos[:, None] == key_pos[None, :]))
    counted = jnp.zeros((head_ids.shape[0], query_pos.shape[0], key_pos.shape[0]), jnp.float32)
    for branch in range(BRANCHES):
        stride = 2**branch
        span = seg_unit * stride
        same_seg = query_pos[:, None] // span == key_pos[None, :] // span
        query_on = query_pos[None, :] % stride == head_ids[:, None] % stride
        key_on = key_pos[None, :] % stride == head_ids[:, None] % stride
        counted = counted + (same_seg[None] & query_on[:, :, None] & key_on[:, None, :]).astype(
            jnp.float32
        )
    return counted * visible[None].astype(jnp.float32)


def head_total(partial_sum):
    return lax.psum(partial_sum.astype(jnp.bfloat16), "head").astype(jnp.float32)


def per_device(
    tokens,
    cotangent,
    lengths,
    coords,
    keep_mask,
    ln_gains,
    ln_shifts,
    out_bias,
    w_qkv,
    qv_bias,
    w_out,
    w_up,
    up_bias,
    w_down,
):
    micro_count, tok_local, width = tokens.shape
    row_len = tok_local * lax.axis_size("seq")
    seg_unit = UNIT
    block_count = row_len // seg_unit
    heads_local = w_qkv.shape[2] // HDIM
    local_width = heads_local * HDIM
    inv_root = 1.0 / math.sqrt(HDIM)
    head_ids = lax.axis_index("head") * heads_local + jnp.arange(heads_local, dtype=jnp.int32)
    own_pos = lax.axis_index("seq") * tok_local + jnp.arange(tok_local, dtype=jnp.int32)
    block_starts = jnp.arange(block_count, dtype=jnp.int32) * seg_unit
    bias_qv = qv_bias.astype(jnp.float32)
    bias_up = up_bias.astype(jnp.float32)
    sum_qkv = jnp.zeros((width, 3, local_width), jnp.float32)
    sum_out = jnp.zeros((local_width, width), jnp.float32)
    sum_up = jnp.zeros((width, w_up.shape[1]), jnp.float32)
    sum_down = jnp.zeros((w_down.shape[0], width), jnp.float32)
    sum_gain = jnp.zeros((2, width), jnp.float32)
    sum_shift = jnp.zeros((2, width), jnp.float32)
    sum_obias = jnp.zeros((2, width), jnp.float32)
    sum_qvb = jnp.zeros((2, local_width), jnp.float32)
    sum_upb = jnp.zeros((w_up.shape[1],), jnp.float32)
    out_rows = []
    grad_rows = []
    for micro_id in range(micro_count):
        full_qkv, full_out, full_up, full_down, gain_rows, shift_rows, obias_rows = (
            lax.all_gather(w_qkv, "seq", axis=0, tiled=True),
            lax.all_gather(w_out, "seq", axis=1, tiled=True),
            lax.all_gather(w_up, "seq", axis=0, tiled=True),
            lax.all_gather(w_down, "seq", axis=1, tiled=True),
            lax.all_gather(ln_gains, "seq", axis=1, tiled=True),
            lax.all_gather(ln_shifts, "seq", axis=1, tiled=True),
            lax.all_gather(out_bias, "seq", axis=1, tiled=True),
        )
        gain_rows = gain_rows.astype(jnp.float32)
        shift_rows = shift_rows.astype(jnp.float32)
        obias_rows = obias_rows.astype(jnp.float32)
        bounds = jnp.cumsum(lengths[micro_id])[:-1]
        inputs = tokens[micro_id].astype(jnp.float32) + position_table(coords[:, micro_id], width)
        normed = layer_norm(inputs, gain_rows[0], shift_rows[0]).astype(jnp.bfloat16)
        projected = jnp.einsum("td,dcf->tcf", normed, full_qkv, preferred_element_type=jnp.float32)
        queries = (
            (projected[:, 0] + bias_qv[0])
            .astype(jnp.bfloat16)
            .reshape(tok_local, heads_local, HDIM)
        )
        key_rows = projected[:, 1].astype(jnp.bfloat16).reshape(tok_local, heads_local, HDIM)
        value_rows = (
            (projected[:, 2] + bias_qv[1])
            .astype(jnp.bfloat16)
            .reshape(tok_local, heads_local, HDIM)
        )
        keep_local = keep_mask[micro_id].astype(jnp.bfloat16)
        key_all, value_all, keep_all = (
            lax.all_gather(key_rows, "seq", axis=0, tiled=True),
            lax.all_gather(value_rows, "seq", axis=0, tiled=True),
            lax.all_gather(keep_local, "seq", axis=0, tiled=True),
        )

        def key_block(key_src, value_src, keep_src, offset):
            key_blk = lax.dynamic_slice_in_dim(key_src, offset, seg_unit, 0)
            value_blk = lax.dynamic_slice_in_dim(value_src, offset, seg_unit, 0)
            keep_blk = lax.dynamic_slice_in_dim(keep_src, offset, seg_unit, 0)
            key_pos = offset + jnp.arange(seg_unit, dtype=jnp.int32)
            scores = (
                jnp.einsum("thd,khd->htk", queries, key_blk, preferred_element_type=jnp.float32)
                * inv_root
            )
            weight = pair_weight(own_pos, key_pos, keep_blk, head_ids, bounds, seg_unit)
            return (key_blk, value_blk, scores, weight)

        def stats_step(running, offset):
            row_peak, row_total = running
            _, _, scores, weight = key_block(key_all, value_all, keep_all, offset)
            live = weight > 0
            new_peak = jnp.maximum(row_peak, jnp.max(jnp.where(live, scores, -1e30), axis=2))
            fresh = jnp.sum(
                jnp.where(live, weight * jnp.exp(scores - new_peak[:, :, None]), 0.0), axis=2
            )
            return ((new_peak, row_total * jnp.exp(row_peak - new_peak) + fresh), None)

        start_stats = (
            jnp.full((heads_local, tok_local), -1e30, jnp.float32),
            jnp.zeros((heads_local, tok_local), jnp.float32),
        )
        (row_peak, row_total), _ = lax.scan(stats_step, start_stats, block_starts)
        log_total = row_peak + jnp.log(row_total)

        def value_step(running, offset):
            _, value_blk, scores, weight = key_block(key_all, value_all, keep_all, offset)
            prob_low = (weight * jnp.exp(scores - log_total[:, :, None])).astype(jnp.bfloat16)
            return (
                running
                + jnp.einsum(
                    "htk,khd->thd", prob_low, value_blk, preferred_element_type=jnp.float32
                ),
                None,
            )

        attended, _ = lax.scan(
            value_step, jnp.zeros((tok_local, heads_local, HDIM), jnp.float32), block_starts
        )
        attended_low = attended.astype(jnp.bfloat16).reshape(tok_local, local_width)
        middle = (
            inputs
            + head_total(jnp.dot(attended_low, full_out, preferred_element_type=jnp.float32))
            + obias_rows[0]
        )
        normed_two = layer_norm(middle, gain_rows[1], shift_rows[1]).astype(jnp.bfloat16)
        hidden_pre = jnp.dot(normed_two, full_up, preferred_element_type=jnp.float32) + bias_up
        activated = jax.nn.gelu(hidden_pre, approximate=False).astype(jnp.bfloat16)
        result = (
            middle
            + head_total(jnp.dot(activated, full_down, preferred_element_type=jnp.float32))
            + obias_rows[1]
        )
        out_rows.append(result.astype(jnp.bfloat16))
        grad_out_low = cotangent[micro_id]
        grad_out_f32 = grad_out_low.astype(jnp.float32)
        sum_down = sum_down + jnp.einsum(
            "tf,td->fd", activated, grad_out_low, preferred_element_type=jnp.float32
        )
        grad_act = jnp.einsum(
            "td,fd->tf", grad_out_low, full_down, preferred_element_type=jnp.float32
        )
        _, gelu_back = jax.vjp(partial(jax.nn.gelu, approximate=False), hidden_pre)
        grad_pre_low = gelu_back(grad_act)[0].astype(jnp.bfloat16)
        sum_upb = sum_upb + jnp.sum(grad_pre_low.astype(jnp.float32), axis=0)
        sum_up = sum_up + jnp.einsum(
            "td,tf->df", normed_two, grad_pre_low, preferred_element_type=jnp.float32
        )
        grad_normed_two = head_total(
            jnp.einsum("tf,df->td", grad_pre_low, full_up, preferred_element_type=jnp.float32)
        )
        _, norm_back_two = jax.vjp(layer_norm, middle, gain_rows[1], shift_rows[1])
        grad_from_two, grad_gain_two, grad_shift_two = norm_back_two(grad_normed_two)
        grad_middle = grad_out_f32 + grad_from_two
        grad_branch_low = grad_middle.astype(jnp.bfloat16)
        sum_obias = sum_obias + jnp.stack(
            [jnp.sum(grad_branch_low.astype(jnp.float32), axis=0), jnp.sum(grad_out_f32, axis=0)]
        )
        sum_out = sum_out + jnp.einsum(
            "tf,td->fd", attended_low, grad_branch_low, preferred_element_type=jnp.float32
        )
        grad_attn_low = (
            jnp.einsum("td,fd->tf", grad_branch_low, full_out, preferred_element_type=jnp.float32)
            .astype(jnp.bfloat16)
            .reshape(tok_local, heads_local, HDIM)
        )
        row_delta = jnp.einsum("thd,thd->ht", grad_attn_low.astype(jnp.float32), attended)
        back_keys, back_values, back_keep = (
            lax.all_gather(key_rows, "seq", axis=0, tiled=True),
            lax.all_gather(value_rows, "seq", axis=0, tiled=True),
            lax.all_gather(keep_local, "seq", axis=0, tiled=True),
        )

        def key_side_step(running, offset):
            key_blk, value_blk, scores, weight = key_block(
                back_keys, back_values, back_keep, offset
            )
            prob_f32 = weight * jnp.exp(scores - log_total[:, :, None])
            grad_prob = jnp.einsum(
                "thd,khd->htk", grad_attn_low, value_blk, preferred_element_type=jnp.float32
            )
            grad_scores = (prob_f32 * (grad_prob - row_delta[:, :, None])).astype(jnp.bfloat16)
            running = running + jnp.einsum(
                "htk,khd->thd", grad_scores, key_blk, preferred_element_type=jnp.float32
            )
            prob_low = prob_f32.astype(jnp.bfloat16)
            key_term = (
                jnp.einsum("htk,thd->khd", grad_scores, queries, preferred_element_type=jnp.float32)
                * inv_root
            )
            value_term = jnp.einsum(
                "htk,thd->khd", prob_low, grad_attn_low, preferred_element_type=jnp.float32
            )
            return (
                running,
                jnp.concatenate(
                    [
                        key_term.reshape(seg_unit, local_width),
                        value_term.reshape(seg_unit, local_width),
                    ],
                    axis=1,
                ),
            )

        query_sum, terms = lax.scan(
            key_side_step, jnp.zeros((tok_local, heads_local, HDIM), jnp.float32), block_starts
        )
        owned = lax.psum_scatter(
            terms.reshape(row_len, 2 * local_width), "seq", scatter_dimension=0, tiled=True
        )
        grad_queries = query_sum * inv_root
        grad_keys = owned[:, :local_width].reshape(tok_local, heads_local, HDIM)
        grad_values = owned[:, local_width:].reshape(tok_local, heads_local, HDIM)
        grad_q_low = grad_queries.astype(jnp.bfloat16).reshape(tok_local, local_width)
        grad_k_low = grad_keys.astype(jnp.bfloat16).reshape(tok_local, local_width)
        grad_v_low = grad_values.astype(jnp.bfloat16).reshape(tok_local, local_width)
        sum_qvb = sum_qvb + jnp.stack(
            [
                jnp.sum(grad_q_low.astype(jnp.float32), axis=0),
                jnp.sum(grad_v_low.astype(jnp.float32), axis=0),
            ]
        )
        grad_proj = jnp.stack([grad_q_low, grad_k_low, grad_v_low], axis=1)
        sum_qkv = sum_qkv + jnp.einsum(
            "td,tcf->dcf", normed, grad_proj, preferred_element_type=jnp.float32
        )
        grad_normed = head_total(
            jnp.einsum("tcf,dcf->td", grad_proj, full_qkv, preferred_element_type=jnp.float32)
        )
        _, norm_back_one = jax.vjp(layer_norm, inputs, gain_rows[0], shift_rows[0])
        grad_from_one, grad_gain_one, grad_shift_one = norm_back_one(grad_normed)
        grad_rows.append((grad_middle + grad_from_one).astype(jnp.bfloat16))
        sum_gain = sum_gain + jnp.stack([grad_gain_one, grad_gain_two])
        sum_shift = sum_shift + jnp.stack([grad_shift_one, grad_shift_two])
    grad_qkv, grad_out, grad_up, grad_down, grad_gain, grad_shift, grad_obias = (
        lax.psum_scatter(sum_qkv, "seq", scatter_dimension=0, tiled=True),
        lax.psum_scatter(sum_out, "seq", scatter_dimension=1, tiled=True),
        lax.psum_scatter(sum_up, "seq", scatter_dimension=0, tiled=True),
        lax.psum_scatter(sum_down, "seq", scatter_dimension=1, tiled=True),
        lax.psum_scatter(sum_gain, "seq", scatter_dimension=1, tiled=True),
        lax.psum_scatter(sum_shift, "seq", scatter_dimension=1, tiled=True),
        lax.psum_scatter(sum_obias, "seq", scatter_dimension=1, tiled=True),
    )
    grad_qvb, grad_upb = lax.psum((sum_qvb, sum_upb), "seq")
    return (
        jnp.stack(out_rows),
        jnp.stack(grad_rows),
        grad_gain,
        grad_shift,
        grad_obias,
        grad_qkv,
        grad_qvb,
        grad_out,
        grad_up,
        grad_upb,
        grad_down,
    )


NEG = 1792.0
ROOT = 1.0 / math.sqrt(HDIM)
BF = jnp.bfloat16
F32 = jnp.float32
MESH = pl.DeviceIdType.MESH
LEVELS = [math.sqrt(HDIM) * math.log((b + 1) / b) for b in range(1, BRANCHES)]
LEVEL_HIGH = [float(np.asarray(v, ml_dtypes.bfloat16)) for v in LEVELS]
LEVEL_LOW = [v - w for v, w in zip(LEVELS, LEVEL_HIGH)]


def nn(a, b):
    return lax.dot_general(a, b, (((1,), (0,)), ((), ())), preferred_element_type=F32)


def nt(a, b):
    return lax.dot_general(a, b, (((1,), (1,)), ((), ())), preferred_element_type=F32)


def tn(a, b):
    return lax.dot_general(a, b, (((0,), (0,)), ((), ())), preferred_element_type=F32)


def tt(a, b):
    return lax.dot_general(a, b, (((0,), (1,)), ((), ())), preferred_element_type=F32)


def four(index, values):
    return jnp.where(
        index == 0,
        values[0],
        jnp.where(index == 1, values[1], jnp.where(index == 2, values[2], values[3])),
    )


def pair_features(pos, slide, keep, head, for_keys):
    shape = (16, pos.shape[1])
    row = lax.broadcasted_iota(jnp.int32, shape, 0)
    pos = jnp.broadcast_to(pos, shape)
    slide = jnp.broadcast_to(slide, shape)
    level = jnp.where(row >= 8, row - 8, row - 4)
    on = jnp.bitwise_and(pos - head, four(level, [1, 3, 7, 15])) == 0
    on = on & (row < 12)
    if for_keys:
        keep = jnp.broadcast_to(keep, shape)
        size = jnp.where(row < 8, four(level, LEVEL_HIGH), four(level, LEVEL_LOW))
        other = jnp.where(slide != row, -NEG, 0.0)
        padding = jnp.where(keep > 0.0, 0.0, -NEG)
    else:
        size = jnp.ones(shape, F32)
        other = jnp.where(slide == row, 1.0, 0.0)
        padding = jnp.ones(shape, F32)
    value = jnp.where(row < 3, other, jnp.where(row == 3, padding, jnp.where(on, size, 0.0)))
    return value.astype(BF)


def layer_kernel(*refs, names):
    r_ = dict(zip(names, refs))

    class N:
        pass

    g = N()
    for k, v in r_.items():
        setattr(g, k, v)
    s = lax.axis_index("seq")
    h = lax.axis_index("head")
    z, y = lax.div(s, 2), lax.rem(s, 2)
    x, c = lax.div(h, 2), lax.rem(h, 2)
    a, j = lax.div(s, 4), lax.rem(s, 4)
    sib = (s, h + 1 - 2 * c)
    xp = (s, lax.rem(h + 2, 4))
    yp = (s + 1 - 2 * y, h)
    zs = [lax.rem(z + d, 4) for d in (1, 2, 3)]
    zm = [(2 * q + y, h) for q in zs]
    part = [(4 * c + i, 2 * x + a) for i in range(4)]
    own = [(a == c) & (j == i) for i in range(4)]
    is_own = jnp.where(a == c, 1, 0)
    head = 8 * x + s
    R = 3
    T = 128

    def rdma(src, dst, ss, rs, dev):
        return pltpu.make_async_remote_copy(
            src_ref=src, dst_ref=dst, send_sem=ss, recv_sem=rs, device_id=dev, device_id_type=MESH
        )

    def not_own(i):
        return jnp.logical_not(own[i])

    def lanes(r, n=128):
        return pl.ds(pl.multiple_of(n * r, n), n)

    def rows(r, n=128):
        return pl.ds(pl.multiple_of(n * r, n), n)

    def half(r, who):
        return pl.ds(pl.multiple_of(T * r + 64 * who, 64), 64)

    bar = pltpu.get_barrier_semaphore()
    for dev in [sib, xp, yp] + zm:
        pl.semaphore_signal(bar, inc=1, device_id=dev, device_id_type=MESH)
    for i in range(4):

        @pl.when(not_own(i))
        def _():
            pl.semaphore_signal(bar, inc=1, device_id=part[i], device_id_type=MESH)

    pl.semaphore_wait(bar, 10 - is_own)

    W = [g.wq, g.wo, g.wu, g.wd]

    def ag_start(p):
        w = W[p]
        for t, dev in enumerate([yp] + zm):
            rdma(w.at[s], w.at[s], g.ag_s.at[p, t], g.ag_r.at[p, s], dev).start()

    def ag_forward(p):
        w = W[p]
        for t in range(3):
            k = zm[t][0]
            rdma(w.at[k], w.at[k], g.ag_s.at[p, 4 + t], g.ag_r.at[p, k], zm[t]).wait_recv()
            rdma(w.at[k], w.at[k], g.ag_s.at[p, 4 + t], g.ag_r.at[p, k], yp).start()

    def ag_wait(p):
        w = W[p]
        for q in range(4):
            k = 2 * q + 1 - y
            rdma(w.at[k], w.at[k], g.ag_s.at[p, 0], g.ag_r.at[p, k], yp).wait_recv()

    def ag_drain(p):
        w = W[p]
        for t in range(7):
            rdma(w.at[s], w.at[s], g.ag_s.at[p, t], g.ag_r.at[p, s], yp).wait_send()

    g.wq[s] = g.in_wq[...]
    ag_start(0)
    g.wu[s] = g.in_wu[...]
    g.wo[s] = jnp.transpose(g.in_wo[...])
    g.wd[s] = jnp.transpose(g.in_wd[...])

    lane = lax.broadcasted_iota(jnp.int32, (1, 768), 1)
    freq = jnp.exp(
        -math.log(10000.0) * lax.rem(lane, 192).astype(F32) / 192.0
    )
    for r in range(R):
        col = jnp.transpose(g.in_crd[r])
        pieces = []
        for t in range(6):
            f = freq[:, 128 * t : 128 * t + 128]
            ang = col[:, (0 if t < 3 else 1) : (1 if t < 3 else 2)] * f
            if t % 3 == 0:
                pieces.append(jnp.sin(ang))
            elif t % 3 == 2:
                pieces.append(jnp.cos(ang))
            else:
                low_half = lax.broadcasted_iota(jnp.int32, (T, 128), 1) < 64
                pieces.append(jnp.where(low_half, jnp.sin(ang), jnp.cos(ang)))
        v = g.in_tok[rows(r), :].astype(F32) + jnp.concatenate(pieces, axis=1)
        g.inp[rows(r), :] = v
        v = v - jnp.mean(v, axis=1, keepdims=True)
        rstd = lax.rsqrt(jnp.mean(v * v, axis=1, keepdims=True) + EPSILON)
        g.n1[rows(r), :] = v * rstd
        g.rstd1[rows(r), :] = rstd
        g.cotT[:, 128 * r : 128 * r + 128] = jnp.transpose(g.in_cot[rows(r), :])
    g.sums[...] = jnp.zeros_like(g.sums)

    ag_forward(0)
    ag_start(1)
    ag_start(2)
    ag_wait(0)

    par = jnp.concatenate([g.wq[k, 96:112, 0:96].astype(F32) for k in range(8)], axis=1)
    g.par[...] = par
    g1, s1, ob0, ob1 = par[1:2], par[3:4], par[4:5], par[5:6]
    g0 = par[0:1]
    qvb = g.in_qvb[...].astype(F32)
    qkv_bias = jnp.concatenate([qvb[0:1], jnp.zeros((1, 192), F32), qvb[1:2]], axis=1)

    def send_part(i, r, src, dst, ss, rs):
        @pl.when(not_own(i))
        def _():
            rdma(src.at[i, r], dst.at[j, r], ss.at[i, r], rs.at[j, r], part[i]).start()

        @pl.when(own[i])
        def _():
            dst[i, r] = src[i, r]

    def wait_part(i, r, dst, ss, rs):
        @pl.when(not_own(i))
        def _():
            rdma(dst.at[i, r], dst.at[i, r], ss.at[i, r], rs.at[i, r], part[i]).wait_recv()

    def drain_part(i, r, src, ss, rs):
        @pl.when(not_own(i))
        def _():
            rdma(src.at[i, r], src.at[i, r], ss.at[i, r], rs.at[i, r], part[i]).wait_send()

    for r in range(R):
        nr = (g.n1[rows(r), :] * g0 + par[2:3]).astype(BF)
        g.nrmT[:, 128 * r : 128 * r + 128] = jnp.transpose(nr)
        proj = nn(nr, g.wq[:, 0:96, :].reshape(768, 576)) + qkv_bias
        projT = jnp.transpose(proj).astype(BF)
        for i in range(4):
            for t in range(3):
                g.snA[i, r, 48 * t : 48 * t + 48, :] = projT[192 * t + 48 * i : 192 * t + 48 * i + 48]
            send_part(i, r, g.snA, g.rcA, g.qa_s, g.qa_r)

    ag_forward(1)
    ag_start(3)

    def slide_of_row(r, pos):
        b0 = g.in_len[r, 0]
        b1 = b0 + g.in_len[r, 1]
        return jnp.where(pos >= b0, 1, 0) + jnp.where(pos >= b1, 1, 0)

    ones_rows = jnp.where(lax.broadcasted_iota(jnp.int32, (16, 1024), 0) == 0, 1.0, 0.0).astype(BF)

    def attn_fwd(r):
        for i in range(4):
            wait_part(i, r, g.rcA, g.qa_s, g.qa_r)
            rdma(
                g.rcA.at[i, r, pl.ds(48, 96)], g.sbA.at[i, r], g.sa_s.at[i, r], g.sa_r.at[i, r], sib
            ).start()
        iota = lax.broadcasted_iota(jnp.int32, (1, 512), 1)
        pos_own = 512 * c + iota
        pos_sib = 512 * (1 - c) + iota
        keep_own = jnp.concatenate(
            [g.wq[4 * c + i, 96:112, 0:128].astype(F32)[6 + r : 7 + r] for i in range(4)], axis=1
        )
        keep_sib = jnp.concatenate(
            [g.wq[4 * (1 - c) + i, 96:112, 0:128].astype(F32)[6 + r : 7 + r] for i in range(4)], axis=1
        )
        pos = jnp.concatenate([pos_own, pos_sib], axis=1)
        kf = pair_features(
            pos, slide_of_row(r, pos), jnp.concatenate([keep_own, keep_sib], axis=1), head, True
        )
        qf = pair_features(pos_own, slide_of_row(r, pos_own), None, head, False)
        g.QT[r, 0:48, :] = jnp.concatenate([g.rcA[i, r, 0:48, :] for i in range(4)], axis=1)
        g.QT[r, 48:64, :] = qf
        g.KT[r, 48:64, :] = kf
        g.VT[r, 48:64, :] = ones_rows
        for i in range(4):
            g.KT[r, 0:48, 128 * i : 128 * i + 128] = g.rcA[i, r, 48:96, :]
            g.VT[r, 0:48, 128 * i : 128 * i + 128] = g.rcA[i, r, 96:144, :]
        for i in range(4):
            rdma(g.sbA.at[i, r], g.sbA.at[i, r], g.sa_s.at[i, r], g.sa_r.at[i, r], sib).wait_recv()
            g.KT[r, 0:48, 512 + 128 * i : 640 + 128 * i] = g.sbA[i, r, 0:48, :]
            g.VT[r, 0:48, 512 + 128 * i : 640 + 128 * i] = g.sbA[i, r, 48:96, :]
        eye = lax.broadcasted_iota(jnp.int32, (256, 256), 0) == lax.broadcasted_iota(
            jnp.int32, (256, 256), 1
        )
        for qc in range(2):
            q0 = 256 * qc
            sc = tn(g.KT[r], g.QT[r, :, q0 : q0 + 256])
            lift = jnp.where(eye, NEG * (1.0 - keep_own[:, q0 : q0 + 256]), 0.0)
            blocks = [sc[256 * t : 256 * t + 256] for t in range(4)]
            blocks[qc] = blocks[qc] + lift
            sc = jnp.concatenate(blocks, axis=0)
            peak = jnp.max(sc, axis=0, keepdims=True)
            pb = jnp.exp((sc - peak) * ROOT).astype(BF)
            g.P[r, :, q0 : q0 + 256] = pb
            o = nn(g.VT[r], pb)
            inv = 1.0 / o[48:49]
            o = o[0:48] * inv
            g.O[r, :, q0 : q0 + 256] = o
            g.inv[r, :, q0 : q0 + 256] = jnp.broadcast_to(inv, (8, 256))
            for u in range(2):
                i = 2 * qc + u
                g.snO[i, r] = o[:, 128 * u : 128 * u + 128].astype(BF)
                send_part(i, r, g.snO, g.rcO, g.o_s, g.o_r)

    attn_fwd(0)
    ag_forward(2)
    attn_fwd(1)
    attn_fwd(2)
    ag_forward(3)

    def ps_start(kind, r, part_sum):
        g.ps[kind, r] = part_sum.astype(BF)
        rdma(
            g.ps.at[kind, r, pl.ds(pl.multiple_of(64 * (1 - c), 64), 64)],
            g.psA.at[kind, r],
            g.ps_s.at[kind, r, 0],
            g.ps_r.at[kind, r, 0],
            sib,
        ).start()

    def ps_mid(kind, r):
        dst = g.psA.at[kind, r]
        rdma(dst, dst, g.ps_s.at[kind, r, 0], g.ps_r.at[kind, r, 0], sib).wait_recv()
        mine = g.ps[kind, r, pl.ds(pl.multiple_of(64 * c, 64), 64), :].astype(F32)
        g.psH[kind, r] = (mine + g.psA[kind, r].astype(F32)).astype(BF)
        rdma(
            g.psH.at[kind, r], g.psB.at[kind, r], g.ps_s.at[kind, r, 1], g.ps_r.at[kind, r, 1], xp
        ).start()

    def ps_end(kind, r):
        dst = g.psB.at[kind, r]
        rdma(dst, dst, g.ps_s.at[kind, r, 1], g.ps_r.at[kind, r, 1], xp).wait_recv()
        return g.psH[kind, r].astype(F32) + g.psB[kind, r].astype(F32)

    def share_start(ref, r, ss, rs):
        rdma(ref.at[half(r, c)], ref.at[half(r, c)], ss.at[r], rs.at[r], sib).start()

    def share_wait(ref, r, ss, rs):
        dst = ref.at[half(r, 1 - c)]
        rdma(dst, dst, ss.at[r], rs.at[r], sib).wait_recv()

    ag_wait(1)
    for r in range(R):
        for i in range(4):
            wait_part(i, r, g.rcO, g.o_s, g.o_r)
            g.attT[48 * i : 48 * i + 48, 128 * r : 128 * r + 128] = g.rcO[i, r]
        att = jnp.transpose(g.attT[:, 128 * r : 128 * r + 128])
        ps_start(0, r, nt(att, g.wo[...].reshape(768, 192)))
        if r > 0:
            ps_mid(0, r - 1)
    ps_mid(0, R - 1)
    ag_wait(2)
    ag_wait(3)

    def second_norm(r):
        v = g.inp[half(r, c), :] + ps_end(0, r) + ob0
        g.mid[r] = v
        v = v - jnp.mean(v, axis=1, keepdims=True)
        rstd = lax.rsqrt(jnp.mean(v * v, axis=1, keepdims=True) + EPSILON)
        v = v * rstd
        g.n2[r] = v
        g.rstd2[r] = rstd
        g.ntk[half(r, c), :] = (v * g1 + s1).astype(BF)
        share_start(g.ntk, r, g.nt_s, g.nt_r)

    up_bias = g.in_upb[...].astype(F32)

    def feed_forward(r):
        share_wait(g.ntk, r, g.nt_s, g.nt_r)
        pre = nn(g.ntk[rows(r), :], g.wu[...].reshape(768, 768)) + up_bias
        cdf = 0.5 * (1.0 + lax.erf(pre * (1.0 / math.sqrt(2.0))))
        pdf = jnp.exp(-0.5 * pre * pre) * (1.0 / math.sqrt(2.0 * math.pi))
        g.act[rows(r), :] = (pre * cdf).astype(BF)
        gact = nn(g.in_cot[rows(r), :], g.wd[...].reshape(768, 768))
        g.gp[rows(r), :] = (gact * (cdf + pre * pdf)).astype(BF)
        ps_start(1, r, nt(g.gp[rows(r), :], g.wu[...].reshape(768, 768)))

    second_norm(0)
    second_norm(1)
    feed_forward(0)
    second_norm(2)
    feed_forward(1)
    ps_mid(1, 0)
    feed_forward(2)
    ps_mid(1, 1)

    def block(p, k):
        b = pl.ds(pl.multiple_of(96 * k, 96), 96)
        if p == 0:
            return nt(g.nrmT[b, :], g.gpT[...])
        if p == 1:
            return nt(g.gbT[b, :], g.attT[...])
        if p == 2:
            return nn(g.ntT[b, :], g.gp[...])
        return nn(g.cotT[b, :], g.act[...])

    L1S = [g.l1s0, g.l1s1, g.l1s2, g.l1s3]
    L1R = [g.l1r0, g.l1r1, g.l1r2, g.l1r3]
    L2S = [g.l2s0, g.l2s1, g.l2s2, g.l2s3]
    L2R = [g.l2r0, g.l2r1, g.l2r2, g.l2r3]
    ACC = [g.out_gqkv, g.out_gout, g.out_gup, g.out_gdown]

    def rs_first(p):
        def step(q, _):
            L1S[p][q] = block(p, 2 * q + 1 - y).astype(BF)
            rdma(L1S[p].at[q], L1R[p].at[q], g.l1_s.at[p, q], g.l1_r.at[p, q], yp).start()
            return 0

        lax.fori_loop(0, 4, step, 0)

    def rs_second(p):
        def step(t, _):
            q = lax.rem(z + t, 4)
            dst = L1R[p].at[q]
            rdma(dst, dst, g.l1_s.at[p, q], g.l1_r.at[p, q], yp).wait_recv()
            L2S[p][q] = (block(p, 2 * q + y) + L1R[p][q].astype(F32)).astype(BF)
            rdma(
                L2S[p].at[q], L2R[p].at[z], g.l2_s.at[p, q], g.l2_r.at[p, z], (2 * q + y, h)
            ).start()
            return 0

        lax.fori_loop(1, 4, step, 0)
        dst = L1R[p].at[z]
        rdma(dst, dst, g.l1_s.at[p, z], g.l1_r.at[p, z], yp).wait_recv()
        ACC[p][...] = block(p, s) + L1R[p][z].astype(F32)

    def rs_third(p):
        for t in (1, 2, 3):
            q = lax.rem(z + t, 4)
            dst = L2R[p].at[q]
            rdma(dst, dst, g.l2_s.at[p, q], g.l2_r.at[p, q], yp).wait_recv()
            ACC[p][...] += dst[...].astype(F32)

    def rs_drain(p):
        for q in range(4):
            rdma(L1S[p].at[q], L1R[p].at[q], g.l1_s.at[p, q], g.l1_r.at[p, q], yp).wait_send()
        for t in (1, 2, 3):
            q = lax.rem(z + t, 4)
            rdma(L2S[p].at[q], L2R[p].at[q], g.l2_s.at[p, q], g.l2_r.at[p, q], yp).wait_send()

    rs_first(3)
    ps_mid(1, 2)
    g.ntT[...] = jnp.transpose(g.ntk[...])
    rs_first(2)

    def add_sum(row, value):
        g.sums[row : row + 1, :] += jnp.sum(value, axis=0, keepdims=True)

    def norm_back(grad, n, rstd, gain):
        e = grad * gain
        return rstd * (
            e - jnp.mean(e, axis=1, keepdims=True) - n * jnp.mean(e * n, axis=1, keepdims=True)
        )

    def second_back(r):
        gn = ps_end(1, r)
        n = g.n2[r]
        cot = g.in_cot[half(r, c), :].astype(F32)
        gm = cot + norm_back(gn, n, g.rstd2[r], g1)
        g.gm[r] = gm
        gb = gm.astype(BF)
        g.gb[half(r, c), :] = gb
        share_start(g.gb, r, g.gb_s, g.gb_r)
        add_sum(1, gn * n)
        add_sum(3, gn)
        add_sum(4, gb.astype(F32))
        add_sum(5, cot)

    def grad_attended(r):
        share_wait(g.gb, r, g.gb_s, g.gb_r)
        ga = jnp.transpose(nn(g.gb[rows(r), :], g.wo[...].reshape(768, 192))).astype(BF)
        for i in range(4):
            g.snD[i, r] = ga[48 * i : 48 * i + 48]
            send_part(i, r, g.snD, g.rcD, g.d_s, g.d_r)

    second_back(0)
    second_back(1)
    grad_attended(0)
    second_back(2)
    grad_attended(1)
    grad_attended(2)

    for r in range(R):
        ps_start(2, r, nt(g.act[rows(r), :], g.wd[...].reshape(768, 768)))
    g.gbT[...] = jnp.transpose(g.gb[...])
    rs_first(1)
    for r in range(R):
        ps_mid(2, r)

    def attn_bwd(r):
        for i in range(4):
            wait_part(i, r, g.rcD, g.d_s, g.d_r)
        dk = None
        dv = None
        for qc in range(2):
            q0 = 256 * qc
            do = jnp.concatenate([g.rcD[2 * qc, r], g.rcD[2 * qc + 1, r]], axis=1)
            delta = jnp.sum(do.astype(F32) * g.O[r, :, q0 : q0 + 256], axis=0, keepdims=True)
            dp = tn(g.VT[r, 0:48, :], do)
            pn = g.P[r, :, q0 : q0 + 256].astype(F32) * g.inv[r, 0:1, q0 : q0 + 256]
            ds = (pn * (dp - delta)).astype(BF)
            pn = pn.astype(BF)
            dq = nn(g.KT[r, 0:48, :], ds) * ROOT
            for u in range(2):
                g.snG[2 * qc + u, r, 0:48, :] = dq[:, 128 * u : 128 * u + 128].astype(BF)
            dk_part = nt(g.QT[r, 0:48, q0 : q0 + 256], ds)
            dv_part = nt(do, pn)
            dk = dk_part if dk is None else dk + dk_part
            dv = dv_part if dv is None else dv + dv_part
        dk = dk * ROOT
        g.snX[r, 0:48, :] = dk[:, 512:1024]
        g.snX[r, 48:96, :] = dv[:, 512:1024]
        rdma(g.snX.at[r], g.rcX.at[r], g.x_s.at[r], g.x_r.at[r], sib).start()
        g.kvX[r, 0:48, :] = dk[:, 0:512]
        g.kvX[r, 48:96, :] = dv[:, 0:512]

    def attn_bwd_end(r):
        rdma(g.rcX.at[r], g.rcX.at[r], g.x_s.at[r], g.x_r.at[r], sib).wait_recv()
        kv = (g.kvX[r] + g.rcX[r]).astype(BF)
        for i in range(4):
            g.snG[i, r, 48:144, :] = kv[:, 128 * i : 128 * i + 128]
            send_part(i, r, g.snG, g.rcG, g.g_s, g.g_r)

    attn_bwd(0)
    rs_second(3)
    attn_bwd_end(0)
    attn_bwd(1)
    rs_second(2)
    attn_bwd_end(1)
    attn_bwd(2)
    rs_second(1)
    attn_bwd_end(2)

    for r in range(R):
        g.out_tok[half(r, c), :] = (g.mid[r] + ps_end(2, r) + ob1).astype(BF)
        share_start(g.out_tok, r, g.ot_s, g.ot_r)
    ones = jnp.ones((8, 384), BF)
    g.sums[6:7, :] = nn(ones, g.gp[...])[0:1]

    for r in range(R):
        for i in range(4):
            wait_part(i, r, g.rcG, g.g_s, g.g_r)
            for t in range(3):
                g.gpT[192 * t + 48 * i : 192 * t + 48 * i + 48, 128 * r : 128 * r + 128] = g.rcG[
                    i, r, 48 * t : 48 * t + 48, :
                ]
        ps_start(3, r, tt(g.gpT[:, 128 * r : 128 * r + 128], g.wq[:, 0:96, :].reshape(768, 576)))
        if r > 0:
            ps_mid(3, r - 1)
    rs_first(0)
    ps_mid(3, R - 1)
    g.sums[7:8, 0:576] = nt(ones, g.gpT[...])[0:1]

    rs_third(3)
    rs_third(2)
    rs_third(1)

    def first_back(r):
        gn = ps_end(3, r)
        n = g.n1[half(r, c), :]
        gt = g.gm[r] + norm_back(gn, n, g.rstd1[half(r, c), :], g0)
        g.out_gtok[half(r, c), :] = gt.astype(BF)
        share_start(g.out_gtok, r, g.gt_s, g.gt_r)
        add_sum(0, gn * n)
        add_sum(2, gn)

    for r in range(R):
        first_back(r)
    rdma(g.sums, g.sumA, g.sm_s.at[0], g.sm_r.at[0], sib).start()
    rs_second(0)
    rdma(g.sumA, g.sumA, g.sm_s.at[0], g.sm_r.at[0], sib).wait_recv()
    both = lax.broadcasted_iota(jnp.int32, (8, 768), 0) < 6
    g.sumB[...] = g.sums[...] + jnp.where(both, g.sumA[...], 0.0)
    rdma(g.sumB, g.sumC, g.sm_s.at[1], g.sm_r.at[1], yp).start()
    rdma(g.sumC, g.sumC, g.sm_s.at[1], g.sm_r.at[1], yp).wait_recv()
    g.sumD[z] = g.sumB[...] + g.sumC[...]
    for t in range(3):
        rdma(g.sumD.at[z], g.sumD.at[z], g.sm_s.at[2 + t], g.sm_r.at[2 + z], zm[t]).start()
    rs_third(0)
    for t in range(3):
        q = zs[t]
        rdma(g.sumD.at[q], g.sumD.at[q], g.sm_s.at[2 + t], g.sm_r.at[2 + q], zm[t]).wait_recv()
    total = g.sumD[0] + g.sumD[1] + g.sumD[2] + g.sumD[3]
    g.out_sums[...] = total
    for k in range(8):
        g.cut[k] = total[:, 96 * k : 96 * k + 96]
    g.out_cut[...] = g.cut[s]

    for r in range(R):
        share_wait(g.out_tok, r, g.ot_s, g.ot_r)
        share_wait(g.out_gtok, r, g.gt_s, g.gt_r)
    for p in range(4):
        ag_drain(p)
        rs_drain(p)
    for r in range(R):
        for i in range(4):
            drain_part(i, r, g.snA, g.qa_s, g.qa_r)
            drain_part(i, r, g.snO, g.o_s, g.o_r)
            drain_part(i, r, g.snD, g.d_s, g.d_r)
            drain_part(i, r, g.snG, g.g_s, g.g_r)
            rdma(g.sbA.at[i, r], g.sbA.at[i, r], g.sa_s.at[i, r], g.sa_r.at[i, r], sib).wait_send()
        rdma(g.snX.at[r], g.rcX.at[r], g.x_s.at[r], g.x_r.at[r], sib).wait_send()
        for kind in range(4):
            for t in range(2):
                rdma(
                    g.psH.at[kind, r], g.psB.at[kind, r], g.ps_s.at[kind, r, t], g.ps_r.at[kind, r, t], xp
                ).wait_send()
        for ref, ss, rs in (
            (g.ntk, g.nt_s, g.nt_r),
            (g.gb, g.gb_s, g.gb_r),
            (g.out_tok, g.ot_s, g.ot_r),
            (g.out_gtok, g.gt_s, g.gt_r),
        ):
            rdma(ref.at[half(r, c)], ref.at[half(r, c)], ss.at[r], rs.at[r], sib).wait_send()
    rdma(g.sums, g.sumA, g.sm_s.at[0], g.sm_r.at[0], sib).wait_send()
    rdma(g.sumB, g.sumC, g.sm_s.at[1], g.sm_r.at[1], yp).wait_send()
    for t in range(3):
        rdma(g.sumD.at[z], g.sumD.at[z], g.sm_s.at[2 + t], g.sm_r.at[2 + z], zm[t]).wait_send()


def fast_device(
    tokens, cotangent, lengths, coords, keep_mask, ln_gains, ln_shifts, out_bias,
    w_qkv, qv_bias, w_out, w_up, up_bias, w_down,
):
    small = jnp.concatenate([ln_gains, ln_shifts, out_bias], axis=0)
    small = jnp.pad(small, ((0, 0), (0, 480)))
    keep = jnp.pad(keep_mask.astype(BF), ((0, 7), (0, 448)))
    shard = jnp.concatenate([w_qkv.reshape(96, 576), small, keep], axis=0)
    crd = jnp.pad(jnp.transpose(coords, (1, 0, 2)).astype(F32), ((0, 0), (0, 6), (0, 0)))
    inputs = [
        ("in_tok", tokens.reshape(384, 768)),
        ("in_cot", cotangent.reshape(384, 768)),
        ("in_len", lengths),
        ("in_crd", crd),
        ("in_wq", shard),
        ("in_qvb", qv_bias),
        ("in_wo", w_out),
        ("in_wu", w_up),
        ("in_upb", up_bias.reshape(1, 768)),
        ("in_wd", w_down),
    ]
    outputs = [
        ("out_tok", (384, 768), BF),
        ("out_gtok", (384, 768), BF),
        ("out_gqkv", (96, 576), F32),
        ("out_gout", (96, 192), F32),
        ("out_gup", (96, 768), F32),
        ("out_gdown", (96, 768), F32),
        ("out_sums", (8, 768), F32),
        ("out_cut", (8, 96), F32),
    ]
    vm = [
        ("wq", (8, 112, 576), BF),
        ("wo", (8, 96, 192), BF),
        ("wu", (8, 96, 768), BF),
        ("wd", (8, 96, 768), BF),
        ("inp", (384, 768), F32),
        ("n1", (384, 768), F32),
        ("rstd1", (384, 1), F32),
        ("cotT", (768, 384), BF),
        ("nrmT", (768, 384), BF),
        ("par", (16, 768), F32),
        ("sums", (8, 768), F32),
        ("sumA", (8, 768), F32),
        ("sumB", (8, 768), F32),
        ("sumC", (8, 768), F32),
        ("sumD", (4, 8, 768), F32),
        ("cut", (8, 8, 96), F32),
        ("snA", (4, 3, 144, 128), BF),
        ("rcA", (4, 3, 144, 128), BF),
        ("sbA", (4, 3, 96, 128), BF),
        ("QT", (3, 64, 512), BF),
        ("KT", (3, 64, 1024), BF),
        ("VT", (3, 64, 1024), BF),
        ("P", (3, 1024, 512), BF),
        ("O", (3, 48, 512), F32),
        ("inv", (3, 8, 512), F32),
        ("snO", (4, 3, 48, 128), BF),
        ("rcO", (4, 3, 48, 128), BF),
        ("snD", (4, 3, 48, 128), BF),
        ("rcD", (4, 3, 48, 128), BF),
        ("snG", (4, 3, 144, 128), BF),
        ("rcG", (4, 3, 144, 128), BF),
        ("snX", (3, 96, 512), F32),
        ("rcX", (3, 96, 512), F32),
        ("kvX", (3, 96, 512), F32),
        ("attT", (192, 384), BF),
        ("gpT", (576, 384), BF),
        ("ps", (4, 3, 128, 768), BF),
        ("psA", (4, 3, 64, 768), BF),
        ("psH", (4, 3, 64, 768), BF),
        ("psB", (4, 3, 64, 768), BF),
        ("mid", (3, 64, 768), F32),
        ("n2", (3, 64, 768), F32),
        ("rstd2", (3, 64, 1), F32),
        ("gm", (3, 64, 768), F32),
        ("ntk", (384, 768), BF),
        ("ntT", (768, 384), BF),
        ("act", (384, 768), BF),
        ("gp", (384, 768), BF),
        ("gb", (384, 768), BF),
        ("gbT", (768, 384), BF),
    ]
    for p, width in enumerate((576, 192, 768, 768)):
        for kind in ("l1s", "l1r", "l2s", "l2r"):
            vm.append((f"{kind}{p}", (4, 96, width), BF))
    sems = [
        ("ag_s", (4, 7)), ("ag_r", (4, 8)),
        ("qa_s", (4, 3)), ("qa_r", (4, 3)),
        ("sa_s", (4, 3)), ("sa_r", (4, 3)),
        ("o_s", (4, 3)), ("o_r", (4, 3)),
        ("d_s", (4, 3)), ("d_r", (4, 3)),
        ("g_s", (4, 3)), ("g_r", (4, 3)),
        ("x_s", (3,)), ("x_r", (3,)),
        ("ps_s", (4, 3, 2)), ("ps_r", (4, 3, 2)),
        ("nt_s", (3,)), ("nt_r", (3,)),
        ("gb_s", (3,)), ("gb_r", (3,)),
        ("ot_s", (3,)), ("ot_r", (3,)),
        ("gt_s", (3,)), ("gt_r", (3,)),
        ("l1_s", (4, 4)), ("l1_r", (4, 4)),
        ("l2_s", (4, 4)), ("l2_r", (4, 4)),
        ("sm_s", (8,)), ("sm_r", (8,)),
    ]
    names = [n for n, _ in inputs] + [o[0] for o in outputs] + [v[0] for v in vm] + [n for n, _ in sems]
    vmem = pl.BlockSpec(memory_space=pltpu.VMEM)
    out = pl.pallas_call(
        partial(layer_kernel, names=names),
        out_shape=[jax.ShapeDtypeStruct(shape, dtype) for _, shape, dtype in outputs],
        in_specs=[
            pl.BlockSpec(memory_space=pltpu.SMEM) if n == "in_len" else vmem for n, _ in inputs
        ],
        out_specs=[vmem] * len(outputs),
        scratch_shapes=[pltpu.VMEM(shape, dtype) for _, shape, dtype in vm]
        + [pltpu.SemaphoreType.DMA(shape) for _, shape in sems],
        compiler_params=pltpu.CompilerParams(
            collective_id=0, has_side_effects=True, vmem_limit_bytes=60 * 1024 * 1024
        ),
    )(*[v for _, v in inputs])
    out_tok, out_gtok, gqkv, gout, gup, gdown, sums, cut = out
    return (
        out_tok.reshape(3, 128, 768),
        out_gtok.reshape(3, 128, 768),
        cut[0:2],
        cut[2:4],
        cut[4:6],
        gqkv.reshape(96, 3, 192),
        jnp.stack([sums[7, 0:192], sums[7, 384:576]]),
        jnp.transpose(gout),
        gup,
        sums[6],
        jnp.transpose(gdown),
    )


def solution(mesh):
    placed = (
        P(None, "seq", None),
        P(None, "seq", None),
        P(),
        P(None, None, "seq"),
        P(None, "seq"),
        P(None, "seq"),
        P(None, "seq"),
        P(None, "seq"),
        P("seq", None, "head"),
        P(None, "head"),
        P("head", "seq"),
        P("seq", "head"),
        P("head"),
        P("head", "seq"),
    )
    layout = (mesh.shape["seq"], mesh.shape["head"])

    def step(tokens, *others):
        one_kernel = layout == (8, 4) and tokens.shape == (3, 1024, 768)
        return over(fast_device if one_kernel else per_device)(tokens, *others)

    def over(device):
        return jax.shard_map(
        device,
        mesh=mesh,
        in_specs=placed,
        out_specs=(
            P(None, "seq", None),
            P(None, "seq", None),
            P(None, "seq"),
            P(None, "seq"),
            P(None, "seq"),
            P("seq", None, "head"),
            P(None, "head"),
            P("head", "seq"),
            P("seq", "head"),
            P("head"),
            P("head", "seq"),
        ),
        check_vma=False,
    )

    return step
```

```python
from functools import partial
import math

import jax
import jax.numpy as jnp
import ml_dtypes
import numpy as np
from jax import lax
from jax.experimental import pallas as pl
from jax.experimental.pallas import tpu as pltpu
from jax.sharding import PartitionSpec as P

HDIM = 48
UNIT = 1024
BRANCHES = 5


EPSILON = 1e-05


def position_table(grid_rows, width):
    quarter = width // 4
    frequency = jnp.exp(-jnp.log(10000.0) * jnp.arange(quarter, dtype=jnp.float32) / quarter)
    along_row = grid_rows[0].astype(jnp.float32)[:, None] * frequency[None, :]
    along_col = grid_rows[1].astype(jnp.float32)[:, None] * frequency[None, :]
    return jnp.concatenate(
        [jnp.sin(along_row), jnp.cos(along_row), jnp.sin(along_col), jnp.cos(along_col)], axis=1
    )


def layer_norm(values, gain_vec, shift_vec):
    centre = values - jnp.mean(values, axis=-1, keepdims=True)
    spread = jnp.mean(centre * centre, axis=-1, keepdims=True)
    return centre * lax.rsqrt(spread + EPSILON) * gain_vec + shift_vec


def slide_of(positions, bounds):
    return jnp.sum((positions[:, None] >= bounds[None, :]).astype(jnp.int32), axis=1)


def pair_weight(query_pos, key_pos, key_keep, head_ids, bounds, seg_unit):
    same_slide = slide_of(query_pos, bounds)[:, None] == slide_of(key_pos, bounds)[None, :]
    visible = same_slide & ((key_keep[None, :] > 0) | (query_pos[:, None] == key_pos[None, :]))
    counted = jnp.zeros((head_ids.shape[0], query_pos.shape[0], key_pos.shape[0]), jnp.float32)
    for branch in range(BRANCHES):
        stride = 2**branch
        span = seg_unit * stride
        same_seg = query_pos[:, None] // span == key_pos[None, :] // span
        query_on = query_pos[None, :] % stride == head_ids[:, None] % stride
        key_on = key_pos[None, :] % stride == head_ids[:, None] % stride
        counted = counted + (same_seg[None] & query_on[:, :, None] & key_on[:, None, :]).astype(
            jnp.float32
        )
    return counted * visible[None].astype(jnp.float32)


def head_total(partial_sum):
    return lax.psum(partial_sum.astype(jnp.bfloat16), "head").astype(jnp.float32)


def per_device(
    tokens,
    cotangent,
    lengths,
    coords,
    keep_mask,
    ln_gains,
    ln_shifts,
    out_bias,
    w_qkv,
    qv_bias,
    w_out,
    w_up,
    up_bias,
    w_down,
):
    micro_count, tok_local, width = tokens.shape
    row_len = tok_local * lax.axis_size("seq")
    seg_unit = UNIT
    block_count = row_len // seg_unit
    heads_local = w_qkv.shape[2] // HDIM
    local_width = heads_local * HDIM
    inv_root = 1.0 / math.sqrt(HDIM)
    head_ids = lax.axis_index("head") * heads_local + jnp.arange(heads_local, dtype=jnp.int32)
    own_pos = lax.axis_index("seq") * tok_local + jnp.arange(tok_local, dtype=jnp.int32)
    block_starts = jnp.arange(block_count, dtype=jnp.int32) * seg_unit
    bias_qv = qv_bias.astype(jnp.float32)
    bias_up = up_bias.astype(jnp.float32)
    sum_qkv = jnp.zeros((width, 3, local_width), jnp.float32)
    sum_out = jnp.zeros((local_width, width), jnp.float32)
    sum_up = jnp.zeros((width, w_up.shape[1]), jnp.float32)
    sum_down = jnp.zeros((w_down.shape[0], width), jnp.float32)
    sum_gain = jnp.zeros((2, width), jnp.float32)
    sum_shift = jnp.zeros((2, width), jnp.float32)
    sum_obias = jnp.zeros((2, width), jnp.float32)
    sum_qvb = jnp.zeros((2, local_width), jnp.float32)
    sum_upb = jnp.zeros((w_up.shape[1],), jnp.float32)
    out_rows = []
    grad_rows = []
    for micro_id in range(micro_count):
        full_qkv, full_out, full_up, full_down, gain_rows, shift_rows, obias_rows = (
            lax.all_gather(w_qkv, "seq", axis=0, tiled=True),
            lax.all_gather(w_out, "seq", axis=1, tiled=True),
            lax.all_gather(w_up, "seq", axis=0, tiled=True),
            lax.all_gather(w_down, "seq", axis=1, tiled=True),
            lax.all_gather(ln_gains, "seq", axis=1, tiled=True),
            lax.all_gather(ln_shifts, "seq", axis=1, tiled=True),
            lax.all_gather(out_bias, "seq", axis=1, tiled=True),
        )
        gain_rows = gain_rows.astype(jnp.float32)
        shift_rows = shift_rows.astype(jnp.float32)
        obias_rows = obias_rows.astype(jnp.float32)
        bounds = jnp.cumsum(lengths[micro_id])[:-1]
        inputs = tokens[micro_id].astype(jnp.float32) + position_table(coords[:, micro_id], width)
        normed = layer_norm(inputs, gain_rows[0], shift_rows[0]).astype(jnp.bfloat16)
        projected = jnp.einsum("td,dcf->tcf", normed, full_qkv, preferred_element_type=jnp.float32)
        queries = (
            (projected[:, 0] + bias_qv[0])
            .astype(jnp.bfloat16)
            .reshape(tok_local, heads_local, HDIM)
        )
        key_rows = projected[:, 1].astype(jnp.bfloat16).reshape(tok_local, heads_local, HDIM)
        value_rows = (
            (projected[:, 2] + bias_qv[1])
            .astype(jnp.bfloat16)
            .reshape(tok_local, heads_local, HDIM)
        )
        keep_local = keep_mask[micro_id].astype(jnp.bfloat16)
        key_all, value_all, keep_all = (
            lax.all_gather(key_rows, "seq", axis=0, tiled=True),
            lax.all_gather(value_rows, "seq", axis=0, tiled=True),
            lax.all_gather(keep_local, "seq", axis=0, tiled=True),
        )

        def key_block(key_src, value_src, keep_src, offset):
            key_blk = lax.dynamic_slice_in_dim(key_src, offset, seg_unit, 0)
            value_blk = lax.dynamic_slice_in_dim(value_src, offset, seg_unit, 0)
            keep_blk = lax.dynamic_slice_in_dim(keep_src, offset, seg_unit, 0)
            key_pos = offset + jnp.arange(seg_unit, dtype=jnp.int32)
            scores = (
                jnp.einsum("thd,khd->htk", queries, key_blk, preferred_element_type=jnp.float32)
                * inv_root
            )
            weight = pair_weight(own_pos, key_pos, keep_blk, head_ids, bounds, seg_unit)
            return (key_blk, value_blk, scores, weight)

        def stats_step(running, offset):
            row_peak, row_total = running
            _, _, scores, weight = key_block(key_all, value_all, keep_all, offset)
            live = weight > 0
            new_peak = jnp.maximum(row_peak, jnp.max(jnp.where(live, scores, -1e30), axis=2))
            fresh = jnp.sum(
                jnp.where(live, weight * jnp.exp(scores - new_peak[:, :, None]), 0.0), axis=2
            )
            return ((new_peak, row_total * jnp.exp(row_peak - new_peak) + fresh), None)

        start_stats = (
            jnp.full((heads_local, tok_local), -1e30, jnp.float32),
            jnp.zeros((heads_local, tok_local), jnp.float32),
        )
        (row_peak, row_total), _ = lax.scan(stats_step, start_stats, block_starts)
        log_total = row_peak + jnp.log(row_total)

        def value_step(running, offset):
            _, value_blk, scores, weight = key_block(key_all, value_all, keep_all, offset)
            prob_low = (weight * jnp.exp(scores - log_total[:, :, None])).astype(jnp.bfloat16)
            return (
                running
                + jnp.einsum(
                    "htk,khd->thd", prob_low, value_blk, preferred_element_type=jnp.float32
                ),
                None,
            )

        attended, _ = lax.scan(
            value_step, jnp.zeros((tok_local, heads_local, HDIM), jnp.float32), block_starts
        )
        attended_low = attended.astype(jnp.bfloat16).reshape(tok_local, local_width)
        middle = (
            inputs
            + head_total(jnp.dot(attended_low, full_out, preferred_element_type=jnp.float32))
            + obias_rows[0]
        )
        normed_two = layer_norm(middle, gain_rows[1], shift_rows[1]).astype(jnp.bfloat16)
        hidden_pre = jnp.dot(normed_two, full_up, preferred_element_type=jnp.float32) + bias_up
        activated = jax.nn.gelu(hidden_pre, approximate=False).astype(jnp.bfloat16)
        result = (
            middle
            + head_total(jnp.dot(activated, full_down, preferred_element_type=jnp.float32))
            + obias_rows[1]
        )
        out_rows.append(result.astype(jnp.bfloat16))
        grad_out_low = cotangent[micro_id]
        grad_out_f32 = grad_out_low.astype(jnp.float32)
        sum_down = sum_down + jnp.einsum(
            "tf,td->fd", activated, grad_out_low, preferred_element_type=jnp.float32
        )
        grad_act = jnp.einsum(
            "td,fd->tf", grad_out_low, full_down, preferred_element_type=jnp.float32
        )
        _, gelu_back = jax.vjp(partial(jax.nn.gelu, approximate=False), hidden_pre)
        grad_pre_low = gelu_back(grad_act)[0].astype(jnp.bfloat16)
        sum_upb = sum_upb + jnp.sum(grad_pre_low.astype(jnp.float32), axis=0)
        sum_up = sum_up + jnp.einsum(
            "td,tf->df", normed_two, grad_pre_low, preferred_element_type=jnp.float32
        )
        grad_normed_two = head_total(
            jnp.einsum("tf,df->td", grad_pre_low, full_up, preferred_element_type=jnp.float32)
        )
        _, norm_back_two = jax.vjp(layer_norm, middle, gain_rows[1], shift_rows[1])
        grad_from_two, grad_gain_two, grad_shift_two = norm_back_two(grad_normed_two)
        grad_middle = grad_out_f32 + grad_from_two
        grad_branch_low = grad_middle.astype(jnp.bfloat16)
        sum_obias = sum_obias + jnp.stack(
            [jnp.sum(grad_branch_low.astype(jnp.float32), axis=0), jnp.sum(grad_out_f32, axis=0)]
        )
        sum_out = sum_out + jnp.einsum(
            "tf,td->fd", attended_low, grad_branch_low, preferred_element_type=jnp.float32
        )
        grad_attn_low = (
            jnp.einsum("td,fd->tf", grad_branch_low, full_out, preferred_element_type=jnp.float32)
            .astype(jnp.bfloat16)
            .reshape(tok_local, heads_local, HDIM)
        )
        row_delta = jnp.einsum("thd,thd->ht", grad_attn_low.astype(jnp.float32), attended)
        back_keys, back_values, back_keep = (
            lax.all_gather(key_rows, "seq", axis=0, tiled=True),
            lax.all_gather(value_rows, "seq", axis=0, tiled=True),
            lax.all_gather(keep_local, "seq", axis=0, tiled=True),
        )

        def key_side_step(running, offset):
            key_blk, value_blk, scores, weight = key_block(
                back_keys, back_values, back_keep, offset
            )
            prob_f32 = weight * jnp.exp(scores - log_total[:, :, None])
            grad_prob = jnp.einsum(
                "thd,khd->htk", grad_attn_low, value_blk, preferred_element_type=jnp.float32
            )
            grad_scores = (prob_f32 * (grad_prob - row_delta[:, :, None])).astype(jnp.bfloat16)
            running = running + jnp.einsum(
                "htk,khd->thd", grad_scores, key_blk, preferred_element_type=jnp.float32
            )
            prob_low = prob_f32.astype(jnp.bfloat16)
            key_term = (
                jnp.einsum("htk,thd->khd", grad_scores, queries, preferred_element_type=jnp.float32)
                * inv_root
            )
            value_term = jnp.einsum(
                "htk,thd->khd", prob_low, grad_attn_low, preferred_element_type=jnp.float32
            )
            return (
                running,
                jnp.concatenate(
                    [
                        key_term.reshape(seg_unit, local_width),
                        value_term.reshape(seg_unit, local_width),
                    ],
                    axis=1,
                ),
            )

        query_sum, terms = lax.scan(
            key_side_step, jnp.zeros((tok_local, heads_local, HDIM), jnp.float32), block_starts
        )
        owned = lax.psum_scatter(
            terms.reshape(row_len, 2 * local_width), "seq", scatter_dimension=0, tiled=True
        )
        grad_queries = query_sum * inv_root
        grad_keys = owned[:, :local_width].reshape(tok_local, heads_local, HDIM)
        grad_values = owned[:, local_width:].reshape(tok_local, heads_local, HDIM)
        grad_q_low = grad_queries.astype(jnp.bfloat16).reshape(tok_local, local_width)
        grad_k_low = grad_keys.astype(jnp.bfloat16).reshape(tok_local, local_width)
        grad_v_low = grad_values.astype(jnp.bfloat16).reshape(tok_local, local_width)
        sum_qvb = sum_qvb + jnp.stack(
            [
                jnp.sum(grad_q_low.astype(jnp.float32), axis=0),
                jnp.sum(grad_v_low.astype(jnp.float32), axis=0),
            ]
        )
        grad_proj = jnp.stack([grad_q_low, grad_k_low, grad_v_low], axis=1)
        sum_qkv = sum_qkv + jnp.einsum(
            "td,tcf->dcf", normed, grad_proj, preferred_element_type=jnp.float32
        )
        grad_normed = head_total(
            jnp.einsum("tcf,dcf->td", grad_proj, full_qkv, preferred_element_type=jnp.float32)
        )
        _, norm_back_one = jax.vjp(layer_norm, inputs, gain_rows[0], shift_rows[0])
        grad_from_one, grad_gain_one, grad_shift_one = norm_back_one(grad_normed)
        grad_rows.append((grad_middle + grad_from_one).astype(jnp.bfloat16))
        sum_gain = sum_gain + jnp.stack([grad_gain_one, grad_gain_two])
        sum_shift = sum_shift + jnp.stack([grad_shift_one, grad_shift_two])
    grad_qkv, grad_out, grad_up, grad_down, grad_gain, grad_shift, grad_obias = (
        lax.psum_scatter(sum_qkv, "seq", scatter_dimension=0, tiled=True),
        lax.psum_scatter(sum_out, "seq", scatter_dimension=1, tiled=True),
        lax.psum_scatter(sum_up, "seq", scatter_dimension=0, tiled=True),
        lax.psum_scatter(sum_down, "seq", scatter_dimension=1, tiled=True),
        lax.psum_scatter(sum_gain, "seq", scatter_dimension=1, tiled=True),
        lax.psum_scatter(sum_shift, "seq", scatter_dimension=1, tiled=True),
        lax.psum_scatter(sum_obias, "seq", scatter_dimension=1, tiled=True),
    )
    grad_qvb, grad_upb = lax.psum((sum_qvb, sum_upb), "seq")
    return (
        jnp.stack(out_rows),
        jnp.stack(grad_rows),
        grad_gain,
        grad_shift,
        grad_obias,
        grad_qkv,
        grad_qvb,
        grad_out,
        grad_up,
        grad_upb,
        grad_down,
    )


NEG = 1792.0
ROOT = 1.0 / math.sqrt(HDIM)
BF = jnp.bfloat16
F32 = jnp.float32
MESH = pl.DeviceIdType.MESH
LEVELS = [math.sqrt(HDIM) * math.log((b + 1) / b) for b in range(1, BRANCHES)]
LEVEL_HIGH = [float(np.asarray(v, ml_dtypes.bfloat16)) for v in LEVELS]
LEVEL_LOW = [v - w for v, w in zip(LEVELS, LEVEL_HIGH)]


def nn(a, b):
    return lax.dot_general(a, b, (((1,), (0,)), ((), ())), preferred_element_type=F32)


def nt(a, b):
    return lax.dot_general(a, b, (((1,), (1,)), ((), ())), preferred_element_type=F32)


def tn(a, b):
    return lax.dot_general(a, b, (((0,), (0,)), ((), ())), preferred_element_type=F32)


def tt(a, b):
    return lax.dot_general(a, b, (((0,), (1,)), ((), ())), preferred_element_type=F32)


def four(index, values):
    return jnp.where(
        index == 0,
        values[0],
        jnp.where(index == 1, values[1], jnp.where(index == 2, values[2], values[3])),
    )


def pair_features(pos, slide, keep, head, for_keys):
    shape = (16, pos.shape[1])
    row = lax.broadcasted_iota(jnp.int32, shape, 0)
    pos = jnp.broadcast_to(pos, shape)
    slide = jnp.broadcast_to(slide, shape)
    level = jnp.where(row >= 8, row - 8, row - 4)
    on = jnp.bitwise_and(pos - head, four(level, [1, 3, 7, 15])) == 0
    on = on & (row < 12)
    if for_keys:
        keep = jnp.broadcast_to(keep, shape)
        size = jnp.where(row < 8, four(level, LEVEL_HIGH), four(level, LEVEL_LOW))
        other = jnp.where(slide != row, -NEG, 0.0)
        padding = jnp.where(keep > 0.0, 0.0, -NEG)
    else:
        size = jnp.ones(shape, F32)
        other = jnp.where(slide == row, 1.0, 0.0)
        padding = jnp.ones(shape, F32)
    value = jnp.where(row < 3, other, jnp.where(row == 3, padding, jnp.where(on, size, 0.0)))
    return value.astype(BF)


def layer_kernel(*refs, names):
    r_ = dict(zip(names, refs))

    class N:
        pass

    g = N()
    for k, v in r_.items():
        setattr(g, k, v)
    s = lax.axis_index("seq")
    h = lax.axis_index("head")
    z, y = lax.div(s, 2), lax.rem(s, 2)
    x, c = lax.div(h, 2), lax.rem(h, 2)
    a, j = lax.div(s, 4), lax.rem(s, 4)
    sib = (s, h + 1 - 2 * c)
    xp = (s, lax.rem(h + 2, 4))
    yp = (s + 1 - 2 * y, h)
    top = lax.div(z, 2)
    zs = [z + 1 - 2 * lax.rem(z, 2), 2 - top, 3 - 3 * top]
    zm = [(2 * q + y, h) for q in zs]
    zy = [(2 * q + 1 - y, h) for q in zs]
    qs = zs + [z]
    inner = (z == 1) | (z == 2)
    outer = jnp.logical_not(inner)
    part = [(4 * c + i, 2 * x + a) for i in range(4)]
    own = [(a == c) & (j == i) for i in range(4)]
    is_own = jnp.where(a == c, 1, 0)
    head = 8 * x + s
    R = 3
    T = 128

    def rdma(src, dst, ss, rs, dev):
        return pltpu.make_async_remote_copy(
            src_ref=src, dst_ref=dst, send_sem=ss, recv_sem=rs, device_id=dev, device_id_type=MESH
        )

    def not_own(i):
        return jnp.logical_not(own[i])

    def lanes(r, n=128):
        return pl.ds(pl.multiple_of(n * r, n), n)

    def rows(r, n=128):
        return pl.ds(pl.multiple_of(n * r, n), n)

    def half(r, who):
        return pl.ds(pl.multiple_of(T * r + 64 * who, 64), 64)

    bar = pltpu.get_barrier_semaphore()
    for dev in [sib, xp, yp] + zm + zy:
        pl.semaphore_signal(bar, inc=1, device_id=dev, device_id_type=MESH)
    for i in range(4):

        @pl.when(not_own(i))
        def _():
            pl.semaphore_signal(bar, inc=1, device_id=part[i], device_id_type=MESH)

    W = [g.wq, None, g.wu, g.wd]

    def four_of(name):
        return [r_[f"{name}{q}"] for q in range(4)]

    AGS, AGR, PSS, PSR = four_of("ag_s"), four_of("ag_r"), four_of("ps_s"), four_of("ps_r")
    L1SS, L1RS, L2SS, L2RS = four_of("l1_s"), four_of("l1_r"), four_of("l2_s"), four_of("l2_r")

    def ag_y(p):
        w = W[p]
        rdma(w.at[s], w.at[s], AGS[p].at[0], AGR[p].at[s], yp).start()

    def ag_z(p):
        w = W[p]
        for t in range(2):
            rdma(w.at[s], w.at[s], AGS[p].at[1 + t], AGR[p].at[s], zm[t]).start()

        @pl.when(inner)
        def _():
            rdma(w.at[s], w.at[s], AGS[p].at[3], AGR[p].at[s], zm[2]).start()

    def ag_forward(p, t):
        w = W[p]
        k = zm[t][0]
        rdma(w.at[k], w.at[k], AGS[p].at[4 + t], AGR[p].at[k], zm[t]).wait_recv()
        if t == 2:

            @pl.when(inner)
            def _():
                rdma(w.at[k], w.at[k], AGS[p].at[7], AGR[p].at[k], zm[0]).start()

        rdma(w.at[k], w.at[k], AGS[p].at[4 + t], AGR[p].at[k], yp).start()

    def ag_wait(p):
        w = W[p]
        for q in qs:
            k = 2 * q + 1 - y
            rdma(w.at[k], w.at[k], AGS[p].at[0], AGR[p].at[k], yp).wait_recv()

    def ag_drain(p):
        w = W[p]
        for t in (0, 1, 2, 4, 5, 6):
            rdma(w.at[s], w.at[s], AGS[p].at[t], AGR[p].at[s], yp).wait_send()

        @pl.when(inner)
        def _():
            for t in (3, 7):
                rdma(w.at[s], w.at[s], AGS[p].at[t], AGR[p].at[s], yp).wait_send()

    g.wq[s] = jnp.concatenate(
        [g.in_w3[0], g.in_w3[1], g.in_w3[2], jnp.transpose(g.in_wo[...])], axis=1
    )
    g.tmp[...] = jnp.zeros_like(g.tmp)
    g.tmp[0:2, 0:96] = g.in_lng[...].astype(F32)
    g.tmp[2:4, 0:96] = g.in_lns[...].astype(F32)
    g.tmp[4:6, 0:96] = g.in_ob[...].astype(F32)
    g.tmp[6:9, :] = g.in_keep[...].astype(F32)
    g.sml[s] = g.tmp[...].astype(BF)
    g.wu[s] = g.in_wu[...]
    g.wd[s] = g.in_wd[...]
    pl.semaphore_wait(bar, 13 - is_own)
    others = [yp] + zm + zy
    for t, dev in enumerate(others):
        rdma(g.sml.at[s], g.sml.at[s], g.sml_s.at[t], g.sml_r.at[s], dev).start()
    ag_y(0)
    ag_z(0)
    ag_y(2)
    ag_z(2)

    lane = lax.broadcasted_iota(jnp.int32, (1, 768), 1)
    freq = jnp.exp(
        -math.log(10000.0) * lax.rem(lane, 192).astype(F32) / 192.0
    )
    for r in range(R):
        col = jnp.transpose(
            jnp.concatenate([g.in_crd[r].astype(F32), jnp.zeros((6, 128), F32)], axis=0)
        )
        pieces = []
        for t in range(6):
            f = freq[:, 128 * t : 128 * t + 128]
            ang = col[:, (0 if t < 3 else 1) : (1 if t < 3 else 2)] * f
            if t % 3 == 0:
                pieces.append(jnp.sin(ang))
            elif t % 3 == 2:
                pieces.append(jnp.cos(ang))
            else:
                low_half = lax.broadcasted_iota(jnp.int32, (T, 128), 1) < 64
                pieces.append(jnp.where(low_half, jnp.sin(ang), jnp.cos(ang)))
        v = g.in_tok[rows(r), :].astype(F32) + jnp.concatenate(pieces, axis=1)
        g.inp[rows(r), :] = v
        v = v - jnp.mean(v, axis=1, keepdims=True)
        rstd = lax.rsqrt(jnp.mean(v * v, axis=1, keepdims=True) + EPSILON)
        g.n1[rows(r), :] = v * rstd
        g.rstd1[rows(r), :] = rstd
        g.cotT[:, 128 * r : 128 * r + 128] = jnp.transpose(g.in_cot[rows(r), :])
    g.sums[...] = jnp.zeros_like(g.sums)

    for t, dev in enumerate(others):
        k = dev[0]
        rdma(g.sml.at[k], g.sml.at[k], g.sml_s.at[t], g.sml_r.at[k], dev).wait_recv()
    par = jnp.concatenate([g.sml[k].astype(F32)[:, 0:96] for k in range(8)], axis=1)
    g.par[...] = par
    g1, s1, ob0, ob1 = par[1:2], par[3:4], par[4:5], par[5:6]
    g0 = par[0:1]
    qvb = g.in_qvb[...].astype(F32)
    qkv_bias = jnp.concatenate([qvb[0:1], jnp.zeros((1, 192), F32), qvb[1:2]], axis=1)
    for r in range(R):
        nr = (g.n1[rows(r), :] * g0 + par[2:3]).astype(BF)
        g.nrm[rows(r), :] = nr
        g.nrmT[:, 128 * r : 128 * r + 128] = jnp.transpose(nr)
    for t in range(3):
        ag_forward(0, t)
    ag_wait(0)

    def send_part(i, r, src, dst, ss, rs):
        @pl.when(not_own(i))
        def _():
            rdma(src.at[i, r], dst.at[j, r], ss.at[i, r], rs.at[j, r], part[i]).start()

        @pl.when(own[i])
        def _():
            dst[i, r] = src[i, r]

    def wait_part(i, r, dst, ss, rs):
        @pl.when(not_own(i))
        def _():
            rdma(dst.at[i, r], dst.at[i, r], ss.at[i, r], rs.at[i, r], part[i]).wait_recv()

    def drain_part(i, r, src, ss, rs):
        @pl.when(not_own(i))
        def _():
            rdma(src.at[i, r], src.at[i, r], ss.at[i, r], rs.at[i, r], part[i]).wait_send()

    for r in range(R):
        proj = nn(g.nrm[rows(r), :], g.wq[:, :, 0:576].reshape(768, 576)) + qkv_bias
        projT = jnp.transpose(proj).astype(BF)
        for i in range(4):
            for t in range(3):
                g.snA[i, r, 48 * t : 48 * t + 48, :] = projT[192 * t + 48 * i : 192 * t + 48 * i + 48]
            send_part(i, r, g.snA, g.rcA, g.qa_s, g.qa_r)

    ag_y(3)
    for t in range(3):
        ag_forward(2, t)
    ag_z(3)
    g.wo[...] = g.wq[:, :, 576:768].reshape(768, 192)

    def slide_of_row(r, pos):
        b0 = g.in_len[r, 0]
        b1 = b0 + g.in_len[r, 1]
        return jnp.where(pos >= b0, 1, 0) + jnp.where(pos >= b1, 1, 0)

    ones_rows = jnp.where(lax.broadcasted_iota(jnp.int32, (16, 1024), 0) == 0, 1.0, 0.0).astype(BF)

    def attn_fwd(r):
        for i in range(4):
            wait_part(i, r, g.rcA, g.qa_s, g.qa_r)
            rdma(
                g.rcA.at[i, r, pl.ds(48, 96)], g.sbA.at[i, r], g.sa_s.at[i, r], g.sa_r.at[i, r], sib
            ).start()
        iota = lax.broadcasted_iota(jnp.int32, (1, 512), 1)
        pos_own = 512 * c + iota
        pos_sib = 512 * (1 - c) + iota
        keep_own = jnp.concatenate(
            [g.sml[4 * c + i].astype(F32)[6 + r : 7 + r] for i in range(4)], axis=1
        )
        keep_sib = jnp.concatenate(
            [g.sml[4 * (1 - c) + i].astype(F32)[6 + r : 7 + r] for i in range(4)], axis=1
        )
        pos = jnp.concatenate([pos_own, pos_sib], axis=1)
        kf = pair_features(
            pos, slide_of_row(r, pos), jnp.concatenate([keep_own, keep_sib], axis=1), head, True
        )
        qf = pair_features(pos_own, slide_of_row(r, pos_own), None, head, False)
        g.QT[r, 0:48, :] = jnp.concatenate([g.rcA[i, r, 0:48, :] for i in range(4)], axis=1)
        g.QT[r, 48:64, :] = qf
        g.KT[r, 48:64, :] = kf
        g.VT[r, 48:64, :] = ones_rows
        for i in range(4):
            g.KT[r, 0:48, 128 * i : 128 * i + 128] = g.rcA[i, r, 48:96, :]
            g.VT[r, 0:48, 128 * i : 128 * i + 128] = g.rcA[i, r, 96:144, :]
        for i in range(4):
            rdma(g.sbA.at[i, r], g.sbA.at[i, r], g.sa_s.at[i, r], g.sa_r.at[i, r], sib).wait_recv()
            g.KT[r, 0:48, 512 + 128 * i : 640 + 128 * i] = g.sbA[i, r, 0:48, :]
            g.VT[r, 0:48, 512 + 128 * i : 640 + 128 * i] = g.sbA[i, r, 48:96, :]
        eye = lax.broadcasted_iota(jnp.int32, (256, 256), 0) == lax.broadcasted_iota(
            jnp.int32, (256, 256), 1
        )
        for qc in range(2):
            q0 = 256 * qc
            sc = tn(g.KT[r], g.QT[r, :, q0 : q0 + 256])
            lift = jnp.where(eye, NEG * (1.0 - keep_own[:, q0 : q0 + 256]), 0.0)
            blocks = [sc[256 * t : 256 * t + 256] for t in range(4)]
            blocks[qc] = blocks[qc] + lift
            sc = jnp.concatenate(blocks, axis=0)
            peak = jnp.max(sc, axis=0, keepdims=True)
            pb = jnp.exp((sc - peak) * ROOT).astype(BF)
            g.P[r, :, q0 : q0 + 256] = pb
            o = nn(g.VT[r], pb)
            inv = 1.0 / o[48:49]
            o = o[0:48] * inv
            g.O[r, :, q0 : q0 + 256] = o
            g.inv[r, :, q0 : q0 + 256] = jnp.broadcast_to(inv, (8, 256))
            for u in range(2):
                i = 2 * qc + u
                g.snO[i, r] = o[:, 128 * u : 128 * u + 128].astype(BF)
                send_part(i, r, g.snO, g.rcO, g.o_s, g.o_r)

    attn_fwd(0)
    attn_fwd(1)
    attn_fwd(2)
    ag_forward(3, 0)

    def ps_start(kind, r, part_sum):
        g.ps[kind, r] = part_sum.astype(BF)
        rdma(
            g.ps.at[kind, r, pl.ds(pl.multiple_of(64 * (1 - c), 64), 64)],
            g.psA.at[kind, r],
            PSS[kind].at[r, 0],
            PSR[kind].at[r, 0],
            sib,
        ).start()

    def ps_mid(kind, r):
        dst = g.psA.at[kind, r]
        rdma(dst, dst, PSS[kind].at[r, 0], PSR[kind].at[r, 0], sib).wait_recv()
        mine = g.ps[kind, r, pl.ds(pl.multiple_of(64 * c, 64), 64), :].astype(F32)
        g.psH[kind, r] = (mine + g.psA[kind, r].astype(F32)).astype(BF)
        rdma(
            g.psH.at[kind, r], g.psB.at[kind, r], PSS[kind].at[r, 1], PSR[kind].at[r, 1], xp
        ).start()

    def ps_end(kind, r):
        dst = g.psB.at[kind, r]
        rdma(dst, dst, PSS[kind].at[r, 1], PSR[kind].at[r, 1], xp).wait_recv()
        return g.psH[kind, r].astype(F32) + g.psB[kind, r].astype(F32)

    def share_start(ref, r, ss, rs):
        rdma(ref.at[half(r, c)], ref.at[half(r, c)], ss.at[r], rs.at[r], sib).start()

    def share_wait(ref, r, ss, rs):
        dst = ref.at[half(r, 1 - c)]
        rdma(dst, dst, ss.at[r], rs.at[r], sib).wait_recv()

    for r in range(R):
        for i in range(4):
            wait_part(i, r, g.rcO, g.o_s, g.o_r)
            g.attT[48 * i : 48 * i + 48, 128 * r : 128 * r + 128] = g.rcO[i, r]
        att = jnp.transpose(g.attT[:, 128 * r : 128 * r + 128])
        ps_start(0, r, nt(att, g.wo[...]))
        if r > 0:
            ps_mid(0, r - 1)
    ag_forward(3, 1)
    ps_mid(0, R - 1)
    ag_forward(3, 2)
    ag_wait(2)

    def second_norm(r):
        v = g.inp[half(r, c), :] + ps_end(0, r) + ob0
        g.mid[r] = v
        v = v - jnp.mean(v, axis=1, keepdims=True)
        rstd = lax.rsqrt(jnp.mean(v * v, axis=1, keepdims=True) + EPSILON)
        v = v * rstd
        g.n2[r] = v
        g.rstd2[r] = rstd
        g.ntk[half(r, c), :] = (v * g1 + s1).astype(BF)
        share_start(g.ntk, r, g.nt_s, g.nt_r)

    up_bias = g.in_upb[...].astype(F32)

    def feed_up(r):
        share_wait(g.ntk, r, g.nt_s, g.nt_r)
        pre = nn(g.ntk[rows(r), :], g.wu[...].reshape(768, 768)) + up_bias
        cdf = 0.5 * (1.0 + lax.erf(pre * (1.0 / math.sqrt(2.0))))
        pdf = jnp.exp(-0.5 * pre * pre) * (1.0 / math.sqrt(2.0 * math.pi))
        g.act[rows(r), :] = (pre * cdf).astype(BF)
        g.gd[rows(r), :] = cdf + pre * pdf

    def feed_back(r):
        gact = nn(g.in_cot[rows(r), :], g.wd[...].reshape(768, 768))
        g.gp[rows(r), :] = (gact * g.gd[rows(r), :]).astype(BF)
        ps_start(1, r, nt(g.gp[rows(r), :], g.wu[...].reshape(768, 768)))

    def block(p, k):
        b = pl.ds(pl.multiple_of(96 * k, 96), 96)
        if p == 0:
            return nt(g.nrmT[b, :], g.gpT[...])
        if p == 1:
            return nt(g.gbT[b, :], g.attT[...])
        if p == 2:
            return nn(g.ntT[b, :], g.gp[...])
        return nn(g.cotT[b, :], g.act[...])

    L1S = [g.l1s0, g.l1s1, g.l1s2, g.l1s3]
    L1R = [g.l1r0, g.l1r1, g.l1r2, g.l1r3]
    L2S = [g.l2s0, g.l2s1, g.l2s2, g.l2s3]
    L2R = [g.l2r0, g.l2r1, g.l2r2, g.l2r3]
    g.acc = [g.acc0, g.acc1, g.out_gup, g.out_gdown]

    def rs_first(p, start=0, stop=4):
        def step(t, _):
            q = four(t, qs)
            L1S[p][q] = block(p, 2 * q + 1 - y).astype(BF)
            rdma(L1S[p].at[q], L1R[p].at[q], L1SS[p].at[q], L1RS[p].at[q], yp).start()
            return 0

        lax.fori_loop(start, stop, step, 0)

    def rs_second(p, t):
        q = zs[t]
        dst = L1R[p].at[q]
        rdma(dst, dst, L1SS[p].at[q], L1RS[p].at[q], yp).wait_recv()
        mine = block(p, 2 * q + y) + L1R[p][q].astype(F32)

        def send():
            rdma(L2S[p].at[q], L2R[p].at[z], L2SS[p].at[q], L2RS[p].at[z], zm[t]).start()

        if t < 2:
            L2S[p][q] = mine.astype(BF)
            send()
        else:
            via = L2R[p].at[z]

            @pl.when(outer)
            def _():
                L2S[p][q] = mine.astype(BF)
                rdma(L2S[p].at[q], L2R[p].at[zs[0]], L2SS[p].at[q], L2RS[p].at[zs[0]], zm[0]).start()

            @pl.when(inner)
            def _():
                rdma(via, via, L2SS[p].at[q], L2RS[p].at[z], zm[0]).wait_recv()
                L2S[p][q] = (mine + via[...].astype(F32)).astype(BF)
                send()

    def rs_own(p):
        dst = L1R[p].at[z]
        rdma(dst, dst, L1SS[p].at[z], L1RS[p].at[z], yp).wait_recv()
        g.acc[p][...] = block(p, s) + L1R[p][z].astype(F32)

    def rs_third(p):
        acc = g.acc[p]
        for t, q in enumerate(zs):
            dst = L2R[p].at[q]

            def add(dst=dst, q=q):
                rdma(dst, dst, L2SS[p].at[q], L2RS[p].at[q], yp).wait_recv()
                acc[...] += dst[...].astype(F32)

            if t < 2:
                add()
            else:
                pl.when(inner)(add)
        return acc[...]

    def rs_drain(p):
        for q in qs:
            rdma(L1S[p].at[q], L1R[p].at[q], L1SS[p].at[q], L1RS[p].at[q], yp).wait_send()
        for q in zs:
            rdma(L2S[p].at[q], L2R[p].at[q], L2SS[p].at[q], L2RS[p].at[q], yp).wait_send()

    second_norm(0)
    second_norm(1)
    feed_up(0)
    second_norm(2)
    feed_up(1)
    feed_up(2)
    rs_first(3)
    ag_wait(3)
    feed_back(0)
    feed_back(1)
    ps_mid(1, 0)
    feed_back(2)
    ps_mid(1, 1)
    g.ntT[...] = jnp.transpose(g.ntk[...])
    ps_mid(1, 2)

    def add_sum(row, value):
        g.sums[row : row + 1, :] += jnp.sum(value, axis=0, keepdims=True)

    def norm_back(grad, n, rstd, gain):
        e = grad * gain
        return rstd * (
            e - jnp.mean(e, axis=1, keepdims=True) - n * jnp.mean(e * n, axis=1, keepdims=True)
        )

    def second_back(r):
        gn = ps_end(1, r)
        n = g.n2[r]
        cot = g.in_cot[half(r, c), :].astype(F32)
        gm = cot + norm_back(gn, n, g.rstd2[r], g1)
        g.gm[r] = gm
        gb = gm.astype(BF)
        g.gb[half(r, c), :] = gb
        share_start(g.gb, r, g.gb_s, g.gb_r)
        add_sum(1, gn * n)
        add_sum(3, gn)
        add_sum(4, gb.astype(F32))
        add_sum(5, cot)

    def grad_attended(r):
        share_wait(g.gb, r, g.gb_s, g.gb_r)
        ga = jnp.transpose(nn(g.gb[rows(r), :], g.wo[...])).astype(BF)
        for i in range(4):
            g.snD[i, r] = ga[48 * i : 48 * i + 48]
            send_part(i, r, g.snD, g.rcD, g.d_s, g.d_r)

    second_back(0)
    rs_second(3, 0)
    second_back(1)
    grad_attended(0)
    second_back(2)
    grad_attended(1)
    grad_attended(2)
    rs_second(3, 1)
    rs_first(2, 0, 2)
    for r in range(R):
        ps_start(2, r, nt(g.act[rows(r), :], g.wd[...].reshape(768, 768)))
    g.gbT[...] = jnp.transpose(g.gb[...])

    def attn_bwd(r):
        for i in range(4):
            wait_part(i, r, g.rcD, g.d_s, g.d_r)
        dk = None
        dv = None
        for qc in range(2):
            q0 = 256 * qc
            do = jnp.concatenate([g.rcD[2 * qc, r], g.rcD[2 * qc + 1, r]], axis=1)
            delta = jnp.sum(do.astype(F32) * g.O[r, :, q0 : q0 + 256], axis=0, keepdims=True)
            dp = tn(g.VT[r, 0:48, :], do)
            pn = g.P[r, :, q0 : q0 + 256].astype(F32) * g.inv[r, 0:1, q0 : q0 + 256]
            ds = (pn * (dp - delta)).astype(BF)
            pn = pn.astype(BF)
            dq = nn(g.KT[r, 0:48, :], ds) * ROOT
            for u in range(2):
                g.snG[2 * qc + u, r, 0:48, :] = dq[:, 128 * u : 128 * u + 128].astype(BF)
            dk_part = nt(g.QT[r, 0:48, q0 : q0 + 256], ds)
            dv_part = nt(do, pn)
            dk = dk_part if dk is None else dk + dk_part
            dv = dv_part if dv is None else dv + dv_part
        dk = dk * ROOT
        g.snX[r, 0:48, :] = dk[:, 512:1024]
        g.snX[r, 48:96, :] = dv[:, 512:1024]
        rdma(g.snX.at[r], g.rcX.at[r], g.x_s.at[r], g.x_r.at[r], sib).start()
        g.kvX[r, 0:48, :] = dk[:, 0:512]
        g.kvX[r, 48:96, :] = dv[:, 0:512]

    def attn_bwd_end(r):
        rdma(g.rcX.at[r], g.rcX.at[r], g.x_s.at[r], g.x_r.at[r], sib).wait_recv()
        kv = (g.kvX[r] + g.rcX[r]).astype(BF)
        for i in range(4):
            g.snG[i, r, 48:144, :] = kv[:, 128 * i : 128 * i + 128]
            send_part(i, r, g.snG, g.rcG, g.g_s, g.g_r)

    attn_bwd(0)
    ps_mid(2, 0)
    attn_bwd(1)
    attn_bwd_end(0)
    rs_first(2, 2, 3)
    ps_mid(2, 1)
    attn_bwd(2)
    attn_bwd_end(1)
    rs_first(2, 3, 4)
    ps_mid(2, 2)
    attn_bwd_end(2)
    rs_second(3, 2)
    rs_first(1)
    rs_second(2, 0)
    rs_second(2, 1)
    rs_own(3)

    for r in range(R):
        g.out_tok[half(r, c), :] = (g.mid[r] + ps_end(2, r) + ob1).astype(BF)
        share_start(g.out_tok, r, g.ot_s, g.ot_r)
    ones = jnp.ones((8, 384), BF)
    g.sums[6:7, :] = nn(ones, g.gp[...])[0:1]

    def project_back(r):
        for i in range(4):
            wait_part(i, r, g.rcG, g.g_s, g.g_r)
            for t in range(3):
                g.gpT[192 * t + 48 * i : 192 * t + 48 * i + 48, 128 * r : 128 * r + 128] = g.rcG[
                    i, r, 48 * t : 48 * t + 48, :
                ]
        ps_start(3, r, tt(g.gpT[:, 128 * r : 128 * r + 128], g.wq[:, :, 0:576].reshape(768, 576)))

    project_back(0)
    rs_second(2, 2)
    project_back(1)
    ps_mid(3, 0)
    rs_own(2)
    project_back(2)
    ps_mid(3, 1)
    rs_first(0)
    ps_mid(3, 2)
    for t in range(3):
        rs_second(1, t)
    rs_own(1)
    g.sums[7:8, 0:576] = nt(ones, g.gpT[...])[0:1]

    def first_back(r):
        gn = ps_end(3, r)
        n = g.n1[half(r, c), :]
        gt = g.gm[r] + norm_back(gn, n, g.rstd1[half(r, c), :], g0)
        g.out_gtok[half(r, c), :] = gt.astype(BF)
        share_start(g.out_gtok, r, g.gt_s, g.gt_r)
        add_sum(0, gn * n)
        add_sum(2, gn)

    for r in range(R):
        first_back(r)
    rdma(g.sums, g.sumA, g.sm_s.at[0], g.sm_r.at[0], sib).start()
    rdma(g.sumA, g.sumA, g.sm_s.at[0], g.sm_r.at[0], sib).wait_recv()
    both = lax.broadcasted_iota(jnp.int32, (8, 768), 0) < 6
    g.sumB[...] = g.sums[...] + jnp.where(both, g.sumA[...], 0.0)
    rdma(g.sumB, g.sumC, g.sm_s.at[1], g.sm_r.at[1], yp).start()
    for t in range(3):
        rs_second(0, t)
    rdma(g.sumC, g.sumC, g.sm_s.at[1], g.sm_r.at[1], yp).wait_recv()
    g.sumD[z] = g.sumB[...] + g.sumC[...]
    for t in range(3):
        rdma(g.sumD.at[z], g.sumD.at[z], g.sm_s.at[2 + t], g.sm_r.at[2 + z], zm[t]).start()
    rs_own(0)
    rs_third(3)
    rs_third(2)
    g.out_gout[...] = jnp.transpose(rs_third(1))
    total = rs_third(0)
    for t in range(3):
        g.out_gqkv[t] = total[:, 192 * t : 192 * t + 192]
    for t in range(3):
        q = zs[t]
        rdma(g.sumD.at[q], g.sumD.at[q], g.sm_s.at[2 + t], g.sm_r.at[2 + q], zm[t]).wait_recv()
    total = g.sumD[0] + g.sumD[1] + g.sumD[2] + g.sumD[3]
    for k in range(8):
        g.cut[k] = total[:, 96 * k : 96 * k + 96]
    mine = g.cut[s]
    g.out_gain[...] = mine[0:2]
    g.out_shift[...] = mine[2:4]
    g.out_obias[...] = mine[4:6]
    g.out_upb[...] = total[6:7]
    g.out_qvb[0:1, :] = total[7:8, 0:192]
    g.out_qvb[1:2, :] = total[7:8, 384:576]

    for r in range(R):
        share_wait(g.out_tok, r, g.ot_s, g.ot_r)
        share_wait(g.out_gtok, r, g.gt_s, g.gt_r)
    for t, dev in enumerate(others):
        rdma(g.sml.at[s], g.sml.at[s], g.sml_s.at[t], g.sml_r.at[s], dev).wait_send()
    for p in (0, 2, 3):
        ag_drain(p)
    for p in range(4):
        rs_drain(p)
    for r in range(R):
        for i in range(4):
            drain_part(i, r, g.snA, g.qa_s, g.qa_r)
            drain_part(i, r, g.snO, g.o_s, g.o_r)
            drain_part(i, r, g.snD, g.d_s, g.d_r)
            drain_part(i, r, g.snG, g.g_s, g.g_r)
            rdma(g.sbA.at[i, r], g.sbA.at[i, r], g.sa_s.at[i, r], g.sa_r.at[i, r], sib).wait_send()
        rdma(g.snX.at[r], g.rcX.at[r], g.x_s.at[r], g.x_r.at[r], sib).wait_send()
        for kind in range(4):
            for t in range(2):
                rdma(
                    g.psH.at[kind, r], g.psB.at[kind, r], PSS[kind].at[r, t], PSR[kind].at[r, t], xp
                ).wait_send()
        for ref, ss, rs in (
            (g.ntk, g.nt_s, g.nt_r),
            (g.gb, g.gb_s, g.gb_r),
            (g.out_tok, g.ot_s, g.ot_r),
            (g.out_gtok, g.gt_s, g.gt_r),
        ):
            rdma(ref.at[half(r, c)], ref.at[half(r, c)], ss.at[r], rs.at[r], sib).wait_send()
    rdma(g.sums, g.sumA, g.sm_s.at[0], g.sm_r.at[0], sib).wait_send()
    rdma(g.sumB, g.sumC, g.sm_s.at[1], g.sm_r.at[1], yp).wait_send()
    for t in range(3):
        rdma(g.sumD.at[z], g.sumD.at[z], g.sm_s.at[2 + t], g.sm_r.at[2 + z], zm[t]).wait_send()


def fast_device(
    tokens, cotangent, lengths, coords, keep_mask, ln_gains, ln_shifts, out_bias,
    w_qkv, qv_bias, w_out, w_up, up_bias, w_down,
):
    inputs = [
        ("in_tok", tokens.reshape(384, 768)),
        ("in_cot", cotangent.reshape(384, 768)),
        ("in_len", lengths),
        ("in_crd", jnp.transpose(coords, (1, 0, 2))),
        ("in_keep", keep_mask),
        ("in_lng", ln_gains),
        ("in_lns", ln_shifts),
        ("in_ob", out_bias),
        ("in_w3", jnp.transpose(w_qkv, (1, 0, 2))),
        ("in_qvb", qv_bias),
        ("in_wo", w_out),
        ("in_wu", w_up),
        ("in_upb", up_bias.reshape(1, 768)),
        ("in_wd", jnp.transpose(w_down)),
    ]
    outputs = [
        ("out_tok", (384, 768), BF),
        ("out_gtok", (384, 768), BF),
        ("out_gain", (2, 96), F32),
        ("out_shift", (2, 96), F32),
        ("out_obias", (2, 96), F32),
        ("out_gqkv", (3, 96, 192), F32),
        ("out_qvb", (2, 192), F32),
        ("out_gout", (192, 96), F32),
        ("out_gup", (96, 768), F32),
        ("out_upb", (1, 768), F32),
        ("out_gdown", (96, 768), F32),
    ]
    vm = [
        ("wq", (8, 96, 768), BF),
        ("wo", (768, 192), BF),
        ("sml", (8, 16, 128), BF),
        ("tmp", (16, 128), F32),
        ("nrm", (384, 768), BF),
        ("gd", (384, 768), F32),
        ("acc0", (96, 576), F32),
        ("acc1", (96, 192), F32),
        ("wu", (8, 96, 768), BF),
        ("wd", (8, 96, 768), BF),
        ("inp", (384, 768), F32),
        ("n1", (384, 768), F32),
        ("rstd1", (384, 1), F32),
        ("cotT", (768, 384), BF),
        ("nrmT", (768, 384), BF),
        ("par", (16, 768), F32),
        ("sums", (8, 768), F32),
        ("sumA", (8, 768), F32),
        ("sumB", (8, 768), F32),
        ("sumC", (8, 768), F32),
        ("sumD", (4, 8, 768), F32),
        ("cut", (8, 8, 96), F32),
        ("snA", (4, 3, 144, 128), BF),
        ("rcA", (4, 3, 144, 128), BF),
        ("sbA", (4, 3, 96, 128), BF),
        ("QT", (3, 64, 512), BF),
        ("KT", (3, 64, 1024), BF),
        ("VT", (3, 64, 1024), BF),
        ("P", (3, 1024, 512), BF),
        ("O", (3, 48, 512), F32),
        ("inv", (3, 8, 512), F32),
        ("snO", (4, 3, 48, 128), BF),
        ("rcO", (4, 3, 48, 128), BF),
        ("snD", (4, 3, 48, 128), BF),
        ("rcD", (4, 3, 48, 128), BF),
        ("snG", (4, 3, 144, 128), BF),
        ("rcG", (4, 3, 144, 128), BF),
        ("snX", (3, 96, 512), F32),
        ("rcX", (3, 96, 512), F32),
        ("kvX", (3, 96, 512), F32),
        ("attT", (192, 384), BF),
        ("gpT", (576, 384), BF),
        ("ps", (4, 3, 128, 768), BF),
        ("psA", (4, 3, 64, 768), BF),
        ("psH", (4, 3, 64, 768), BF),
        ("psB", (4, 3, 64, 768), BF),
        ("mid", (3, 64, 768), F32),
        ("n2", (3, 64, 768), F32),
        ("rstd2", (3, 64, 1), F32),
        ("gm", (3, 64, 768), F32),
        ("ntk", (384, 768), BF),
        ("ntT", (768, 384), BF),
        ("act", (384, 768), BF),
        ("gp", (384, 768), BF),
        ("gb", (384, 768), BF),
        ("gbT", (768, 384), BF),
    ]
    for p, width in enumerate((576, 192, 768, 768)):
        for kind in ("l1s", "l1r", "l2s", "l2r"):
            vm.append((f"{kind}{p}", (4, 96, width), BF))
    sems = [
        ("qa_s", (4, 3)), ("qa_r", (4, 3)),
        ("sa_s", (4, 3)), ("sa_r", (4, 3)),
        ("o_s", (4, 3)), ("o_r", (4, 3)),
        ("d_s", (4, 3)), ("d_r", (4, 3)),
        ("g_s", (4, 3)), ("g_r", (4, 3)),
        ("x_s", (3,)), ("x_r", (3,)),
        ("nt_s", (3,)), ("nt_r", (3,)),
        ("gb_s", (3,)), ("gb_r", (3,)),
        ("ot_s", (3,)), ("ot_r", (3,)),
        ("gt_s", (3,)), ("gt_r", (3,)),
        ("sm_s", (8,)), ("sm_r", (8,)),
        ("sml_s", (7,)), ("sml_r", (8,)),
    ]
    for name, shape in (
        ("ag_s", (8,)), ("ag_r", (8,)), ("ps_s", (3, 2)), ("ps_r", (3, 2)),
        ("l1_s", (4,)), ("l1_r", (4,)), ("l2_s", (4,)), ("l2_r", (4,)),
    ):
        sems += [(f"{name}{q}", shape) for q in range(4)]
    names = [n for n, _ in inputs] + [o[0] for o in outputs] + [v[0] for v in vm] + [n for n, _ in sems]
    vmem = pl.BlockSpec(memory_space=pltpu.VMEM)
    out = pl.pallas_call(
        partial(layer_kernel, names=names),
        out_shape=[jax.ShapeDtypeStruct(shape, dtype) for _, shape, dtype in outputs],
        in_specs=[
            pl.BlockSpec(memory_space=pltpu.SMEM) if n == "in_len" else vmem for n, _ in inputs
        ],
        out_specs=[vmem] * len(outputs),
        scratch_shapes=[pltpu.VMEM(shape, dtype) for _, shape, dtype in vm]
        + [pltpu.SemaphoreType.DMA(shape) for _, shape in sems],
        compiler_params=pltpu.CompilerParams(
            collective_id=0, has_side_effects=True, vmem_limit_bytes=60 * 1024 * 1024
        ),
    )(*[v for _, v in inputs])
    shapes = [jax.ShapeDtypeStruct(o.shape, o.dtype) for o in out]

    def hand_over(*refs):
        for n in range(len(shapes)):
            refs[len(shapes) + n][...] = refs[n][...]

    out = pl.pallas_call(
        hand_over,
        out_shape=shapes,
        in_specs=[vmem] * len(shapes),
        out_specs=[vmem] * len(shapes),
    )(*out)
    out_tok, out_gtok, gain, shift, obias, gqkv, qvb, gout, gup, upb, gdown = out
    return (
        out_tok.reshape(3, 128, 768),
        out_gtok.reshape(3, 128, 768),
        gain,
        shift,
        obias,
        jnp.transpose(gqkv, (1, 0, 2)),
        qvb,
        gout,
        gup,
        upb.reshape(768),
        jnp.transpose(gdown),
    )


def solution(mesh):
    placed = (
        P(None, "seq", None),
        P(None, "seq", None),
        P(),
        P(None, None, "seq"),
        P(None, "seq"),
        P(None, "seq"),
        P(None, "seq"),
        P(None, "seq"),
        P("seq", None, "head"),
        P(None, "head"),
        P("head", "seq"),
        P("seq", "head"),
        P("head"),
        P("head", "seq"),
    )
    layout = (mesh.shape["seq"], mesh.shape["head"])

    def step(tokens, *others):
        one_kernel = layout == (8, 4) and tokens.shape == (3, 1024, 768)
        return over(fast_device if one_kernel else per_device)(tokens, *others)

    def over(device):
        return jax.shard_map(
        device,
        mesh=mesh,
        in_specs=placed,
        out_specs=(
            P(None, "seq", None),
            P(None, "seq", None),
            P(None, "seq"),
            P(None, "seq"),
            P(None, "seq"),
            P("seq", None, "head"),
            P(None, "head"),
            P("head", "seq"),
            P("seq", "head"),
            P("head"),
            P("head", "seq"),
        ),
        check_vma=False,
    )

    return step
```

```python
from functools import partial
import math

import jax
import jax.numpy as jnp
import ml_dtypes
import numpy as np
from jax import lax
from jax.experimental import pallas as pl
from jax.experimental.pallas import tpu as pltpu
from jax.sharding import PartitionSpec as P

HDIM = 48
UNIT = 1024
BRANCHES = 5


EPSILON = 1e-05


def position_table(grid_rows, width):
    quarter = width // 4
    frequency = jnp.exp(-jnp.log(10000.0) * jnp.arange(quarter, dtype=jnp.float32) / quarter)
    along_row = grid_rows[0].astype(jnp.float32)[:, None] * frequency[None, :]
    along_col = grid_rows[1].astype(jnp.float32)[:, None] * frequency[None, :]
    return jnp.concatenate(
        [jnp.sin(along_row), jnp.cos(along_row), jnp.sin(along_col), jnp.cos(along_col)], axis=1
    )


def layer_norm(values, gain_vec, shift_vec):
    centre = values - jnp.mean(values, axis=-1, keepdims=True)
    spread = jnp.mean(centre * centre, axis=-1, keepdims=True)
    return centre * lax.rsqrt(spread + EPSILON) * gain_vec + shift_vec


def slide_of(positions, bounds):
    return jnp.sum((positions[:, None] >= bounds[None, :]).astype(jnp.int32), axis=1)


def pair_weight(query_pos, key_pos, key_keep, head_ids, bounds, seg_unit):
    same_slide = slide_of(query_pos, bounds)[:, None] == slide_of(key_pos, bounds)[None, :]
    visible = same_slide & ((key_keep[None, :] > 0) | (query_pos[:, None] == key_pos[None, :]))
    counted = jnp.zeros((head_ids.shape[0], query_pos.shape[0], key_pos.shape[0]), jnp.float32)
    for branch in range(BRANCHES):
        stride = 2**branch
        span = seg_unit * stride
        same_seg = query_pos[:, None] // span == key_pos[None, :] // span
        query_on = query_pos[None, :] % stride == head_ids[:, None] % stride
        key_on = key_pos[None, :] % stride == head_ids[:, None] % stride
        counted = counted + (same_seg[None] & query_on[:, :, None] & key_on[:, None, :]).astype(
            jnp.float32
        )
    return counted * visible[None].astype(jnp.float32)


def head_total(partial_sum):
    return lax.psum(partial_sum.astype(jnp.bfloat16), "head").astype(jnp.float32)


def per_device(
    tokens,
    cotangent,
    lengths,
    coords,
    keep_mask,
    ln_gains,
    ln_shifts,
    out_bias,
    w_qkv,
    qv_bias,
    w_out,
    w_up,
    up_bias,
    w_down,
):
    micro_count, tok_local, width = tokens.shape
    row_len = tok_local * lax.axis_size("seq")
    seg_unit = UNIT
    block_count = row_len // seg_unit
    heads_local = w_qkv.shape[2] // HDIM
    local_width = heads_local * HDIM
    inv_root = 1.0 / math.sqrt(HDIM)
    head_ids = lax.axis_index("head") * heads_local + jnp.arange(heads_local, dtype=jnp.int32)
    own_pos = lax.axis_index("seq") * tok_local + jnp.arange(tok_local, dtype=jnp.int32)
    block_starts = jnp.arange(block_count, dtype=jnp.int32) * seg_unit
    bias_qv = qv_bias.astype(jnp.float32)
    bias_up = up_bias.astype(jnp.float32)
    sum_qkv = jnp.zeros((width, 3, local_width), jnp.float32)
    sum_out = jnp.zeros((local_width, width), jnp.float32)
    sum_up = jnp.zeros((width, w_up.shape[1]), jnp.float32)
    sum_down = jnp.zeros((w_down.shape[0], width), jnp.float32)
    sum_gain = jnp.zeros((2, width), jnp.float32)
    sum_shift = jnp.zeros((2, width), jnp.float32)
    sum_obias = jnp.zeros((2, width), jnp.float32)
    sum_qvb = jnp.zeros((2, local_width), jnp.float32)
    sum_upb = jnp.zeros((w_up.shape[1],), jnp.float32)
    out_rows = []
    grad_rows = []
    for micro_id in range(micro_count):
        full_qkv, full_out, full_up, full_down, gain_rows, shift_rows, obias_rows = (
            lax.all_gather(w_qkv, "seq", axis=0, tiled=True),
            lax.all_gather(w_out, "seq", axis=1, tiled=True),
            lax.all_gather(w_up, "seq", axis=0, tiled=True),
            lax.all_gather(w_down, "seq", axis=1, tiled=True),
            lax.all_gather(ln_gains, "seq", axis=1, tiled=True),
            lax.all_gather(ln_shifts, "seq", axis=1, tiled=True),
            lax.all_gather(out_bias, "seq", axis=1, tiled=True),
        )
        gain_rows = gain_rows.astype(jnp.float32)
        shift_rows = shift_rows.astype(jnp.float32)
        obias_rows = obias_rows.astype(jnp.float32)
        bounds = jnp.cumsum(lengths[micro_id])[:-1]
        inputs = tokens[micro_id].astype(jnp.float32) + position_table(coords[:, micro_id], width)
        normed = layer_norm(inputs, gain_rows[0], shift_rows[0]).astype(jnp.bfloat16)
        projected = jnp.einsum("td,dcf->tcf", normed, full_qkv, preferred_element_type=jnp.float32)
        queries = (
            (projected[:, 0] + bias_qv[0])
            .astype(jnp.bfloat16)
            .reshape(tok_local, heads_local, HDIM)
        )
        key_rows = projected[:, 1].astype(jnp.bfloat16).reshape(tok_local, heads_local, HDIM)
        value_rows = (
            (projected[:, 2] + bias_qv[1])
            .astype(jnp.bfloat16)
            .reshape(tok_local, heads_local, HDIM)
        )
        keep_local = keep_mask[micro_id].astype(jnp.bfloat16)
        key_all, value_all, keep_all = (
            lax.all_gather(key_rows, "seq", axis=0, tiled=True),
            lax.all_gather(value_rows, "seq", axis=0, tiled=True),
            lax.all_gather(keep_local, "seq", axis=0, tiled=True),
        )

        def key_block(key_src, value_src, keep_src, offset):
            key_blk = lax.dynamic_slice_in_dim(key_src, offset, seg_unit, 0)
            value_blk = lax.dynamic_slice_in_dim(value_src, offset, seg_unit, 0)
            keep_blk = lax.dynamic_slice_in_dim(keep_src, offset, seg_unit, 0)
            key_pos = offset + jnp.arange(seg_unit, dtype=jnp.int32)
            scores = (
                jnp.einsum("thd,khd->htk", queries, key_blk, preferred_element_type=jnp.float32)
                * inv_root
            )
            weight = pair_weight(own_pos, key_pos, keep_blk, head_ids, bounds, seg_unit)
            return (key_blk, value_blk, scores, weight)

        def stats_step(running, offset):
            row_peak, row_total = running
            _, _, scores, weight = key_block(key_all, value_all, keep_all, offset)
            live = weight > 0
            new_peak = jnp.maximum(row_peak, jnp.max(jnp.where(live, scores, -1e30), axis=2))
            fresh = jnp.sum(
                jnp.where(live, weight * jnp.exp(scores - new_peak[:, :, None]), 0.0), axis=2
            )
            return ((new_peak, row_total * jnp.exp(row_peak - new_peak) + fresh), None)

        start_stats = (
            jnp.full((heads_local, tok_local), -1e30, jnp.float32),
            jnp.zeros((heads_local, tok_local), jnp.float32),
        )
        (row_peak, row_total), _ = lax.scan(stats_step, start_stats, block_starts)
        log_total = row_peak + jnp.log(row_total)

        def value_step(running, offset):
            _, value_blk, scores, weight = key_block(key_all, value_all, keep_all, offset)
            prob_low = (weight * jnp.exp(scores - log_total[:, :, None])).astype(jnp.bfloat16)
            return (
                running
                + jnp.einsum(
                    "htk,khd->thd", prob_low, value_blk, preferred_element_type=jnp.float32
                ),
                None,
            )

        attended, _ = lax.scan(
            value_step, jnp.zeros((tok_local, heads_local, HDIM), jnp.float32), block_starts
        )
        attended_low = attended.astype(jnp.bfloat16).reshape(tok_local, local_width)
        middle = (
            inputs
            + head_total(jnp.dot(attended_low, full_out, preferred_element_type=jnp.float32))
            + obias_rows[0]
        )
        normed_two = layer_norm(middle, gain_rows[1], shift_rows[1]).astype(jnp.bfloat16)
        hidden_pre = jnp.dot(normed_two, full_up, preferred_element_type=jnp.float32) + bias_up
        activated = jax.nn.gelu(hidden_pre, approximate=False).astype(jnp.bfloat16)
        result = (
            middle
            + head_total(jnp.dot(activated, full_down, preferred_element_type=jnp.float32))
            + obias_rows[1]
        )
        out_rows.append(result.astype(jnp.bfloat16))
        grad_out_low = cotangent[micro_id]
        grad_out_f32 = grad_out_low.astype(jnp.float32)
        sum_down = sum_down + jnp.einsum(
            "tf,td->fd", activated, grad_out_low, preferred_element_type=jnp.float32
        )
        grad_act = jnp.einsum(
            "td,fd->tf", grad_out_low, full_down, preferred_element_type=jnp.float32
        )
        _, gelu_back = jax.vjp(partial(jax.nn.gelu, approximate=False), hidden_pre)
        grad_pre_low = gelu_back(grad_act)[0].astype(jnp.bfloat16)
        sum_upb = sum_upb + jnp.sum(grad_pre_low.astype(jnp.float32), axis=0)
        sum_up = sum_up + jnp.einsum(
            "td,tf->df", normed_two, grad_pre_low, preferred_element_type=jnp.float32
        )
        grad_normed_two = head_total(
            jnp.einsum("tf,df->td", grad_pre_low, full_up, preferred_element_type=jnp.float32)
        )
        _, norm_back_two = jax.vjp(layer_norm, middle, gain_rows[1], shift_rows[1])
        grad_from_two, grad_gain_two, grad_shift_two = norm_back_two(grad_normed_two)
        grad_middle = grad_out_f32 + grad_from_two
        grad_branch_low = grad_middle.astype(jnp.bfloat16)
        sum_obias = sum_obias + jnp.stack(
            [jnp.sum(grad_branch_low.astype(jnp.float32), axis=0), jnp.sum(grad_out_f32, axis=0)]
        )
        sum_out = sum_out + jnp.einsum(
            "tf,td->fd", attended_low, grad_branch_low, preferred_element_type=jnp.float32
        )
        grad_attn_low = (
            jnp.einsum("td,fd->tf", grad_branch_low, full_out, preferred_element_type=jnp.float32)
            .astype(jnp.bfloat16)
            .reshape(tok_local, heads_local, HDIM)
        )
        row_delta = jnp.einsum("thd,thd->ht", grad_attn_low.astype(jnp.float32), attended)
        back_keys, back_values, back_keep = (
            lax.all_gather(key_rows, "seq", axis=0, tiled=True),
            lax.all_gather(value_rows, "seq", axis=0, tiled=True),
            lax.all_gather(keep_local, "seq", axis=0, tiled=True),
        )

        def key_side_step(running, offset):
            key_blk, value_blk, scores, weight = key_block(
                back_keys, back_values, back_keep, offset
            )
            prob_f32 = weight * jnp.exp(scores - log_total[:, :, None])
            grad_prob = jnp.einsum(
                "thd,khd->htk", grad_attn_low, value_blk, preferred_element_type=jnp.float32
            )
            grad_scores = (prob_f32 * (grad_prob - row_delta[:, :, None])).astype(jnp.bfloat16)
            running = running + jnp.einsum(
                "htk,khd->thd", grad_scores, key_blk, preferred_element_type=jnp.float32
            )
            prob_low = prob_f32.astype(jnp.bfloat16)
            key_term = (
                jnp.einsum("htk,thd->khd", grad_scores, queries, preferred_element_type=jnp.float32)
                * inv_root
            )
            value_term = jnp.einsum(
                "htk,thd->khd", prob_low, grad_attn_low, preferred_element_type=jnp.float32
            )
            return (
                running,
                jnp.concatenate(
                    [
                        key_term.reshape(seg_unit, local_width),
                        value_term.reshape(seg_unit, local_width),
                    ],
                    axis=1,
                ),
            )

        query_sum, terms = lax.scan(
            key_side_step, jnp.zeros((tok_local, heads_local, HDIM), jnp.float32), block_starts
        )
        owned = lax.psum_scatter(
            terms.reshape(row_len, 2 * local_width), "seq", scatter_dimension=0, tiled=True
        )
        grad_queries = query_sum * inv_root
        grad_keys = owned[:, :local_width].reshape(tok_local, heads_local, HDIM)
        grad_values = owned[:, local_width:].reshape(tok_local, heads_local, HDIM)
        grad_q_low = grad_queries.astype(jnp.bfloat16).reshape(tok_local, local_width)
        grad_k_low = grad_keys.astype(jnp.bfloat16).reshape(tok_local, local_width)
        grad_v_low = grad_values.astype(jnp.bfloat16).reshape(tok_local, local_width)
        sum_qvb = sum_qvb + jnp.stack(
            [
                jnp.sum(grad_q_low.astype(jnp.float32), axis=0),
                jnp.sum(grad_v_low.astype(jnp.float32), axis=0),
            ]
        )
        grad_proj = jnp.stack([grad_q_low, grad_k_low, grad_v_low], axis=1)
        sum_qkv = sum_qkv + jnp.einsum(
            "td,tcf->dcf", normed, grad_proj, preferred_element_type=jnp.float32
        )
        grad_normed = head_total(
            jnp.einsum("tcf,dcf->td", grad_proj, full_qkv, preferred_element_type=jnp.float32)
        )
        _, norm_back_one = jax.vjp(layer_norm, inputs, gain_rows[0], shift_rows[0])
        grad_from_one, grad_gain_one, grad_shift_one = norm_back_one(grad_normed)
        grad_rows.append((grad_middle + grad_from_one).astype(jnp.bfloat16))
        sum_gain = sum_gain + jnp.stack([grad_gain_one, grad_gain_two])
        sum_shift = sum_shift + jnp.stack([grad_shift_one, grad_shift_two])
    grad_qkv, grad_out, grad_up, grad_down, grad_gain, grad_shift, grad_obias = (
        lax.psum_scatter(sum_qkv, "seq", scatter_dimension=0, tiled=True),
        lax.psum_scatter(sum_out, "seq", scatter_dimension=1, tiled=True),
        lax.psum_scatter(sum_up, "seq", scatter_dimension=0, tiled=True),
        lax.psum_scatter(sum_down, "seq", scatter_dimension=1, tiled=True),
        lax.psum_scatter(sum_gain, "seq", scatter_dimension=1, tiled=True),
        lax.psum_scatter(sum_shift, "seq", scatter_dimension=1, tiled=True),
        lax.psum_scatter(sum_obias, "seq", scatter_dimension=1, tiled=True),
    )
    grad_qvb, grad_upb = lax.psum((sum_qvb, sum_upb), "seq")
    return (
        jnp.stack(out_rows),
        jnp.stack(grad_rows),
        grad_gain,
        grad_shift,
        grad_obias,
        grad_qkv,
        grad_qvb,
        grad_out,
        grad_up,
        grad_upb,
        grad_down,
    )


NEG = 1792.0
ROOT = 1.0 / math.sqrt(HDIM)
BF = jnp.bfloat16
F32 = jnp.float32
MESH = pl.DeviceIdType.MESH
LEVELS = [math.sqrt(HDIM) * math.log((b + 1) / b) for b in range(1, BRANCHES)]
LEVEL_HIGH = [float(np.asarray(v, ml_dtypes.bfloat16)) for v in LEVELS]
LEVEL_LOW = [v - w for v, w in zip(LEVELS, LEVEL_HIGH)]


def nn(a, b):
    return lax.dot_general(a, b, (((1,), (0,)), ((), ())), preferred_element_type=F32)


def nt(a, b):
    return lax.dot_general(a, b, (((1,), (1,)), ((), ())), preferred_element_type=F32)


def tn(a, b):
    return lax.dot_general(a, b, (((0,), (0,)), ((), ())), preferred_element_type=F32)


def tt(a, b):
    return lax.dot_general(a, b, (((0,), (1,)), ((), ())), preferred_element_type=F32)


def four(index, values):
    return jnp.where(
        index == 0,
        values[0],
        jnp.where(index == 1, values[1], jnp.where(index == 2, values[2], values[3])),
    )


def pair_features(pos, slide, keep, head, for_keys):
    shape = (16, pos.shape[1])
    row = lax.broadcasted_iota(jnp.int32, shape, 0)
    pos = jnp.broadcast_to(pos, shape)
    slide = jnp.broadcast_to(slide, shape)
    level = jnp.where(row >= 8, row - 8, row - 4)
    on = jnp.bitwise_and(pos - head, four(level, [1, 3, 7, 15])) == 0
    on = on & (row < 12)
    if for_keys:
        keep = jnp.broadcast_to(keep, shape)
        size = jnp.where(row < 8, four(level, LEVEL_HIGH), four(level, LEVEL_LOW))
        other = jnp.where(slide != row, -NEG, 0.0)
        padding = jnp.where(keep > 0.0, 0.0, -NEG)
    else:
        size = jnp.ones(shape, F32)
        other = jnp.where(slide == row, 1.0, 0.0)
        padding = jnp.ones(shape, F32)
    value = jnp.where(row < 3, other, jnp.where(row == 3, padding, jnp.where(on, size, 0.0)))
    return value.astype(BF)


def layer_kernel(*refs, names):
    r_ = dict(zip(names, refs))

    class N:
        pass

    g = N()
    for k, v in r_.items():
        setattr(g, k, v)
    s = lax.axis_index("seq")
    h = lax.axis_index("head")
    z, y = lax.div(s, 2), lax.rem(s, 2)
    x, c = lax.div(h, 2), lax.rem(h, 2)
    a, j = lax.div(s, 4), lax.rem(s, 4)
    sib = (s, h + 1 - 2 * c)
    xp = (s, lax.rem(h + 2, 4))
    yp = (s + 1 - 2 * y, h)
    top = lax.div(z, 2)
    zs = [z + 1 - 2 * lax.rem(z, 2), 2 - top, 3 - 3 * top]
    zm = [(2 * q + y, h) for q in zs]
    zy = [(2 * q + 1 - y, h) for q in zs]
    qs = zs + [z]
    inner = (z == 1) | (z == 2)
    outer = jnp.logical_not(inner)
    part = [(4 * c + i, 2 * x + a) for i in range(4)]
    own = [(a == c) & (j == i) for i in range(4)]
    is_own = jnp.where(a == c, 1, 0)
    head = 8 * x + s
    R = 3
    T = 128

    def rdma(src, dst, ss, rs, dev):
        return pltpu.make_async_remote_copy(
            src_ref=src, dst_ref=dst, send_sem=ss, recv_sem=rs, device_id=dev, device_id_type=MESH
        )

    def not_own(i):
        return jnp.logical_not(own[i])

    def lanes(r, n=128):
        return pl.ds(pl.multiple_of(n * r, n), n)

    def rows(r, n=128):
        return pl.ds(pl.multiple_of(n * r, n), n)

    def half(r, who):
        return pl.ds(pl.multiple_of(T * r + 64 * who, 64), 64)

    bar = pltpu.get_barrier_semaphore()
    for dev in [sib, xp, yp] + zm + zy:
        pl.semaphore_signal(bar, inc=1, device_id=dev, device_id_type=MESH)
    for i in range(4):

        @pl.when(not_own(i))
        def _():
            pl.semaphore_signal(bar, inc=1, device_id=part[i], device_id_type=MESH)

    def piece(p, k):
        if p < 2:
            return g.wq.at[k, pl.ds(48 * p, 48)]
        return (g.wu if p == 2 else g.wd).at[k]

    def four_of(name):
        return [r_[f"{name}{q}"] for q in range(4)]

    AGS, AGR, PSS, PSR = four_of("ag_s"), four_of("ag_r"), four_of("ps_s"), four_of("ps_r")
    L1SS, L1RS, L2SS, L2RS = four_of("l1_s"), four_of("l1_r"), four_of("l2_s"), four_of("l2_r")

    def ag_y(p):
        rdma(piece(p, s), piece(p, s), AGS[p].at[0], AGR[p].at[s], yp).start()

    def ag_z(p):
        @pl.when(outer)
        def _():
            for t in (1, 0):
                rdma(piece(p, s), piece(p, s), AGS[p].at[1 + t], AGR[p].at[s], zm[t]).start()

        @pl.when(inner)
        def _():
            for t in range(3):
                rdma(piece(p, s), piece(p, s), AGS[p].at[1 + t], AGR[p].at[s], zm[t]).start()

    def ag_forward(p, t):
        k = zm[t][0]
        w = piece(p, k)
        rdma(w, w, AGS[p].at[4 + t], AGR[p].at[k], zm[t]).wait_recv()
        if t == 2:

            @pl.when(inner)
            def _():
                rdma(w, w, AGS[p].at[7], AGR[p].at[k], zm[0]).start()

        rdma(w, w, AGS[p].at[4 + t], AGR[p].at[k], yp).start()

    def ag_wait(p):
        for q in qs:
            w = piece(p, 2 * q + 1 - y)
            rdma(w, w, AGS[p].at[0], AGR[p].at[2 * q + 1 - y], yp).wait_recv()

    def ag_drain(p):
        w = piece(p, s)
        for t in (0, 1, 2, 4, 5, 6):
            rdma(w, w, AGS[p].at[t], AGR[p].at[s], yp).wait_send()

        @pl.when(inner)
        def _():
            for t in (3, 7):
                rdma(w, w, AGS[p].at[t], AGR[p].at[s], yp).wait_send()

    g.wq[s] = jnp.concatenate(
        [g.in_w3[0], g.in_w3[1], g.in_w3[2], jnp.transpose(g.in_wo[...])], axis=1
    )
    g.tmp[...] = jnp.zeros_like(g.tmp)
    g.tmp[0:2, 0:96] = g.in_lng[...].astype(F32)
    g.tmp[2:4, 0:96] = g.in_lns[...].astype(F32)
    g.tmp[4:6, 0:96] = g.in_ob[...].astype(F32)
    g.tmp[6:9, :] = g.in_keep[...].astype(F32)
    g.sml[s] = g.tmp[...].astype(BF)
    g.wu[s] = g.in_wu[...]
    g.wd[s] = g.in_wd[...]
    pl.semaphore_wait(bar, 13 - is_own)
    others = [yp] + zm + zy
    for t, dev in enumerate(others):
        rdma(g.sml.at[s], g.sml.at[s], g.sml_s.at[t], g.sml_r.at[s], dev).start()
    for p in range(2):
        ag_y(p)
        ag_z(p)
    ag_y(2)
    ag_z(2)
    ag_y(3)

    lane = lax.broadcasted_iota(jnp.int32, (1, 768), 1)
    freq = jnp.exp(
        -math.log(10000.0) * lax.rem(lane, 192).astype(F32) / 192.0
    )
    for r in range(R):
        col = jnp.transpose(
            jnp.concatenate([g.in_crd[r].astype(F32), jnp.zeros((6, 128), F32)], axis=0)
        )
        pieces = []
        for t in range(6):
            f = freq[:, 128 * t : 128 * t + 128]
            ang = col[:, (0 if t < 3 else 1) : (1 if t < 3 else 2)] * f
            if t % 3 == 0:
                pieces.append(jnp.sin(ang))
            elif t % 3 == 2:
                pieces.append(jnp.cos(ang))
            else:
                low_half = lax.broadcasted_iota(jnp.int32, (T, 128), 1) < 64
                pieces.append(jnp.where(low_half, jnp.sin(ang), jnp.cos(ang)))
        v = g.in_tok[rows(r), :].astype(F32) + jnp.concatenate(pieces, axis=1)
        g.inp[rows(r), :] = v
        v = v - jnp.mean(v, axis=1, keepdims=True)
        rstd = lax.rsqrt(jnp.mean(v * v, axis=1, keepdims=True) + EPSILON)
        g.n1[rows(r), :] = v * rstd
        g.rstd1[rows(r), :] = rstd
        g.cotT[:, 128 * r : 128 * r + 128] = jnp.transpose(g.in_cot[rows(r), :])
    g.sums[...] = jnp.zeros_like(g.sums)

    for t, dev in enumerate(others):
        k = dev[0]
        rdma(g.sml.at[k], g.sml.at[k], g.sml_s.at[t], g.sml_r.at[k], dev).wait_recv()
    par = jnp.concatenate([g.sml[k].astype(F32)[:, 0:96] for k in range(8)], axis=1)
    g.par[...] = par
    g1, s1, ob0, ob1 = par[1:2], par[3:4], par[4:5], par[5:6]
    g0 = par[0:1]
    qvb = g.in_qvb[...].astype(F32)
    qkv_bias = jnp.concatenate([qvb[0:1], jnp.zeros((1, 192), F32), qvb[1:2]], axis=1)
    for r in range(R):
        nr = (g.n1[rows(r), :] * g0 + par[2:3]).astype(BF)
        g.nrm[rows(r), :] = nr
        g.nrmT[:, 128 * r : 128 * r + 128] = jnp.transpose(nr)
    ag_forward(0, 0)
    ag_forward(1, 0)
    ag_forward(0, 1)
    ag_forward(1, 1)
    ag_forward(0, 2)
    ag_forward(1, 2)
    ag_forward(2, 0)
    ag_wait(0)
    ag_wait(1)

    def send_part(i, r, src, dst, ss, rs):
        @pl.when(not_own(i))
        def _():
            rdma(src.at[i, r], dst.at[j, r], ss.at[i, r], rs.at[j, r], part[i]).start()

        @pl.when(own[i])
        def _():
            dst[i, r] = src[i, r]

    def wait_part(i, r, dst, ss, rs):
        @pl.when(not_own(i))
        def _():
            rdma(dst.at[i, r], dst.at[i, r], ss.at[i, r], rs.at[i, r], part[i]).wait_recv()

    def drain_part(i, r, src, ss, rs):
        @pl.when(not_own(i))
        def _():
            rdma(src.at[i, r], src.at[i, r], ss.at[i, r], rs.at[i, r], part[i]).wait_send()

    for r in range(R):
        proj = nn(g.nrm[rows(r), :], g.wq[:, :, 0:576].reshape(768, 576)) + qkv_bias
        projT = jnp.transpose(proj).astype(BF)
        for i in range(4):
            for t in range(3):
                g.snA[i, r, 48 * t : 48 * t + 48, :] = projT[192 * t + 48 * i : 192 * t + 48 * i + 48]
            send_part(i, r, g.snA, g.rcA, g.qa_s, g.qa_r)
        if r == 1:
            ag_forward(2, 1)
    ag_z(3)

    g.wo[...] = g.wq[:, :, 576:768].reshape(768, 192)

    def slide_of_row(r, pos):
        b0 = g.in_len[r, 0]
        b1 = b0 + g.in_len[r, 1]
        return jnp.where(pos >= b0, 1, 0) + jnp.where(pos >= b1, 1, 0)

    ones_rows = jnp.where(lax.broadcasted_iota(jnp.int32, (16, 1024), 0) == 0, 1.0, 0.0).astype(BF)

    def attn_fwd(r):
        for i in range(4):
            wait_part(i, r, g.rcA, g.qa_s, g.qa_r)
            rdma(
                g.rcA.at[i, r, pl.ds(48, 96)], g.sbA.at[i, r], g.sa_s.at[i, r], g.sa_r.at[i, r], sib
            ).start()
        iota = lax.broadcasted_iota(jnp.int32, (1, 512), 1)
        pos_own = 512 * c + iota
        pos_sib = 512 * (1 - c) + iota
        keep_own = jnp.concatenate(
            [g.sml[4 * c + i].astype(F32)[6 + r : 7 + r] for i in range(4)], axis=1
        )
        keep_sib = jnp.concatenate(
            [g.sml[4 * (1 - c) + i].astype(F32)[6 + r : 7 + r] for i in range(4)], axis=1
        )
        pos = jnp.concatenate([pos_own, pos_sib], axis=1)
        kf = pair_features(
            pos, slide_of_row(r, pos), jnp.concatenate([keep_own, keep_sib], axis=1), head, True
        )
        qf = pair_features(pos_own, slide_of_row(r, pos_own), None, head, False)
        g.QT[r, 0:48, :] = jnp.concatenate([g.rcA[i, r, 0:48, :] for i in range(4)], axis=1)
        g.QT[r, 48:64, :] = qf
        g.KT[r, 48:64, :] = kf
        g.VT[r, 48:64, :] = ones_rows
        for i in range(4):
            g.KT[r, 0:48, 128 * i : 128 * i + 128] = g.rcA[i, r, 48:96, :]
            g.VT[r, 0:48, 128 * i : 128 * i + 128] = g.rcA[i, r, 96:144, :]
        for i in range(4):
            rdma(g.sbA.at[i, r], g.sbA.at[i, r], g.sa_s.at[i, r], g.sa_r.at[i, r], sib).wait_recv()
            g.KT[r, 0:48, 512 + 128 * i : 640 + 128 * i] = g.sbA[i, r, 0:48, :]
            g.VT[r, 0:48, 512 + 128 * i : 640 + 128 * i] = g.sbA[i, r, 48:96, :]
        eye = lax.broadcasted_iota(jnp.int32, (256, 256), 0) == lax.broadcasted_iota(
            jnp.int32, (256, 256), 1
        )
        for qc in range(2):
            q0 = 256 * qc
            sc = tn(g.KT[r], g.QT[r, :, q0 : q0 + 256])
            lift = jnp.where(eye, NEG * (1.0 - keep_own[:, q0 : q0 + 256]), 0.0)
            blocks = [sc[256 * t : 256 * t + 256] for t in range(4)]
            blocks[qc] = blocks[qc] + lift
            sc = jnp.concatenate(blocks, axis=0)
            peak = jnp.max(sc, axis=0, keepdims=True)
            pb = jnp.exp((sc - peak) * ROOT).astype(BF)
            g.P[r, :, q0 : q0 + 256] = pb
            o = nn(g.VT[r], pb)
            inv = 1.0 / o[48:49]
            o = o[0:48] * inv
            g.O[r, :, q0 : q0 + 256] = o
            g.inv[r, :, q0 : q0 + 256] = jnp.broadcast_to(inv, (8, 256))
            for u in range(2):
                i = 2 * qc + u
                g.snO[i, r] = o[:, 128 * u : 128 * u + 128].astype(BF)
                send_part(i, r, g.snO, g.rcO, g.o_s, g.o_r)

    attn_fwd(0)
    ag_forward(2, 2)
    attn_fwd(1)
    ag_forward(3, 0)
    attn_fwd(2)

    def ps_start(kind, r, part_sum):
        g.ps[kind, r] = part_sum.astype(BF)
        rdma(
            g.ps.at[kind, r, pl.ds(pl.multiple_of(64 * (1 - c), 64), 64)],
            g.psA.at[kind, r],
            PSS[kind].at[r, 0],
            PSR[kind].at[r, 0],
            sib,
        ).start()

    def ps_mid(kind, r):
        dst = g.psA.at[kind, r]
        rdma(dst, dst, PSS[kind].at[r, 0], PSR[kind].at[r, 0], sib).wait_recv()
        mine = g.ps[kind, r, pl.ds(pl.multiple_of(64 * c, 64), 64), :].astype(F32)
        g.psH[kind, r] = (mine + g.psA[kind, r].astype(F32)).astype(BF)
        rdma(
            g.psH.at[kind, r], g.psB.at[kind, r], PSS[kind].at[r, 1], PSR[kind].at[r, 1], xp
        ).start()

    def ps_end(kind, r):
        dst = g.psB.at[kind, r]
        rdma(dst, dst, PSS[kind].at[r, 1], PSR[kind].at[r, 1], xp).wait_recv()
        return g.psH[kind, r].astype(F32) + g.psB[kind, r].astype(F32)

    def share_start(ref, r, ss, rs):
        rdma(ref.at[half(r, c)], ref.at[half(r, c)], ss.at[r], rs.at[r], sib).start()

    def share_wait(ref, r, ss, rs):
        dst = ref.at[half(r, 1 - c)]
        rdma(dst, dst, ss.at[r], rs.at[r], sib).wait_recv()

    for r in range(R):
        for i in range(4):
            wait_part(i, r, g.rcO, g.o_s, g.o_r)
            g.attT[48 * i : 48 * i + 48, 128 * r : 128 * r + 128] = g.rcO[i, r]
        att = jnp.transpose(g.attT[:, 128 * r : 128 * r + 128])
        ps_start(0, r, nt(att, g.wo[...]))
        if r > 0:
            ps_mid(0, r - 1)
        if r == 1:
            ag_forward(3, 1)
    ps_mid(0, R - 1)
    ag_forward(3, 2)
    ag_wait(2)

    def second_norm(r):
        v = g.inp[half(r, c), :] + ps_end(0, r) + ob0
        g.mid[r] = v
        v = v - jnp.mean(v, axis=1, keepdims=True)
        rstd = lax.rsqrt(jnp.mean(v * v, axis=1, keepdims=True) + EPSILON)
        v = v * rstd
        g.n2[r] = v
        g.rstd2[r] = rstd
        g.ntk[half(r, c), :] = (v * g1 + s1).astype(BF)
        share_start(g.ntk, r, g.nt_s, g.nt_r)

    up_bias = g.in_upb[...].astype(F32).reshape(1, 768)

    def feed_up(r):
        share_wait(g.ntk, r, g.nt_s, g.nt_r)
        pre = nn(g.ntk[rows(r), :], g.wu[...].reshape(768, 768)) + up_bias
        cdf = 0.5 * (1.0 + lax.erf(pre * (1.0 / math.sqrt(2.0))))
        pdf = jnp.exp(-0.5 * pre * pre) * (1.0 / math.sqrt(2.0 * math.pi))
        g.act[rows(r), :] = (pre * cdf).astype(BF)
        g.gd[rows(r), :] = cdf + pre * pdf

    def feed_back(r):
        gact = nn(g.in_cot[rows(r), :], g.wd[...].reshape(768, 768))
        g.gp[rows(r), :] = (gact * g.gd[rows(r), :]).astype(BF)
        ps_start(1, r, nt(g.gp[rows(r), :], g.wu[...].reshape(768, 768)))

    def pack(v):
        width = v.shape[1]
        tiles = [v[:, 128 * t : 128 * t + 128] for t in range(width // 128)]
        if width % 128:
            rest = v[:, width - 64 :]
            tiles.append(jnp.concatenate([rest[0:48], rest[48:96]], axis=1))
        return jnp.concatenate(tiles, axis=0)

    def unpack(v):
        count = v.shape[0] // 96
        tiles = [v[96 * t : 96 * t + 96] for t in range(count)]
        if v.shape[0] % 96:
            rest = v[96 * count :]
            tiles.append(jnp.concatenate([rest[:, 0:64], rest[:, 64:128]], axis=0))
        return jnp.concatenate(tiles, axis=1)

    def block(p, k):
        return pack(raw_block(p, k))

    def raw_block(p, k):
        b = pl.ds(pl.multiple_of(96 * k, 96), 96)
        if p == 0:
            return nt(g.nrmT[b, :], g.gpT[...])
        if p == 1:
            return nt(g.gbT[b, :], g.attT[...])
        if p == 2:
            return nn(g.ntT[b, :], g.gp[...])
        return nn(g.cotT[b, :], g.act[...])

    L1S = [g.l1s0, g.l1s1, g.l1s2, g.l1s3]
    L1R = [g.l1r0, g.l1r1, g.l1r2, g.l1r3]
    L2S = [g.l2s0, g.l2s1, g.l2s2, g.l2s3]
    L2R = [g.l2r0, g.l2r1, g.l2r2, g.l2r3]
    g.acc = [g.acc0, g.acc1, g.acc2, g.acc3]

    def rs_first(p, start=0, stop=4):
        def step(t, _):
            q = four(t, [zs[2], zs[1], zs[0], z])
            L1S[p][q] = block(p, 2 * q + 1 - y).astype(BF)
            rdma(L1S[p].at[q], L1R[p].at[q], L1SS[p].at[q], L1RS[p].at[q], yp).start()
            return 0

        lax.fori_loop(start, stop, step, 0)

    def reduced(p, q):
        dst = L1R[p].at[q]
        rdma(dst, dst, L1SS[p].at[q], L1RS[p].at[q], yp).wait_recv()
        return block(p, 2 * q + y) + L1R[p][q].astype(F32)

    def rs_far(p):
        @pl.when(outer)
        def _():
            q = zs[2]
            L2S[p][q] = reduced(p, q).astype(BF)
            rdma(L2S[p].at[q], L2R[p].at[zs[0]], L2SS[p].at[q], L2RS[p].at[zs[0]], zm[0]).start()

    def rs_second(p, t):
        q = zs[t]

        def send():
            v = reduced(p, q)
            if t == 2:
                via = L2R[p].at[z]
                rdma(via, via, L2SS[p].at[q], L2RS[p].at[z], zm[0]).wait_recv()
                v = v + via[...].astype(F32)
            L2S[p][q] = v.astype(BF)
            rdma(L2S[p].at[q], L2R[p].at[z], L2SS[p].at[q], L2RS[p].at[z], zm[t]).start()

        if t == 2:
            pl.when(inner)(send)
        else:
            send()

    def rs_own(p):
        dst = L1R[p].at[z]
        rdma(dst, dst, L1SS[p].at[z], L1RS[p].at[z], yp).wait_recv()
        g.acc[p][...] = block(p, s) + L1R[p][z].astype(F32)

    def rs_third(p):
        acc = g.acc[p]
        for t, q in enumerate(zs):
            dst = L2R[p].at[q]

            def add(dst=dst, q=q):
                rdma(dst, dst, L2SS[p].at[q], L2RS[p].at[q], yp).wait_recv()
                acc[...] += dst[...].astype(F32)

            if t < 2:
                add()
            else:
                pl.when(inner)(add)
        return unpack(acc[...])

    def rs_drain(p):
        for q in qs:
            rdma(L1S[p].at[q], L1R[p].at[q], L1SS[p].at[q], L1RS[p].at[q], yp).wait_send()
        for q in zs:
            rdma(L2S[p].at[q], L2R[p].at[q], L2SS[p].at[q], L2RS[p].at[q], yp).wait_send()

    second_norm(0)
    second_norm(1)
    feed_up(0)
    second_norm(2)
    feed_up(1)
    feed_up(2)
    rs_first(3, 0, 1)
    ag_wait(3)
    feed_back(0)
    feed_back(1)
    ps_mid(1, 0)
    rs_first(3, 1, 2)
    feed_back(2)
    ps_mid(1, 1)
    rs_first(3, 2, 3)
    ps_mid(1, 2)
    rs_first(3, 3, 4)
    g.ntT[...] = jnp.transpose(g.ntk[...])

    def add_sum(row, value):
        g.sums[row : row + 1, :] += jnp.sum(value, axis=0, keepdims=True)

    def norm_back(grad, n, rstd, gain):
        e = grad * gain
        return rstd * (
            e - jnp.mean(e, axis=1, keepdims=True) - n * jnp.mean(e * n, axis=1, keepdims=True)
        )

    def second_back(r):
        gn = ps_end(1, r)
        n = g.n2[r]
        cot = g.in_cot[half(r, c), :].astype(F32)
        gm = cot + norm_back(gn, n, g.rstd2[r], g1)
        g.gm[r] = gm
        gb = gm.astype(BF)
        g.gb[half(r, c), :] = gb
        share_start(g.gb, r, g.gb_s, g.gb_r)
        add_sum(1, gn * n)
        add_sum(3, gn)
        add_sum(4, gb.astype(F32))
        add_sum(5, cot)

    def grad_attended(r):
        share_wait(g.gb, r, g.gb_s, g.gb_r)
        ga = jnp.transpose(nn(g.gb[rows(r), :], g.wo[...])).astype(BF)
        for i in range(4):
            g.snD[i, r] = ga[48 * i : 48 * i + 48]
            send_part(i, r, g.snD, g.rcD, g.d_s, g.d_r)

    second_back(0)
    rs_far(3)
    second_back(1)
    grad_attended(0)
    second_back(2)
    grad_attended(1)
    grad_attended(2)
    rs_second(3, 1)
    rs_first(2, 0, 2)
    for r in range(R):
        ps_start(2, r, nt(g.act[rows(r), :], g.wd[...].reshape(768, 768)))
    g.gbT[...] = jnp.transpose(g.gb[...])

    def attn_bwd(r):
        for i in range(4):
            wait_part(i, r, g.rcD, g.d_s, g.d_r)
        dk = None
        dv = None
        for qc in range(2):
            q0 = 256 * qc
            do = jnp.concatenate([g.rcD[2 * qc, r], g.rcD[2 * qc + 1, r]], axis=1)
            delta = jnp.sum(do.astype(F32) * g.O[r, :, q0 : q0 + 256], axis=0, keepdims=True)
            dp = tn(g.VT[r, 0:48, :], do)
            pn = g.P[r, :, q0 : q0 + 256].astype(F32) * g.inv[r, 0:1, q0 : q0 + 256]
            ds = (pn * (dp - delta)).astype(BF)
            pn = pn.astype(BF)
            dq = nn(g.KT[r, 0:48, :], ds) * ROOT
            for u in range(2):
                g.snG[2 * qc + u, r, 0:48, :] = dq[:, 128 * u : 128 * u + 128].astype(BF)
            dk_part = nt(g.QT[r, 0:48, q0 : q0 + 256], ds)
            dv_part = nt(do, pn)
            dk = dk_part if dk is None else dk + dk_part
            dv = dv_part if dv is None else dv + dv_part
        dk = dk * ROOT
        g.snX[r, 0:48, :] = dk[:, 512:1024]
        g.snX[r, 48:96, :] = dv[:, 512:1024]
        rdma(g.snX.at[r], g.rcX.at[r], g.x_s.at[r], g.x_r.at[r], sib).start()
        g.kvX[r, 0:48, :] = dk[:, 0:512]
        g.kvX[r, 48:96, :] = dv[:, 0:512]

    def attn_bwd_end(r):
        rdma(g.rcX.at[r], g.rcX.at[r], g.x_s.at[r], g.x_r.at[r], sib).wait_recv()
        kv = (g.kvX[r] + g.rcX[r]).astype(BF)
        for i in range(4):
            g.snG[i, r, 48:144, :] = kv[:, 128 * i : 128 * i + 128]
            send_part(i, r, g.snG, g.rcG, g.g_s, g.g_r)

    attn_bwd(0)
    ps_mid(2, 0)
    attn_bwd(1)
    attn_bwd_end(0)
    rs_first(2, 2, 3)
    ps_mid(2, 1)
    attn_bwd(2)
    attn_bwd_end(1)
    rs_first(2, 3, 4)
    ps_mid(2, 2)
    attn_bwd_end(2)
    rs_second(3, 0)
    rs_second(3, 2)
    rs_first(1)
    rs_far(2)
    rs_second(2, 1)
    rs_own(3)

    for r in range(R):
        g.out_tok[half(r, c), :] = (g.mid[r] + ps_end(2, r) + ob1).astype(BF)
        share_start(g.out_tok, r, g.ot_s, g.ot_r)
    ones = jnp.ones((8, 384), BF)
    g.sums[6:7, :] = nn(ones, g.gp[...])[0:1]

    def project_back(r):
        for i in range(4):
            wait_part(i, r, g.rcG, g.g_s, g.g_r)
            for t in range(3):
                g.gpT[192 * t + 48 * i : 192 * t + 48 * i + 48, 128 * r : 128 * r + 128] = g.rcG[
                    i, r, 48 * t : 48 * t + 48, :
                ]
        ps_start(3, r, tt(g.gpT[:, 128 * r : 128 * r + 128], g.wq[:, :, 0:576].reshape(768, 576)))

    project_back(0)
    rs_second(2, 0)
    project_back(1)
    ps_mid(3, 0)
    rs_second(2, 2)
    project_back(2)
    ps_mid(3, 1)
    rs_first(0, 0, 2)
    ps_mid(3, 2)
    rs_first(0, 2, 4)
    rs_own(2)
    rs_far(1)
    for t in (1, 0, 2):
        rs_second(1, t)
    rs_own(1)
    rs_far(0)
    g.sums[7:8, 0:576] = nt(ones, g.gpT[...])[0:1]

    def first_back(r):
        gn = ps_end(3, r)
        n = g.n1[half(r, c), :]
        gt = g.gm[r] + norm_back(gn, n, g.rstd1[half(r, c), :], g0)
        g.out_gtok[half(r, c), :] = gt.astype(BF)
        share_start(g.out_gtok, r, g.gt_s, g.gt_r)
        add_sum(0, gn * n)
        add_sum(2, gn)

    for r in range(R):
        first_back(r)
    rdma(g.sums, g.sumA, g.sm_s.at[0], g.sm_r.at[0], sib).start()
    rdma(g.sumA, g.sumA, g.sm_s.at[0], g.sm_r.at[0], sib).wait_recv()
    both = lax.broadcasted_iota(jnp.int32, (8, 768), 0) < 6
    g.sumB[...] = g.sums[...] + jnp.where(both, g.sumA[...], 0.0)
    rdma(g.sumB, g.sumC, g.sm_s.at[1], g.sm_r.at[1], yp).start()
    for t in (1, 0, 2):
        rs_second(0, t)
    rdma(g.sumC, g.sumC, g.sm_s.at[1], g.sm_r.at[1], yp).wait_recv()
    g.sumD[z] = g.sumB[...] + g.sumC[...]
    for t in range(3):
        rdma(g.sumD.at[z], g.sumD.at[z], g.sm_s.at[2 + t], g.sm_r.at[2 + z], zm[t]).start()
    rs_own(0)
    g.out_gdown[...] = rs_third(3)
    g.out_gup[...] = rs_third(2)
    g.out_gout[...] = jnp.transpose(rs_third(1))
    total = rs_third(0)
    for t in range(3):
        g.out_gqkv[t] = total[:, 192 * t : 192 * t + 192]
    for t in range(3):
        q = zs[t]
        rdma(g.sumD.at[q], g.sumD.at[q], g.sm_s.at[2 + t], g.sm_r.at[2 + q], zm[t]).wait_recv()
    total = g.sumD[0] + g.sumD[1] + g.sumD[2] + g.sumD[3]
    for k in range(8):
        g.cut[k] = total[:, 96 * k : 96 * k + 96]
    mine = g.cut[s]
    g.out_gain[...] = mine[0:2]
    g.out_shift[...] = mine[2:4]
    g.out_obias[...] = mine[4:6]
    g.out_upb[...] = total[6:7]
    g.out_qvb[0:1, :] = total[7:8, 0:192]
    g.out_qvb[1:2, :] = total[7:8, 384:576]

    for r in range(R):
        share_wait(g.out_tok, r, g.ot_s, g.ot_r)
        share_wait(g.out_gtok, r, g.gt_s, g.gt_r)
    for t, dev in enumerate(others):
        rdma(g.sml.at[s], g.sml.at[s], g.sml_s.at[t], g.sml_r.at[s], dev).wait_send()
    for p in range(4):
        ag_drain(p)
    for p in range(4):
        rs_drain(p)
    for r in range(R):
        for i in range(4):
            drain_part(i, r, g.snA, g.qa_s, g.qa_r)
            drain_part(i, r, g.snO, g.o_s, g.o_r)
            drain_part(i, r, g.snD, g.d_s, g.d_r)
            drain_part(i, r, g.snG, g.g_s, g.g_r)
            rdma(g.sbA.at[i, r], g.sbA.at[i, r], g.sa_s.at[i, r], g.sa_r.at[i, r], sib).wait_send()
        rdma(g.snX.at[r], g.rcX.at[r], g.x_s.at[r], g.x_r.at[r], sib).wait_send()
        for kind in range(4):
            for t in range(2):
                rdma(
                    g.psH.at[kind, r], g.psB.at[kind, r], PSS[kind].at[r, t], PSR[kind].at[r, t], xp
                ).wait_send()
        for ref, ss, rs in (
            (g.ntk, g.nt_s, g.nt_r),
            (g.gb, g.gb_s, g.gb_r),
            (g.out_tok, g.ot_s, g.ot_r),
            (g.out_gtok, g.gt_s, g.gt_r),
        ):
            rdma(ref.at[half(r, c)], ref.at[half(r, c)], ss.at[r], rs.at[r], sib).wait_send()
    rdma(g.sums, g.sumA, g.sm_s.at[0], g.sm_r.at[0], sib).wait_send()
    rdma(g.sumB, g.sumC, g.sm_s.at[1], g.sm_r.at[1], yp).wait_send()
    for t in range(3):
        rdma(g.sumD.at[z], g.sumD.at[z], g.sm_s.at[2 + t], g.sm_r.at[2 + z], zm[t]).wait_send()


def fast_device(
    tokens, cotangent, lengths, coords, keep_mask, ln_gains, ln_shifts, out_bias,
    w_qkv, qv_bias, w_out, w_up, up_bias, w_down,
):
    inputs = [
        ("in_tok", tokens.reshape(384, 768)),
        ("in_cot", cotangent.reshape(384, 768)),
        ("in_len", lengths),
        ("in_crd", jnp.transpose(coords, (1, 0, 2))),
        ("in_keep", keep_mask),
        ("in_lng", ln_gains),
        ("in_lns", ln_shifts),
        ("in_ob", out_bias),
        ("in_w3", jnp.transpose(w_qkv, (1, 0, 2))),
        ("in_qvb", qv_bias),
        ("in_wo", w_out),
        ("in_wu", w_up),
        ("in_upb", up_bias),
        ("in_wd", jnp.transpose(w_down)),
    ]
    outputs = [
        ("out_tok", (384, 768), BF),
        ("out_gtok", (384, 768), BF),
        ("out_gain", (2, 96), F32),
        ("out_shift", (2, 96), F32),
        ("out_obias", (2, 96), F32),
        ("out_gqkv", (3, 96, 192), F32),
        ("out_qvb", (2, 192), F32),
        ("out_gout", (192, 96), F32),
        ("out_gup", (96, 768), F32),
        ("out_upb", (1, 768), F32),
        ("out_gdown", (96, 768), F32),
    ]
    vm = [
        ("wq", (8, 96, 768), BF),
        ("wo", (768, 192), BF),
        ("sml", (8, 16, 128), BF),
        ("tmp", (16, 128), F32),
        ("nrm", (384, 768), BF),
        ("gd", (384, 768), F32),
        ("acc0", (432, 128), F32),
        ("acc1", (144, 128), F32),
        ("acc2", (576, 128), F32),
        ("acc3", (576, 128), F32),
        ("wu", (8, 96, 768), BF),
        ("wd", (8, 96, 768), BF),
        ("inp", (384, 768), F32),
        ("n1", (384, 768), F32),
        ("rstd1", (384, 1), F32),
        ("cotT", (768, 384), BF),
        ("nrmT", (768, 384), BF),
        ("par", (16, 768), F32),
        ("sums", (8, 768), F32),
        ("sumA", (8, 768), F32),
        ("sumB", (8, 768), F32),
        ("sumC", (8, 768), F32),
        ("sumD", (4, 8, 768), F32),
        ("cut", (8, 8, 96), F32),
        ("snA", (4, 3, 144, 128), BF),
        ("rcA", (4, 3, 144, 128), BF),
        ("sbA", (4, 3, 96, 128), BF),
        ("QT", (3, 64, 512), BF),
        ("KT", (3, 64, 1024), BF),
        ("VT", (3, 64, 1024), BF),
        ("P", (3, 1024, 512), BF),
        ("O", (3, 48, 512), F32),
        ("inv", (3, 8, 512), F32),
        ("snO", (4, 3, 48, 128), BF),
        ("rcO", (4, 3, 48, 128), BF),
        ("snD", (4, 3, 48, 128), BF),
        ("rcD", (4, 3, 48, 128), BF),
        ("snG", (4, 3, 144, 128), BF),
        ("rcG", (4, 3, 144, 128), BF),
        ("snX", (3, 96, 512), F32),
        ("rcX", (3, 96, 512), F32),
        ("kvX", (3, 96, 512), F32),
        ("attT", (192, 384), BF),
        ("gpT", (576, 384), BF),
        ("ps", (4, 3, 128, 768), BF),
        ("psA", (4, 3, 64, 768), BF),
        ("psH", (4, 3, 64, 768), BF),
        ("psB", (4, 3, 64, 768), BF),
        ("mid", (3, 64, 768), F32),
        ("n2", (3, 64, 768), F32),
        ("rstd2", (3, 64, 1), F32),
        ("gm", (3, 64, 768), F32),
        ("ntk", (384, 768), BF),
        ("ntT", (768, 384), BF),
        ("act", (384, 768), BF),
        ("gp", (384, 768), BF),
        ("gb", (384, 768), BF),
        ("gbT", (768, 384), BF),
    ]
    for p, width in enumerate((576, 192, 768, 768)):
        for kind in ("l1s", "l1r", "l2s", "l2r"):
            vm.append((f"{kind}{p}", (4, 96 * width // 128, 128), BF))
    sems = [
        ("qa_s", (4, 3)), ("qa_r", (4, 3)),
        ("sa_s", (4, 3)), ("sa_r", (4, 3)),
        ("o_s", (4, 3)), ("o_r", (4, 3)),
        ("d_s", (4, 3)), ("d_r", (4, 3)),
        ("g_s", (4, 3)), ("g_r", (4, 3)),
        ("x_s", (3,)), ("x_r", (3,)),
        ("nt_s", (3,)), ("nt_r", (3,)),
        ("gb_s", (3,)), ("gb_r", (3,)),
        ("ot_s", (3,)), ("ot_r", (3,)),
        ("gt_s", (3,)), ("gt_r", (3,)),
        ("sm_s", (8,)), ("sm_r", (8,)),
        ("sml_s", (7,)), ("sml_r", (8,)),
    ]
    for name, shape in (
        ("ag_s", (8,)), ("ag_r", (8,)), ("ps_s", (3, 2)), ("ps_r", (3, 2)),
        ("l1_s", (4,)), ("l1_r", (4,)), ("l2_s", (4,)), ("l2_r", (4,)),
    ):
        sems += [(f"{name}{q}", shape) for q in range(4)]
    names = [n for n, _ in inputs] + [o[0] for o in outputs] + [v[0] for v in vm] + [n for n, _ in sems]
    vmem = pl.BlockSpec(memory_space=pltpu.VMEM)
    out = pl.pallas_call(
        partial(layer_kernel, names=names),
        out_shape=[jax.ShapeDtypeStruct(shape, dtype) for _, shape, dtype in outputs],
        in_specs=[
            pl.BlockSpec(memory_space=pltpu.SMEM) if n == "in_len" else vmem for n, _ in inputs
        ],
        out_specs=[vmem] * len(outputs),
        scratch_shapes=[pltpu.VMEM(shape, dtype) for _, shape, dtype in vm]
        + [pltpu.SemaphoreType.DMA(shape) for _, shape in sems],
        compiler_params=pltpu.CompilerParams(
            collective_id=0, has_side_effects=True, vmem_limit_bytes=60 * 1024 * 1024
        ),
    )(*[v for _, v in inputs])
    shapes = [
        jax.ShapeDtypeStruct((768,) if o.shape == (1, 768) else o.shape, o.dtype) for o in out
    ]

    def hand_over(*refs):
        for n in range(len(shapes)):
            refs[len(shapes) + n][...] = refs[n][...].reshape(shapes[n].shape)

    out = pl.pallas_call(
        hand_over,
        out_shape=shapes,
        in_specs=[vmem] * len(shapes),
        out_specs=[vmem] * len(shapes),
    )(*out)
    out_tok, out_gtok, gain, shift, obias, gqkv, qvb, gout, gup, upb, gdown = out
    return (
        out_tok.reshape(3, 128, 768),
        out_gtok.reshape(3, 128, 768),
        gain,
        shift,
        obias,
        jnp.transpose(gqkv, (1, 0, 2)),
        qvb,
        gout,
        gup,
        upb,
        jnp.transpose(gdown),
    )


def solution(mesh):
    placed = (
        P(None, "seq", None),
        P(None, "seq", None),
        P(),
        P(None, None, "seq"),
        P(None, "seq"),
        P(None, "seq"),
        P(None, "seq"),
        P(None, "seq"),
        P("seq", None, "head"),
        P(None, "head"),
        P("head", "seq"),
        P("seq", "head"),
        P("head"),
        P("head", "seq"),
    )
    layout = (mesh.shape["seq"], mesh.shape["head"])

    def step(tokens, *others):
        one_kernel = layout == (8, 4) and tokens.shape == (3, 1024, 768)
        return over(fast_device if one_kernel else per_device)(tokens, *others)

    def over(device):
        return jax.shard_map(
        device,
        mesh=mesh,
        in_specs=placed,
        out_specs=(
            P(None, "seq", None),
            P(None, "seq", None),
            P(None, "seq"),
            P(None, "seq"),
            P(None, "seq"),
            P("seq", None, "head"),
            P(None, "head"),
            P("head", "seq"),
            P("seq", "head"),
            P("head"),
            P("head", "seq"),
        ),
        check_vma=False,
    )

    return step
```

```python
from functools import partial
import math

import jax
import jax.numpy as jnp
import ml_dtypes
import numpy as np
from jax import lax
from jax.experimental import pallas as pl
from jax.experimental.pallas import tpu as pltpu
from jax.sharding import PartitionSpec as P

HDIM = 48
UNIT = 1024
BRANCHES = 5


EPSILON = 1e-05


def position_table(grid_rows, width):
    quarter = width // 4
    frequency = jnp.exp(-jnp.log(10000.0) * jnp.arange(quarter, dtype=jnp.float32) / quarter)
    along_row = grid_rows[0].astype(jnp.float32)[:, None] * frequency[None, :]
    along_col = grid_rows[1].astype(jnp.float32)[:, None] * frequency[None, :]
    return jnp.concatenate(
        [jnp.sin(along_row), jnp.cos(along_row), jnp.sin(along_col), jnp.cos(along_col)], axis=1
    )


def layer_norm(values, gain_vec, shift_vec):
    centre = values - jnp.mean(values, axis=-1, keepdims=True)
    spread = jnp.mean(centre * centre, axis=-1, keepdims=True)
    return centre * lax.rsqrt(spread + EPSILON) * gain_vec + shift_vec


def slide_of(positions, bounds):
    return jnp.sum((positions[:, None] >= bounds[None, :]).astype(jnp.int32), axis=1)


def pair_weight(query_pos, key_pos, key_keep, head_ids, bounds, seg_unit):
    same_slide = slide_of(query_pos, bounds)[:, None] == slide_of(key_pos, bounds)[None, :]
    visible = same_slide & ((key_keep[None, :] > 0) | (query_pos[:, None] == key_pos[None, :]))
    counted = jnp.zeros((head_ids.shape[0], query_pos.shape[0], key_pos.shape[0]), jnp.float32)
    for branch in range(BRANCHES):
        stride = 2**branch
        span = seg_unit * stride
        same_seg = query_pos[:, None] // span == key_pos[None, :] // span
        query_on = query_pos[None, :] % stride == head_ids[:, None] % stride
        key_on = key_pos[None, :] % stride == head_ids[:, None] % stride
        counted = counted + (same_seg[None] & query_on[:, :, None] & key_on[:, None, :]).astype(
            jnp.float32
        )
    return counted * visible[None].astype(jnp.float32)


def head_total(partial_sum):
    return lax.psum(partial_sum.astype(jnp.bfloat16), "head").astype(jnp.float32)


def per_device(
    tokens,
    cotangent,
    lengths,
    coords,
    keep_mask,
    ln_gains,
    ln_shifts,
    out_bias,
    w_qkv,
    qv_bias,
    w_out,
    w_up,
    up_bias,
    w_down,
):
    micro_count, tok_local, width = tokens.shape
    row_len = tok_local * lax.axis_size("seq")
    seg_unit = UNIT
    block_count = row_len // seg_unit
    heads_local = w_qkv.shape[2] // HDIM
    local_width = heads_local * HDIM
    inv_root = 1.0 / math.sqrt(HDIM)
    head_ids = lax.axis_index("head") * heads_local + jnp.arange(heads_local, dtype=jnp.int32)
    own_pos = lax.axis_index("seq") * tok_local + jnp.arange(tok_local, dtype=jnp.int32)
    block_starts = jnp.arange(block_count, dtype=jnp.int32) * seg_unit
    bias_qv = qv_bias.astype(jnp.float32)
    bias_up = up_bias.astype(jnp.float32)
    sum_qkv = jnp.zeros((width, 3, local_width), jnp.float32)
    sum_out = jnp.zeros((local_width, width), jnp.float32)
    sum_up = jnp.zeros((width, w_up.shape[1]), jnp.float32)
    sum_down = jnp.zeros((w_down.shape[0], width), jnp.float32)
    sum_gain = jnp.zeros((2, width), jnp.float32)
    sum_shift = jnp.zeros((2, width), jnp.float32)
    sum_obias = jnp.zeros((2, width), jnp.float32)
    sum_qvb = jnp.zeros((2, local_width), jnp.float32)
    sum_upb = jnp.zeros((w_up.shape[1],), jnp.float32)
    out_rows = []
    grad_rows = []
    for micro_id in range(micro_count):
        full_qkv, full_out, full_up, full_down, gain_rows, shift_rows, obias_rows = (
            lax.all_gather(w_qkv, "seq", axis=0, tiled=True),
            lax.all_gather(w_out, "seq", axis=1, tiled=True),
            lax.all_gather(w_up, "seq", axis=0, tiled=True),
            lax.all_gather(w_down, "seq", axis=1, tiled=True),
            lax.all_gather(ln_gains, "seq", axis=1, tiled=True),
            lax.all_gather(ln_shifts, "seq", axis=1, tiled=True),
            lax.all_gather(out_bias, "seq", axis=1, tiled=True),
        )
        gain_rows = gain_rows.astype(jnp.float32)
        shift_rows = shift_rows.astype(jnp.float32)
        obias_rows = obias_rows.astype(jnp.float32)
        bounds = jnp.cumsum(lengths[micro_id])[:-1]
        inputs = tokens[micro_id].astype(jnp.float32) + position_table(coords[:, micro_id], width)
        normed = layer_norm(inputs, gain_rows[0], shift_rows[0]).astype(jnp.bfloat16)
        projected = jnp.einsum("td,dcf->tcf", normed, full_qkv, preferred_element_type=jnp.float32)
        queries = (
            (projected[:, 0] + bias_qv[0])
            .astype(jnp.bfloat16)
            .reshape(tok_local, heads_local, HDIM)
        )
        key_rows = projected[:, 1].astype(jnp.bfloat16).reshape(tok_local, heads_local, HDIM)
        value_rows = (
            (projected[:, 2] + bias_qv[1])
            .astype(jnp.bfloat16)
            .reshape(tok_local, heads_local, HDIM)
        )
        keep_local = keep_mask[micro_id].astype(jnp.bfloat16)
        key_all, value_all, keep_all = (
            lax.all_gather(key_rows, "seq", axis=0, tiled=True),
            lax.all_gather(value_rows, "seq", axis=0, tiled=True),
            lax.all_gather(keep_local, "seq", axis=0, tiled=True),
        )

        def key_block(key_src, value_src, keep_src, offset):
            key_blk = lax.dynamic_slice_in_dim(key_src, offset, seg_unit, 0)
            value_blk = lax.dynamic_slice_in_dim(value_src, offset, seg_unit, 0)
            keep_blk = lax.dynamic_slice_in_dim(keep_src, offset, seg_unit, 0)
            key_pos = offset + jnp.arange(seg_unit, dtype=jnp.int32)
            scores = (
                jnp.einsum("thd,khd->htk", queries, key_blk, preferred_element_type=jnp.float32)
                * inv_root
            )
            weight = pair_weight(own_pos, key_pos, keep_blk, head_ids, bounds, seg_unit)
            return (key_blk, value_blk, scores, weight)

        def stats_step(running, offset):
            row_peak, row_total = running
            _, _, scores, weight = key_block(key_all, value_all, keep_all, offset)
            live = weight > 0
            new_peak = jnp.maximum(row_peak, jnp.max(jnp.where(live, scores, -1e30), axis=2))
            fresh = jnp.sum(
                jnp.where(live, weight * jnp.exp(scores - new_peak[:, :, None]), 0.0), axis=2
            )
            return ((new_peak, row_total * jnp.exp(row_peak - new_peak) + fresh), None)

        start_stats = (
            jnp.full((heads_local, tok_local), -1e30, jnp.float32),
            jnp.zeros((heads_local, tok_local), jnp.float32),
        )
        (row_peak, row_total), _ = lax.scan(stats_step, start_stats, block_starts)
        log_total = row_peak + jnp.log(row_total)

        def value_step(running, offset):
            _, value_blk, scores, weight = key_block(key_all, value_all, keep_all, offset)
            prob_low = (weight * jnp.exp(scores - log_total[:, :, None])).astype(jnp.bfloat16)
            return (
                running
                + jnp.einsum(
                    "htk,khd->thd", prob_low, value_blk, preferred_element_type=jnp.float32
                ),
                None,
            )

        attended, _ = lax.scan(
            value_step, jnp.zeros((tok_local, heads_local, HDIM), jnp.float32), block_starts
        )
        attended_low = attended.astype(jnp.bfloat16).reshape(tok_local, local_width)
        middle = (
            inputs
            + head_total(jnp.dot(attended_low, full_out, preferred_element_type=jnp.float32))
            + obias_rows[0]
        )
        normed_two = layer_norm(middle, gain_rows[1], shift_rows[1]).astype(jnp.bfloat16)
        hidden_pre = jnp.dot(normed_two, full_up, preferred_element_type=jnp.float32) + bias_up
        activated = jax.nn.gelu(hidden_pre, approximate=False).astype(jnp.bfloat16)
        result = (
            middle
            + head_total(jnp.dot(activated, full_down, preferred_element_type=jnp.float32))
            + obias_rows[1]
        )
        out_rows.append(result.astype(jnp.bfloat16))
        grad_out_low = cotangent[micro_id]
        grad_out_f32 = grad_out_low.astype(jnp.float32)
        sum_down = sum_down + jnp.einsum(
            "tf,td->fd", activated, grad_out_low, preferred_element_type=jnp.float32
        )
        grad_act = jnp.einsum(
            "td,fd->tf", grad_out_low, full_down, preferred_element_type=jnp.float32
        )
        _, gelu_back = jax.vjp(partial(jax.nn.gelu, approximate=False), hidden_pre)
        grad_pre_low = gelu_back(grad_act)[0].astype(jnp.bfloat16)
        sum_upb = sum_upb + jnp.sum(grad_pre_low.astype(jnp.float32), axis=0)
        sum_up = sum_up + jnp.einsum(
            "td,tf->df", normed_two, grad_pre_low, preferred_element_type=jnp.float32
        )
        grad_normed_two = head_total(
            jnp.einsum("tf,df->td", grad_pre_low, full_up, preferred_element_type=jnp.float32)
        )
        _, norm_back_two = jax.vjp(layer_norm, middle, gain_rows[1], shift_rows[1])
        grad_from_two, grad_gain_two, grad_shift_two = norm_back_two(grad_normed_two)
        grad_middle = grad_out_f32 + grad_from_two
        grad_branch_low = grad_middle.astype(jnp.bfloat16)
        sum_obias = sum_obias + jnp.stack(
            [jnp.sum(grad_branch_low.astype(jnp.float32), axis=0), jnp.sum(grad_out_f32, axis=0)]
        )
        sum_out = sum_out + jnp.einsum(
            "tf,td->fd", attended_low, grad_branch_low, preferred_element_type=jnp.float32
        )
        grad_attn_low = (
            jnp.einsum("td,fd->tf", grad_branch_low, full_out, preferred_element_type=jnp.float32)
            .astype(jnp.bfloat16)
            .reshape(tok_local, heads_local, HDIM)
        )
        row_delta = jnp.einsum("thd,thd->ht", grad_attn_low.astype(jnp.float32), attended)
        back_keys, back_values, back_keep = (
            lax.all_gather(key_rows, "seq", axis=0, tiled=True),
            lax.all_gather(value_rows, "seq", axis=0, tiled=True),
            lax.all_gather(keep_local, "seq", axis=0, tiled=True),
        )

        def key_side_step(running, offset):
            key_blk, value_blk, scores, weight = key_block(
                back_keys, back_values, back_keep, offset
            )
            prob_f32 = weight * jnp.exp(scores - log_total[:, :, None])
            grad_prob = jnp.einsum(
                "thd,khd->htk", grad_attn_low, value_blk, preferred_element_type=jnp.float32
            )
            grad_scores = (prob_f32 * (grad_prob - row_delta[:, :, None])).astype(jnp.bfloat16)
            running = running + jnp.einsum(
                "htk,khd->thd", grad_scores, key_blk, preferred_element_type=jnp.float32
            )
            prob_low = prob_f32.astype(jnp.bfloat16)
            key_term = (
                jnp.einsum("htk,thd->khd", grad_scores, queries, preferred_element_type=jnp.float32)
                * inv_root
            )
            value_term = jnp.einsum(
                "htk,thd->khd", prob_low, grad_attn_low, preferred_element_type=jnp.float32
            )
            return (
                running,
                jnp.concatenate(
                    [
                        key_term.reshape(seg_unit, local_width),
                        value_term.reshape(seg_unit, local_width),
                    ],
                    axis=1,
                ),
            )

        query_sum, terms = lax.scan(
            key_side_step, jnp.zeros((tok_local, heads_local, HDIM), jnp.float32), block_starts
        )
        owned = lax.psum_scatter(
            terms.reshape(row_len, 2 * local_width), "seq", scatter_dimension=0, tiled=True
        )
        grad_queries = query_sum * inv_root
        grad_keys = owned[:, :local_width].reshape(tok_local, heads_local, HDIM)
        grad_values = owned[:, local_width:].reshape(tok_local, heads_local, HDIM)
        grad_q_low = grad_queries.astype(jnp.bfloat16).reshape(tok_local, local_width)
        grad_k_low = grad_keys.astype(jnp.bfloat16).reshape(tok_local, local_width)
        grad_v_low = grad_values.astype(jnp.bfloat16).reshape(tok_local, local_width)
        sum_qvb = sum_qvb + jnp.stack(
            [
                jnp.sum(grad_q_low.astype(jnp.float32), axis=0),
                jnp.sum(grad_v_low.astype(jnp.float32), axis=0),
            ]
        )
        grad_proj = jnp.stack([grad_q_low, grad_k_low, grad_v_low], axis=1)
        sum_qkv = sum_qkv + jnp.einsum(
            "td,tcf->dcf", normed, grad_proj, preferred_element_type=jnp.float32
        )
        grad_normed = head_total(
            jnp.einsum("tcf,dcf->td", grad_proj, full_qkv, preferred_element_type=jnp.float32)
        )
        _, norm_back_one = jax.vjp(layer_norm, inputs, gain_rows[0], shift_rows[0])
        grad_from_one, grad_gain_one, grad_shift_one = norm_back_one(grad_normed)
        grad_rows.append((grad_middle + grad_from_one).astype(jnp.bfloat16))
        sum_gain = sum_gain + jnp.stack([grad_gain_one, grad_gain_two])
        sum_shift = sum_shift + jnp.stack([grad_shift_one, grad_shift_two])
    grad_qkv, grad_out, grad_up, grad_down, grad_gain, grad_shift, grad_obias = (
        lax.psum_scatter(sum_qkv, "seq", scatter_dimension=0, tiled=True),
        lax.psum_scatter(sum_out, "seq", scatter_dimension=1, tiled=True),
        lax.psum_scatter(sum_up, "seq", scatter_dimension=0, tiled=True),
        lax.psum_scatter(sum_down, "seq", scatter_dimension=1, tiled=True),
        lax.psum_scatter(sum_gain, "seq", scatter_dimension=1, tiled=True),
        lax.psum_scatter(sum_shift, "seq", scatter_dimension=1, tiled=True),
        lax.psum_scatter(sum_obias, "seq", scatter_dimension=1, tiled=True),
    )
    grad_qvb, grad_upb = lax.psum((sum_qvb, sum_upb), "seq")
    return (
        jnp.stack(out_rows),
        jnp.stack(grad_rows),
        grad_gain,
        grad_shift,
        grad_obias,
        grad_qkv,
        grad_qvb,
        grad_out,
        grad_up,
        grad_upb,
        grad_down,
    )


NEG = 1792.0
ROOT = 1.0 / math.sqrt(HDIM)
BF = jnp.bfloat16
F32 = jnp.float32
MESH = pl.DeviceIdType.MESH
LEVELS = [math.sqrt(HDIM) * math.log((b + 1) / b) for b in range(1, BRANCHES)]
LEVEL_HIGH = [float(np.asarray(v, ml_dtypes.bfloat16)) for v in LEVELS]
LEVEL_LOW = [v - w for v, w in zip(LEVELS, LEVEL_HIGH)]


def nn(a, b):
    return lax.dot_general(a, b, (((1,), (0,)), ((), ())), preferred_element_type=F32)


def nt(a, b):
    return lax.dot_general(a, b, (((1,), (1,)), ((), ())), preferred_element_type=F32)


def tn(a, b):
    return lax.dot_general(a, b, (((0,), (0,)), ((), ())), preferred_element_type=F32)


def tt(a, b):
    return lax.dot_general(a, b, (((0,), (1,)), ((), ())), preferred_element_type=F32)


def four(index, values):
    return jnp.where(
        index == 0,
        values[0],
        jnp.where(index == 1, values[1], jnp.where(index == 2, values[2], values[3])),
    )


def pair_features(pos, slide, keep, head, for_keys):
    shape = (16, pos.shape[1])
    row = lax.broadcasted_iota(jnp.int32, shape, 0)
    pos = jnp.broadcast_to(pos, shape)
    slide = jnp.broadcast_to(slide, shape)
    level = jnp.where(row >= 8, row - 8, row - 4)
    on = jnp.bitwise_and(pos - head, four(level, [1, 3, 7, 15])) == 0
    on = on & (row < 12)
    if for_keys:
        keep = jnp.broadcast_to(keep, shape)
        size = jnp.where(row < 8, four(level, LEVEL_HIGH), four(level, LEVEL_LOW))
        other = jnp.where(slide != row, -NEG, 0.0)
        padding = jnp.where(keep > 0.0, 0.0, -NEG)
    else:
        size = jnp.ones(shape, F32)
        other = jnp.where(slide == row, 1.0, 0.0)
        padding = jnp.ones(shape, F32)
    value = jnp.where(row < 3, other, jnp.where(row == 3, padding, jnp.where(on, size, 0.0)))
    return value.astype(BF)


def layer_kernel(*refs, names):
    r_ = dict(zip(names, refs))

    class N:
        pass

    g = N()
    for k, v in r_.items():
        setattr(g, k, v)
    s = lax.axis_index("seq")
    h = lax.axis_index("head")
    z, y = lax.div(s, 2), lax.rem(s, 2)
    x, c = lax.div(h, 2), lax.rem(h, 2)
    a, j = lax.div(s, 4), lax.rem(s, 4)
    sib = (s, h + 1 - 2 * c)
    xp = (s, lax.rem(h + 2, 4))
    yp = (s + 1 - 2 * y, h)
    top = lax.div(z, 2)
    zs = [z + 1 - 2 * lax.rem(z, 2), 2 - top, 3 - 3 * top]
    zm = [(2 * q + y, h) for q in zs]
    zy = [(2 * q + 1 - y, h) for q in zs]
    qs = zs + [z]
    inner = (z == 1) | (z == 2)
    outer = jnp.logical_not(inner)
    part = [(4 * c + i, 2 * x + a) for i in range(4)]
    own = [(a == c) & (j == i) for i in range(4)]
    is_own = jnp.where(a == c, 1, 0)
    head = 8 * x + s
    R = 3
    T = 128

    def rdma(src, dst, ss, rs, dev):
        return pltpu.make_async_remote_copy(
            src_ref=src, dst_ref=dst, send_sem=ss, recv_sem=rs, device_id=dev, device_id_type=MESH
        )

    def not_own(i):
        return jnp.logical_not(own[i])

    def lanes(r, n=128):
        return pl.ds(pl.multiple_of(n * r, n), n)

    def rows(r, n=128):
        return pl.ds(pl.multiple_of(n * r, n), n)

    def half(r, who):
        return pl.ds(pl.multiple_of(T * r + 64 * who, 64), 64)

    bar = pltpu.get_barrier_semaphore()
    for dev in [sib, xp, yp] + zm + zy:
        pl.semaphore_signal(bar, inc=1, device_id=dev, device_id_type=MESH)
    for i in range(4):

        @pl.when(not_own(i))
        def _():
            pl.semaphore_signal(bar, inc=1, device_id=part[i], device_id_type=MESH)

    def piece(p, k):
        if p < 2:
            return g.wq.at[k, pl.ds(48 * p, 48)]
        return (g.wu if p == 2 else g.wd).at[k]

    def four_of(name):
        return [r_[f"{name}{q}"] for q in range(4)]

    AGS, AGR, PSS, PSR = four_of("ag_s"), four_of("ag_r"), four_of("ps_s"), four_of("ps_r")
    L1SS, L1RS, L2SS, L2RS = four_of("l1_s"), four_of("l1_r"), four_of("l2_s"), four_of("l2_r")

    def ag_y(p):
        rdma(piece(p, s), piece(p, s), AGS[p].at[0], AGR[p].at[s], yp).start()

    def ag_z(p):
        @pl.when(outer)
        def _():
            for t in (1, 0):
                rdma(piece(p, s), piece(p, s), AGS[p].at[1 + t], AGR[p].at[s], zm[t]).start()

        @pl.when(inner)
        def _():
            for t in range(3):
                rdma(piece(p, s), piece(p, s), AGS[p].at[1 + t], AGR[p].at[s], zm[t]).start()

    def ag_forward(p, t):
        k = zm[t][0]
        w = piece(p, k)
        rdma(w, w, AGS[p].at[4 + t], AGR[p].at[k], zm[t]).wait_recv()
        if t == 2:

            @pl.when(inner)
            def _():
                rdma(w, w, AGS[p].at[7], AGR[p].at[k], zm[0]).start()

        rdma(w, w, AGS[p].at[4 + t], AGR[p].at[k], yp).start()

    def ag_wait(p):
        for q in qs:
            w = piece(p, 2 * q + 1 - y)
            rdma(w, w, AGS[p].at[0], AGR[p].at[2 * q + 1 - y], yp).wait_recv()

    def ag_drain(p):
        w = piece(p, s)
        for t in (0, 1, 2, 4, 5, 6):
            rdma(w, w, AGS[p].at[t], AGR[p].at[s], yp).wait_send()

        @pl.when(inner)
        def _():
            for t in (3, 7):
                rdma(w, w, AGS[p].at[t], AGR[p].at[s], yp).wait_send()

    g.wq[s] = jnp.concatenate(
        [g.in_w3[0], g.in_w3[1], g.in_w3[2], jnp.transpose(g.in_wo[...])], axis=1
    )
    g.tmp[...] = jnp.zeros_like(g.tmp)
    g.tmp[0:2, 0:96] = g.in_lng[...].astype(F32)
    g.tmp[2:4, 0:96] = g.in_lns[...].astype(F32)
    g.tmp[4:6, 0:96] = g.in_ob[...].astype(F32)
    g.tmp[6:9, :] = g.in_keep[...].astype(F32)
    g.sml[s] = g.tmp[...].astype(BF)
    g.wu[s] = g.in_wu[...]
    g.wd[s] = g.in_wd[...]
    pl.semaphore_wait(bar, 13 - is_own)
    others = [yp] + zm + zy
    for t, dev in enumerate(others):
        rdma(g.sml.at[s], g.sml.at[s], g.sml_s.at[t], g.sml_r.at[s], dev).start()
    for p in range(2):
        ag_y(p)
        ag_z(p)
    ag_y(2)
    ag_z(2)
    ag_y(3)

    lane = lax.broadcasted_iota(jnp.int32, (1, 768), 1)
    freq = jnp.exp(
        -math.log(10000.0) * lax.rem(lane, 192).astype(F32) / 192.0
    )
    for r in range(R):
        col = jnp.transpose(
            jnp.concatenate([g.in_crd[r].astype(F32), jnp.zeros((6, 128), F32)], axis=0)
        )
        pieces = []
        for t in range(6):
            f = freq[:, 128 * t : 128 * t + 128]
            ang = col[:, (0 if t < 3 else 1) : (1 if t < 3 else 2)] * f
            if t % 3 == 0:
                pieces.append(jnp.sin(ang))
            elif t % 3 == 2:
                pieces.append(jnp.cos(ang))
            else:
                low_half = lax.broadcasted_iota(jnp.int32, (T, 128), 1) < 64
                pieces.append(jnp.where(low_half, jnp.sin(ang), jnp.cos(ang)))
        v = g.in_tok[rows(r), :].astype(F32) + jnp.concatenate(pieces, axis=1)
        g.inp[rows(r), :] = v
        v = v - jnp.mean(v, axis=1, keepdims=True)
        rstd = lax.rsqrt(jnp.mean(v * v, axis=1, keepdims=True) + EPSILON)
        g.n1[rows(r), :] = v * rstd
        g.rstd1[rows(r), :] = rstd
        g.cotT[:, 128 * r : 128 * r + 128] = jnp.transpose(g.in_cot[rows(r), :])
    g.sums[...] = jnp.zeros_like(g.sums)

    for t, dev in enumerate(others):
        k = dev[0]
        rdma(g.sml.at[k], g.sml.at[k], g.sml_s.at[t], g.sml_r.at[k], dev).wait_recv()
    par = jnp.concatenate([g.sml[k].astype(F32)[:, 0:96] for k in range(8)], axis=1)
    g.par[...] = par
    g1, s1, ob0, ob1 = par[1:2], par[3:4], par[4:5], par[5:6]
    g0 = par[0:1]
    qvb = g.in_qvb[...].astype(F32)
    qkv_bias = jnp.concatenate([qvb[0:1], jnp.zeros((1, 192), F32), qvb[1:2]], axis=1)
    for r in range(R):
        nr = (g.n1[rows(r), :] * g0 + par[2:3]).astype(BF)
        g.nrm[rows(r), :] = nr
        g.nrmT[:, 128 * r : 128 * r + 128] = jnp.transpose(nr)
    ag_forward(0, 0)
    ag_forward(1, 0)
    ag_forward(0, 1)
    ag_forward(1, 1)
    ag_forward(0, 2)
    ag_forward(1, 2)
    ag_forward(2, 0)
    ag_wait(0)
    ag_wait(1)

    def send_part(i, r, src, dst, ss, rs):
        @pl.when(not_own(i))
        def _():
            rdma(src.at[i, r], dst.at[j, r], ss.at[i, r], rs.at[j, r], part[i]).start()

        @pl.when(own[i])
        def _():
            dst[i, r] = src[i, r]

    def wait_part(i, r, dst, ss, rs):
        @pl.when(not_own(i))
        def _():
            rdma(dst.at[i, r], dst.at[i, r], ss.at[i, r], rs.at[i, r], part[i]).wait_recv()

    def drain_part(i, r, src, ss, rs):
        @pl.when(not_own(i))
        def _():
            rdma(src.at[i, r], src.at[i, r], ss.at[i, r], rs.at[i, r], part[i]).wait_send()

    for r in range(R):
        proj = nn(g.nrm[rows(r), :], g.wq[:, :, 0:576].reshape(768, 576)) + qkv_bias
        projT = jnp.transpose(proj).astype(BF)
        for i in range(4):
            for t in range(3):
                g.snA[i, r, 48 * t : 48 * t + 48, :] = projT[192 * t + 48 * i : 192 * t + 48 * i + 48]
            send_part(i, r, g.snA, g.rcA, g.qa_s, g.qa_r)
        if r == 1:
            ag_forward(2, 1)
    ag_z(3)

    g.wo[...] = g.wq[:, :, 576:768].reshape(768, 192)

    def slide_of_row(r, pos):
        b0 = g.in_len[r, 0]
        b1 = b0 + g.in_len[r, 1]
        return jnp.where(pos >= b0, 1, 0) + jnp.where(pos >= b1, 1, 0)

    ones_rows = jnp.where(lax.broadcasted_iota(jnp.int32, (16, 1024), 0) == 0, 1.0, 0.0).astype(BF)

    def attn_fwd(r):
        for i in range(4):
            wait_part(i, r, g.rcA, g.qa_s, g.qa_r)
            rdma(
                g.rcA.at[i, r, pl.ds(48, 96)], g.sbA.at[i, r], g.sa_s.at[i, r], g.sa_r.at[i, r], sib
            ).start()
        iota = lax.broadcasted_iota(jnp.int32, (1, 512), 1)
        pos_own = 512 * c + iota
        pos_sib = 512 * (1 - c) + iota
        keep_own = jnp.concatenate(
            [g.sml[4 * c + i].astype(F32)[6 + r : 7 + r] for i in range(4)], axis=1
        )
        keep_sib = jnp.concatenate(
            [g.sml[4 * (1 - c) + i].astype(F32)[6 + r : 7 + r] for i in range(4)], axis=1
        )
        pos = jnp.concatenate([pos_own, pos_sib], axis=1)
        kf = pair_features(
            pos, slide_of_row(r, pos), jnp.concatenate([keep_own, keep_sib], axis=1), head, True
        )
        qf = pair_features(pos_own, slide_of_row(r, pos_own), None, head, False)
        g.QT[r, 0:48, :] = jnp.concatenate([g.rcA[i, r, 0:48, :] for i in range(4)], axis=1)
        g.QT[r, 48:64, :] = qf
        g.KT[r, 48:64, :] = kf
        g.VT[r, 48:64, :] = ones_rows
        for i in range(4):
            g.KT[r, 0:48, 128 * i : 128 * i + 128] = g.rcA[i, r, 48:96, :]
            g.VT[r, 0:48, 128 * i : 128 * i + 128] = g.rcA[i, r, 96:144, :]
        for i in range(4):
            rdma(g.sbA.at[i, r], g.sbA.at[i, r], g.sa_s.at[i, r], g.sa_r.at[i, r], sib).wait_recv()
            g.KT[r, 0:48, 512 + 128 * i : 640 + 128 * i] = g.sbA[i, r, 0:48, :]
            g.VT[r, 0:48, 512 + 128 * i : 640 + 128 * i] = g.sbA[i, r, 48:96, :]
        eye = lax.broadcasted_iota(jnp.int32, (256, 256), 0) == lax.broadcasted_iota(
            jnp.int32, (256, 256), 1
        )
        for qc in range(2):
            q0 = 256 * qc
            sc = tn(g.KT[r], g.QT[r, :, q0 : q0 + 256])
            lift = jnp.where(eye, NEG * (1.0 - keep_own[:, q0 : q0 + 256]), 0.0)
            blocks = [sc[256 * t : 256 * t + 256] for t in range(4)]
            blocks[qc] = blocks[qc] + lift
            sc = jnp.concatenate(blocks, axis=0)
            peak = jnp.max(sc, axis=0, keepdims=True)
            pb = jnp.exp((sc - peak) * ROOT).astype(BF)
            g.P[r, :, q0 : q0 + 256] = pb
            o = nn(g.VT[r], pb)
            inv = 1.0 / o[48:49]
            o = o[0:48] * inv
            g.O[r, :, q0 : q0 + 256] = o
            g.inv[r, :, q0 : q0 + 256] = jnp.broadcast_to(inv, (8, 256))
            for u in range(2):
                i = 2 * qc + u
                g.snO[i, r] = o[:, 128 * u : 128 * u + 128].astype(BF)
                send_part(i, r, g.snO, g.rcO, g.o_s, g.o_r)

    attn_fwd(0)
    ag_forward(2, 2)
    attn_fwd(1)
    ag_forward(3, 0)
    attn_fwd(2)

    def ps_start(kind, r, part_sum):
        g.ps[kind, r] = part_sum.astype(BF)
        rdma(
            g.ps.at[kind, r, pl.ds(pl.multiple_of(64 * (1 - c), 64), 64)],
            g.psA.at[kind, r],
            PSS[kind].at[r, 0],
            PSR[kind].at[r, 0],
            sib,
        ).start()

    def ps_mid(kind, r):
        dst = g.psA.at[kind, r]
        rdma(dst, dst, PSS[kind].at[r, 0], PSR[kind].at[r, 0], sib).wait_recv()
        mine = g.ps[kind, r, pl.ds(pl.multiple_of(64 * c, 64), 64), :].astype(F32)
        g.psH[kind, r] = (mine + g.psA[kind, r].astype(F32)).astype(BF)
        rdma(
            g.psH.at[kind, r], g.psB.at[kind, r], PSS[kind].at[r, 1], PSR[kind].at[r, 1], xp
        ).start()

    def ps_end(kind, r):
        dst = g.psB.at[kind, r]
        rdma(dst, dst, PSS[kind].at[r, 1], PSR[kind].at[r, 1], xp).wait_recv()
        return g.psH[kind, r].astype(F32) + g.psB[kind, r].astype(F32)

    def share_start(ref, r, ss, rs):
        rdma(ref.at[half(r, c)], ref.at[half(r, c)], ss.at[r], rs.at[r], sib).start()

    def share_wait(ref, r, ss, rs):
        dst = ref.at[half(r, 1 - c)]
        rdma(dst, dst, ss.at[r], rs.at[r], sib).wait_recv()

    for r in range(R):
        for i in range(4):
            wait_part(i, r, g.rcO, g.o_s, g.o_r)
            g.attT[48 * i : 48 * i + 48, 128 * r : 128 * r + 128] = g.rcO[i, r]
        att = jnp.transpose(g.attT[:, 128 * r : 128 * r + 128])
        ps_start(0, r, nt(att, g.wo[...]))
        if r > 0:
            ps_mid(0, r - 1)
        if r == 1:
            ag_forward(3, 1)
    ps_mid(0, R - 1)
    ag_forward(3, 2)
    ag_wait(2)

    def second_norm(r):
        v = g.inp[half(r, c), :] + ps_end(0, r) + ob0
        g.mid[r] = v
        v = v - jnp.mean(v, axis=1, keepdims=True)
        rstd = lax.rsqrt(jnp.mean(v * v, axis=1, keepdims=True) + EPSILON)
        v = v * rstd
        g.n2[r] = v
        g.rstd2[r] = rstd
        g.ntk[half(r, c), :] = (v * g1 + s1).astype(BF)
        share_start(g.ntk, r, g.nt_s, g.nt_r)

    up_bias = g.in_upb[...].astype(F32).reshape(1, 768)

    def feed_up(r):
        share_wait(g.ntk, r, g.nt_s, g.nt_r)
        pre = nn(g.ntk[rows(r), :], g.wu[...].reshape(768, 768)) + up_bias
        cdf = 0.5 * (1.0 + lax.erf(pre * (1.0 / math.sqrt(2.0))))
        pdf = jnp.exp(-0.5 * pre * pre) * (1.0 / math.sqrt(2.0 * math.pi))
        g.act[rows(r), :] = (pre * cdf).astype(BF)
        g.gd[rows(r), :] = cdf + pre * pdf

    def feed_back(r):
        gact = nn(g.in_cot[rows(r), :], g.wd[...].reshape(768, 768))
        g.gp[rows(r), :] = (gact * g.gd[rows(r), :]).astype(BF)
        ps_start(1, r, nt(g.gp[rows(r), :], g.wu[...].reshape(768, 768)))

    def pack(v):
        width = v.shape[1]
        tiles = [v[:, 128 * t : 128 * t + 128] for t in range(width // 128)]
        if width % 128:
            rest = v[:, width - 64 :]
            tiles.append(jnp.concatenate([rest[0:48], rest[48:96]], axis=1))
        return jnp.concatenate(tiles, axis=0)

    def unpack(v):
        count = v.shape[0] // 96
        tiles = [v[96 * t : 96 * t + 96] for t in range(count)]
        if v.shape[0] % 96:
            rest = v[96 * count :]
            tiles.append(jnp.concatenate([rest[:, 0:64], rest[:, 64:128]], axis=0))
        return jnp.concatenate(tiles, axis=1)

    def block(p, k):
        return pack(raw_block(p, k))

    def raw_block(p, k):
        b = pl.ds(pl.multiple_of(96 * k, 96), 96)
        if p == 0:
            return nt(g.nrmT[b, :], g.gpT[...])
        if p == 1:
            return nt(g.gbT[b, :], g.attT[...])
        if p == 2:
            return nn(g.ntT[b, :], g.gp[...])
        return nn(g.cotT[b, :], g.act[...])

    L1S = [g.l1s0, g.l1s1, g.l1s2, g.l1s3]
    L1R = [g.l1r0, g.l1r1, g.l1r2, g.l1r3]
    L2S = [g.l2s0, g.l2s1, g.l2s2, g.l2s3]
    L2R = [g.l2r0, g.l2r1, g.l2r2, g.l2r3]
    g.acc = [g.acc0, g.acc1, g.acc2, g.acc3]

    def rs_first(p, start=0, stop=4):
        def step(t, _):
            q = four(t, [zs[2], zs[1], zs[0], z])
            L1S[p][q] = block(p, 2 * q + 1 - y).astype(BF)
            rdma(L1S[p].at[q], L1R[p].at[q], L1SS[p].at[q], L1RS[p].at[q], yp).start()
            return 0

        lax.fori_loop(start, stop, step, 0)

    def reduced(p, q):
        dst = L1R[p].at[q]
        rdma(dst, dst, L1SS[p].at[q], L1RS[p].at[q], yp).wait_recv()
        return block(p, 2 * q + y) + L1R[p][q].astype(F32)

    def rs_far(p):
        @pl.when(outer)
        def _():
            q = zs[2]
            L2S[p][q] = reduced(p, q).astype(BF)
            rdma(L2S[p].at[q], L2R[p].at[zs[0]], L2SS[p].at[q], L2RS[p].at[zs[0]], zm[0]).start()

    def rs_second(p, t):
        q = zs[t]

        def send():
            v = reduced(p, q)
            if t == 2:
                via = L2R[p].at[z]
                rdma(via, via, L2SS[p].at[q], L2RS[p].at[z], zm[0]).wait_recv()
                v = v + via[...].astype(F32)
            L2S[p][q] = v.astype(BF)
            rdma(L2S[p].at[q], L2R[p].at[z], L2SS[p].at[q], L2RS[p].at[z], zm[t]).start()

        if t == 2:
            pl.when(inner)(send)
        else:
            send()

    def rs_own(p):
        dst = L1R[p].at[z]
        rdma(dst, dst, L1SS[p].at[z], L1RS[p].at[z], yp).wait_recv()
        g.acc[p][...] = block(p, s) + L1R[p][z].astype(F32)

    def rs_third(p):
        acc = g.acc[p]
        for t, q in enumerate(zs):
            dst = L2R[p].at[q]

            def add(dst=dst, q=q):
                rdma(dst, dst, L2SS[p].at[q], L2RS[p].at[q], yp).wait_recv()
                acc[...] += dst[...].astype(F32)

            if t < 2:
                add()
            else:
                pl.when(inner)(add)
        return unpack(acc[...])

    def rs_drain(p):
        for q in qs:
            rdma(L1S[p].at[q], L1R[p].at[q], L1SS[p].at[q], L1RS[p].at[q], yp).wait_send()
        for q in zs:
            rdma(L2S[p].at[q], L2R[p].at[q], L2SS[p].at[q], L2RS[p].at[q], yp).wait_send()

    second_norm(0)
    second_norm(1)
    feed_up(0)
    second_norm(2)
    feed_up(1)
    feed_up(2)
    rs_first(3, 0, 1)
    ag_wait(3)
    feed_back(0)
    feed_back(1)
    ps_mid(1, 0)
    rs_first(3, 1, 2)
    feed_back(2)
    ps_mid(1, 1)
    rs_first(3, 2, 3)
    ps_mid(1, 2)
    rs_first(3, 3, 4)
    g.ntT[...] = jnp.transpose(g.ntk[...])

    def add_sum(row, value):
        g.sums[row : row + 1, :] += jnp.sum(value, axis=0, keepdims=True)

    def norm_back(grad, n, rstd, gain):
        e = grad * gain
        return rstd * (
            e - jnp.mean(e, axis=1, keepdims=True) - n * jnp.mean(e * n, axis=1, keepdims=True)
        )

    def second_back(r):
        gn = ps_end(1, r)
        n = g.n2[r]
        cot = g.in_cot[half(r, c), :].astype(F32)
        gm = cot + norm_back(gn, n, g.rstd2[r], g1)
        g.gm[r] = gm
        gb = gm.astype(BF)
        g.gb[half(r, c), :] = gb
        share_start(g.gb, r, g.gb_s, g.gb_r)
        add_sum(1, gn * n)
        add_sum(3, gn)
        add_sum(4, gb.astype(F32))
        add_sum(5, cot)

    def grad_attended(r):
        share_wait(g.gb, r, g.gb_s, g.gb_r)
        ga = jnp.transpose(nn(g.gb[rows(r), :], g.wo[...])).astype(BF)
        for i in range(4):
            g.snD[i, r] = ga[48 * i : 48 * i + 48]
            send_part(i, r, g.snD, g.rcD, g.d_s, g.d_r)

    second_back(0)
    rs_far(3)
    second_back(1)
    grad_attended(0)
    second_back(2)
    grad_attended(1)
    grad_attended(2)
    rs_second(3, 1)
    rs_first(2, 0, 2)
    for r in range(R):
        ps_start(2, r, nt(g.act[rows(r), :], g.wd[...].reshape(768, 768)))
    g.gbT[...] = jnp.transpose(g.gb[...])

    def attn_bwd(r):
        for i in range(4):
            wait_part(i, r, g.rcD, g.d_s, g.d_r)
        dk = None
        dv = None
        for qc in range(2):
            q0 = 256 * qc
            do = jnp.concatenate([g.rcD[2 * qc, r], g.rcD[2 * qc + 1, r]], axis=1)
            delta = jnp.sum(do.astype(F32) * g.O[r, :, q0 : q0 + 256], axis=0, keepdims=True)
            dp = tn(g.VT[r, 0:48, :], do)
            pn = g.P[r, :, q0 : q0 + 256].astype(F32) * g.inv[r, 0:1, q0 : q0 + 256]
            ds = (pn * (dp - delta)).astype(BF)
            pn = pn.astype(BF)
            dq = nn(g.KT[r, 0:48, :], ds) * ROOT
            for u in range(2):
                g.snG[2 * qc + u, r, 0:48, :] = dq[:, 128 * u : 128 * u + 128].astype(BF)
            dk_part = nt(g.QT[r, 0:48, q0 : q0 + 256], ds)
            dv_part = nt(do, pn)
            dk = dk_part if dk is None else dk + dk_part
            dv = dv_part if dv is None else dv + dv_part
        dk = dk * ROOT
        g.snX[r, 0:48, :] = dk[:, 512:1024]
        g.snX[r, 48:96, :] = dv[:, 512:1024]
        rdma(g.snX.at[r], g.rcX.at[r], g.x_s.at[r], g.x_r.at[r], sib).start()
        g.kvX[r, 0:48, :] = dk[:, 0:512]
        g.kvX[r, 48:96, :] = dv[:, 0:512]

    def attn_bwd_end(r):
        rdma(g.rcX.at[r], g.rcX.at[r], g.x_s.at[r], g.x_r.at[r], sib).wait_recv()
        kv = (g.kvX[r] + g.rcX[r]).astype(BF)
        for i in range(4):
            g.snG[i, r, 48:144, :] = kv[:, 128 * i : 128 * i + 128]
            send_part(i, r, g.snG, g.rcG, g.g_s, g.g_r)

    attn_bwd(0)
    ps_mid(2, 0)
    attn_bwd(1)
    attn_bwd_end(0)
    rs_first(2, 2, 3)
    ps_mid(2, 1)
    attn_bwd(2)
    attn_bwd_end(1)
    rs_first(2, 3, 4)
    ps_mid(2, 2)
    attn_bwd_end(2)
    rs_second(3, 0)
    rs_second(3, 2)
    rs_first(1)
    rs_far(2)
    rs_second(2, 1)
    rs_own(3)

    for r in range(R):
        g.out_tok[half(r, c), :] = (g.mid[r] + ps_end(2, r) + ob1).astype(BF)
        share_start(g.out_tok, r, g.ot_s, g.ot_r)
    ones = jnp.ones((8, 384), BF)
    g.sums[6:7, :] = nn(ones, g.gp[...])[0:1]

    def project_back(r):
        for i in range(4):
            wait_part(i, r, g.rcG, g.g_s, g.g_r)
            for t in range(3):
                g.gpT[192 * t + 48 * i : 192 * t + 48 * i + 48, 128 * r : 128 * r + 128] = g.rcG[
                    i, r, 48 * t : 48 * t + 48, :
                ]
        if r == R - 1:
            rs_first(0, 0, 2)
        ps_start(3, r, tt(g.gpT[:, 128 * r : 128 * r + 128], g.wq[:, :, 0:576].reshape(768, 576)))

    project_back(0)
    rs_second(2, 0)
    project_back(1)
    ps_mid(3, 0)
    rs_second(2, 2)
    project_back(2)
    ps_mid(3, 1)
    rs_first(0, 2, 4)
    ps_mid(3, 2)
    rs_own(2)
    rs_far(1)
    for t in (1, 0, 2):
        rs_second(1, t)
    rs_own(1)
    rs_far(0)
    g.sums[7:8, 0:576] = nt(ones, g.gpT[...])[0:1]

    def first_back(r):
        gn = ps_end(3, r)
        n = g.n1[half(r, c), :]
        gt = g.gm[r] + norm_back(gn, n, g.rstd1[half(r, c), :], g0)
        g.out_gtok[half(r, c), :] = gt.astype(BF)
        share_start(g.out_gtok, r, g.gt_s, g.gt_r)
        add_sum(0, gn * n)
        add_sum(2, gn)

    first_back(0)
    first_back(1)
    rs_second(0, 1)
    first_back(2)
    rdma(g.sums, g.sumA, g.sm_s.at[0], g.sm_r.at[0], sib).start()
    rdma(g.sumA, g.sumA, g.sm_s.at[0], g.sm_r.at[0], sib).wait_recv()
    both = lax.broadcasted_iota(jnp.int32, (8, 768), 0) < 6
    g.sumB[...] = g.sums[...] + jnp.where(both, g.sumA[...], 0.0)
    rdma(g.sumB, g.sumC, g.sm_s.at[1], g.sm_r.at[1], yp).start()
    rs_second(0, 0)
    rs_second(0, 2)
    rdma(g.sumC, g.sumC, g.sm_s.at[1], g.sm_r.at[1], yp).wait_recv()
    g.sumD[z] = g.sumB[...] + g.sumC[...]
    for t in range(3):
        rdma(g.sumD.at[z], g.sumD.at[z], g.sm_s.at[2 + t], g.sm_r.at[2 + z], zm[t]).start()
    rs_own(0)
    g.out_gdown[...] = rs_third(3)
    g.out_gup[...] = rs_third(2)
    g.out_gout[...] = jnp.transpose(rs_third(1))
    total = rs_third(0)
    for t in range(3):
        g.out_gqkv[t] = total[:, 192 * t : 192 * t + 192]
    for t in range(3):
        q = zs[t]
        rdma(g.sumD.at[q], g.sumD.at[q], g.sm_s.at[2 + t], g.sm_r.at[2 + q], zm[t]).wait_recv()
    total = g.sumD[0] + g.sumD[1] + g.sumD[2] + g.sumD[3]
    for k in range(8):
        g.cut[k] = total[:, 96 * k : 96 * k + 96]
    mine = g.cut[s]
    g.out_gain[...] = mine[0:2]
    g.out_shift[...] = mine[2:4]
    g.out_obias[...] = mine[4:6]
    g.out_upb[...] = total[6:7]
    g.out_qvb[0:1, :] = total[7:8, 0:192]
    g.out_qvb[1:2, :] = total[7:8, 384:576]

    for r in range(R):
        share_wait(g.out_tok, r, g.ot_s, g.ot_r)
        share_wait(g.out_gtok, r, g.gt_s, g.gt_r)
    for t, dev in enumerate(others):
        rdma(g.sml.at[s], g.sml.at[s], g.sml_s.at[t], g.sml_r.at[s], dev).wait_send()
    for p in range(4):
        ag_drain(p)
    for p in range(4):
        rs_drain(p)
    for r in range(R):
        for i in range(4):
            drain_part(i, r, g.snA, g.qa_s, g.qa_r)
            drain_part(i, r, g.snO, g.o_s, g.o_r)
            drain_part(i, r, g.snD, g.d_s, g.d_r)
            drain_part(i, r, g.snG, g.g_s, g.g_r)
            rdma(g.sbA.at[i, r], g.sbA.at[i, r], g.sa_s.at[i, r], g.sa_r.at[i, r], sib).wait_send()
        rdma(g.snX.at[r], g.rcX.at[r], g.x_s.at[r], g.x_r.at[r], sib).wait_send()
        for kind in range(4):
            for t in range(2):
                rdma(
                    g.psH.at[kind, r], g.psB.at[kind, r], PSS[kind].at[r, t], PSR[kind].at[r, t], xp
                ).wait_send()
        for ref, ss, rs in (
            (g.ntk, g.nt_s, g.nt_r),
            (g.gb, g.gb_s, g.gb_r),
            (g.out_tok, g.ot_s, g.ot_r),
            (g.out_gtok, g.gt_s, g.gt_r),
        ):
            rdma(ref.at[half(r, c)], ref.at[half(r, c)], ss.at[r], rs.at[r], sib).wait_send()
    rdma(g.sums, g.sumA, g.sm_s.at[0], g.sm_r.at[0], sib).wait_send()
    rdma(g.sumB, g.sumC, g.sm_s.at[1], g.sm_r.at[1], yp).wait_send()
    for t in range(3):
        rdma(g.sumD.at[z], g.sumD.at[z], g.sm_s.at[2 + t], g.sm_r.at[2 + z], zm[t]).wait_send()


def fast_device(
    tokens, cotangent, lengths, coords, keep_mask, ln_gains, ln_shifts, out_bias,
    w_qkv, qv_bias, w_out, w_up, up_bias, w_down,
):
    inputs = [
        ("in_tok", tokens.reshape(384, 768)),
        ("in_cot", cotangent.reshape(384, 768)),
        ("in_len", lengths),
        ("in_crd", jnp.transpose(coords, (1, 0, 2))),
        ("in_keep", keep_mask),
        ("in_lng", ln_gains),
        ("in_lns", ln_shifts),
        ("in_ob", out_bias),
        ("in_w3", jnp.transpose(w_qkv, (1, 0, 2))),
        ("in_qvb", qv_bias),
        ("in_wo", w_out),
        ("in_wu", w_up),
        ("in_upb", up_bias),
        ("in_wd", jnp.transpose(w_down)),
    ]
    outputs = [
        ("out_tok", (384, 768), BF),
        ("out_gtok", (384, 768), BF),
        ("out_gain", (2, 96), F32),
        ("out_shift", (2, 96), F32),
        ("out_obias", (2, 96), F32),
        ("out_gqkv", (3, 96, 192), F32),
        ("out_qvb", (2, 192), F32),
        ("out_gout", (192, 96), F32),
        ("out_gup", (96, 768), F32),
        ("out_upb", (1, 768), F32),
        ("out_gdown", (96, 768), F32),
    ]
    vm = [
        ("wq", (8, 96, 768), BF),
        ("wo", (768, 192), BF),
        ("sml", (8, 16, 128), BF),
        ("tmp", (16, 128), F32),
        ("nrm", (384, 768), BF),
        ("gd", (384, 768), F32),
        ("acc0", (432, 128), F32),
        ("acc1", (144, 128), F32),
        ("acc2", (576, 128), F32),
        ("acc3", (576, 128), F32),
        ("wu", (8, 96, 768), BF),
        ("wd", (8, 96, 768), BF),
        ("inp", (384, 768), F32),
        ("n1", (384, 768), F32),
        ("rstd1", (384, 1), F32),
        ("cotT", (768, 384), BF),
        ("nrmT", (768, 384), BF),
        ("par", (16, 768), F32),
        ("sums", (8, 768), F32),
        ("sumA", (8, 768), F32),
        ("sumB", (8, 768), F32),
        ("sumC", (8, 768), F32),
        ("sumD", (4, 8, 768), F32),
        ("cut", (8, 8, 96), F32),
        ("snA", (4, 3, 144, 128), BF),
        ("rcA", (4, 3, 144, 128), BF),
        ("sbA", (4, 3, 96, 128), BF),
        ("QT", (3, 64, 512), BF),
        ("KT", (3, 64, 1024), BF),
        ("VT", (3, 64, 1024), BF),
        ("P", (3, 1024, 512), BF),
        ("O", (3, 48, 512), F32),
        ("inv", (3, 8, 512), F32),
        ("snO", (4, 3, 48, 128), BF),
        ("rcO", (4, 3, 48, 128), BF),
        ("snD", (4, 3, 48, 128), BF),
        ("rcD", (4, 3, 48, 128), BF),
        ("snG", (4, 3, 144, 128), BF),
        ("rcG", (4, 3, 144, 128), BF),
        ("snX", (3, 96, 512), F32),
        ("rcX", (3, 96, 512), F32),
        ("kvX", (3, 96, 512), F32),
        ("attT", (192, 384), BF),
        ("gpT", (576, 384), BF),
        ("ps", (4, 3, 128, 768), BF),
        ("psA", (4, 3, 64, 768), BF),
        ("psH", (4, 3, 64, 768), BF),
        ("psB", (4, 3, 64, 768), BF),
        ("mid", (3, 64, 768), F32),
        ("n2", (3, 64, 768), F32),
        ("rstd2", (3, 64, 1), F32),
        ("gm", (3, 64, 768), F32),
        ("ntk", (384, 768), BF),
        ("ntT", (768, 384), BF),
        ("act", (384, 768), BF),
        ("gp", (384, 768), BF),
        ("gb", (384, 768), BF),
        ("gbT", (768, 384), BF),
    ]
    for p, width in enumerate((576, 192, 768, 768)):
        for kind in ("l1s", "l1r", "l2s", "l2r"):
            vm.append((f"{kind}{p}", (4, 96 * width // 128, 128), BF))
    sems = [
        ("qa_s", (4, 3)), ("qa_r", (4, 3)),
        ("sa_s", (4, 3)), ("sa_r", (4, 3)),
        ("o_s", (4, 3)), ("o_r", (4, 3)),
        ("d_s", (4, 3)), ("d_r", (4, 3)),
        ("g_s", (4, 3)), ("g_r", (4, 3)),
        ("x_s", (3,)), ("x_r", (3,)),
        ("nt_s", (3,)), ("nt_r", (3,)),
        ("gb_s", (3,)), ("gb_r", (3,)),
        ("ot_s", (3,)), ("ot_r", (3,)),
        ("gt_s", (3,)), ("gt_r", (3,)),
        ("sm_s", (8,)), ("sm_r", (8,)),
        ("sml_s", (7,)), ("sml_r", (8,)),
    ]
    for name, shape in (
        ("ag_s", (8,)), ("ag_r", (8,)), ("ps_s", (3, 2)), ("ps_r", (3, 2)),
        ("l1_s", (4,)), ("l1_r", (4,)), ("l2_s", (4,)), ("l2_r", (4,)),
    ):
        sems += [(f"{name}{q}", shape) for q in range(4)]
    names = [n for n, _ in inputs] + [o[0] for o in outputs] + [v[0] for v in vm] + [n for n, _ in sems]
    vmem = pl.BlockSpec(memory_space=pltpu.VMEM)
    out = pl.pallas_call(
        partial(layer_kernel, names=names),
        out_shape=[jax.ShapeDtypeStruct(shape, dtype) for _, shape, dtype in outputs],
        in_specs=[
            pl.BlockSpec(memory_space=pltpu.SMEM) if n == "in_len" else vmem for n, _ in inputs
        ],
        out_specs=[vmem] * len(outputs),
        scratch_shapes=[pltpu.VMEM(shape, dtype) for _, shape, dtype in vm]
        + [pltpu.SemaphoreType.DMA(shape) for _, shape in sems],
        compiler_params=pltpu.CompilerParams(
            collective_id=0, has_side_effects=True, vmem_limit_bytes=60 * 1024 * 1024
        ),
    )(*[v for _, v in inputs])
    shapes = [
        jax.ShapeDtypeStruct((768,) if o.shape == (1, 768) else o.shape, o.dtype) for o in out
    ]

    def hand_over(*refs):
        for n in range(len(shapes)):
            refs[len(shapes) + n][...] = refs[n][...].reshape(shapes[n].shape)

    out = pl.pallas_call(
        hand_over,
        out_shape=shapes,
        in_specs=[vmem] * len(shapes),
        out_specs=[vmem] * len(shapes),
    )(*out)
    out_tok, out_gtok, gain, shift, obias, gqkv, qvb, gout, gup, upb, gdown = out
    return (
        out_tok.reshape(3, 128, 768),
        out_gtok.reshape(3, 128, 768),
        gain,
        shift,
        obias,
        jnp.transpose(gqkv, (1, 0, 2)),
        qvb,
        gout,
        gup,
        upb,
        jnp.transpose(gdown),
    )


def solution(mesh):
    placed = (
        P(None, "seq", None),
        P(None, "seq", None),
        P(),
        P(None, None, "seq"),
        P(None, "seq"),
        P(None, "seq"),
        P(None, "seq"),
        P(None, "seq"),
        P("seq", None, "head"),
        P(None, "head"),
        P("head", "seq"),
        P("seq", "head"),
        P("head"),
        P("head", "seq"),
    )
    layout = (mesh.shape["seq"], mesh.shape["head"])

    def step(tokens, *others):
        one_kernel = layout == (8, 4) and tokens.shape == (3, 1024, 768)
        return over(fast_device if one_kernel else per_device)(tokens, *others)

    def over(device):
        return jax.shard_map(
        device,
        mesh=mesh,
        in_specs=placed,
        out_specs=(
            P(None, "seq", None),
            P(None, "seq", None),
            P(None, "seq"),
            P(None, "seq"),
            P(None, "seq"),
            P("seq", None, "head"),
            P(None, "head"),
            P("head", "seq"),
            P("seq", "head"),
            P("head"),
            P("head", "seq"),
        ),
        check_vma=False,
    )

    return step
```
